32 devices in a mesh: rows: 8 (over y, x, core), cols: 4 (over z).
Axes of the slice: x: 2, y: 2, z: 4, core: 2. Of those that a mesh axis runs over, the one named last changes fastest.
Arguments:
- tiles: bfloat16 [1024, 256, 256], P(('rows', 'cols')), may hold values from -15 to 20
- send_slot: int32 [32, 32], P(('rows', 'cols')), may hold values from 0 to 31, each once within a row
- slot_row: int32 [32, 32], P(('rows', 'cols')), may hold values from 0 to 2, as said below
- slot_fetch: int32 [32, 32], P(('rows', 'cols')), may hold values from 0 to 7
- fetch_list: int32 [32, 8], P(('rows', 'cols')), may hold values from 0 to 1
- basis: bfloat16 [16384, 128], P(('rows', 'cols')), may hold values from -6 to 6
Outputs:
- embedding: bfloat16 [16384, 128], P(('rows', 'cols'))
The draws below stay inside these ranges and needn't reach their ends.
Inputs may be any that keep to these rules, and one draw needn't show every extreme that they name: `slot_row`: value 2 marks an empty slot. Within each block of 8 slots (one source builder) the filled slots come first; some device has all 32 slots filled in every draw.
All inputs are finite; a program needn't handle non-finite values.
Results may differ from the reference program's by a relative error of at most 0.02.
Values may be sent and summed in bfloat16 or wider, within the bound.
No kernel may reach another device: no remote copies, remote signals or barrier semaphores. Data moves between devices by JAX's collectives and lax.ppermute only.
A program may use at most 128 MiB of HBM per device.

```python
import jax
import jax.numpy as jnp
from jax import lax

TILE = 256
WIDTH = 128
BR = 2
Q = 8
ITERS = 6
TB = 32
GROUPS = 8
NPTS = 16384
N_COLS = 4
DEVICES = 32


def draw_tiles(key, part):
    shape = (TB * DEVICES, TILE, TILE)
    key_noise = jax.random.fold_in(key, 21)
    noise = jax.random.truncated_normal(key_noise, -6.0, 6.0, shape, jnp.float32)
    values = 0.25 + noise
    return values.astype(jnp.bfloat16)


def draw_slot_row(key, part):
    ncols = TB // Q
    key_count = jax.random.fold_in(key, 11)
    key_full = jax.random.fold_in(key, 12)
    key_row = jax.random.fold_in(key, 13)
    count = jax.random.randint(key_count, (DEVICES, ncols), 1, Q + 1)
    full_dev = jax.random.randint(key_full, (), 0, DEVICES)
    devs = jnp.arange(DEVICES, dtype=jnp.int32)
    count = jnp.where((devs == full_dev)[:, None], Q, count)
    slots = jnp.arange(TB, dtype=jnp.int32)
    filled = slots[None, :] % Q < count[:, slots // Q]
    rows = jax.random.randint(key_row, (DEVICES, TB), 0, BR)
    return jnp.where(filled, rows, BR).astype(jnp.int32)


def set_ends(entries, key, low, top_value):
    longest = entries.shape.index(max(entries.shape))
    spots = []
    for shift in (0, 1):
        where = [jax.random.randint(jax.random.fold_in(key, axis), (), 0, length) for axis, length in enumerate(entries.shape)]
        where[longest] = (where[longest] + shift) % entries.shape[longest]
        spots.append(tuple(where))
    return entries.at[spots[0]].set(low).at[spots[1]].set(top_value)


def level_of(own_key, extent, pieces, smallest, largest):
    def one(dim, shards_of):
        steps = jax.random.uniform(jax.random.fold_in(jax.random.fold_in(own_key, 6), dim), (shards_of,), jnp.float32, smallest / len(pieces), largest / len(pieces))
        return jnp.repeat(jnp.exp(steps), extent[dim] // shards_of).reshape((-1,) + (1,) * (len(extent) - dim - 1))

    factor_of = one(*pieces[0])
    for cut in pieces[1:]:
        factor_of = factor_of * one(*cut)
    return factor_of


def gaussian(stream_key, dims, scale, bound, shards=(), kind=jnp.bfloat16):
    loudness = level_of(stream_key, dims, shards, -0.22, 0.18) if shards else 1.0
    array = jax.random.normal(stream_key, dims, jnp.float32) * scale * loudness
    return jnp.minimum(jnp.maximum(array, -bound), bound).astype(kind)


def setup_inputs(seed: int = 0) -> dict:
    seeds = jax.random.split(jax.random.key(seed), 7)
    return {
        "tiles": draw_tiles(jax.random.fold_in(seeds[6], 71), 0),
        "send_slot": jax.vmap(lambda own: jax.random.permutation(own, TB))(jax.random.split(seeds[1], DEVICES)).reshape((DEVICES, TB)).astype(jnp.int32),
        "slot_row": draw_slot_row(jax.random.fold_in(seeds[6], 71), 0),
        "slot_fetch": set_ends(jax.random.randint(seeds[3], (DEVICES, TB), 0, GROUPS), jax.random.fold_in(seeds[3], 1), 0, GROUPS - 1).astype(jnp.int32),
        "fetch_list": set_ends(jax.random.randint(seeds[4], (DEVICES, GROUPS), 0, BR), jax.random.fold_in(seeds[4], 1), 0, BR - 1).astype(jnp.int32),
        "basis": gaussian(seeds[5], (NPTS, WIDTH), 1.0, 6.0, ((0, 32),)),
    }


def reference(tiles, send_slot, slot_row, slot_fetch, fetch_list, basis):
    devs = slot_row.shape[0]
    slots_all = slot_row.shape[1]
    ncols = N_COLS
    per_src = slots_all // ncols
    npts = basis.shape[0]
    inverse = jnp.argsort(send_slot, axis=1).astype(jnp.int32)
    slots = jnp.arange(slots_all, dtype=jnp.int32)
    owners = jnp.arange(devs, dtype=jnp.int32)
    group = owners // ncols
    column = owners % ncols
    builder = group[:, None] * ncols + slots[None, :] // per_src
    position = column[:, None] * per_src + slots[None, :] % per_src
    source_tile = (builder * slots_all + inverse[builder, position]).astype(jnp.int32)
    wanted = jnp.take_along_axis(fetch_list, slot_fetch, axis=1)
    col_block = ((slot_fetch * ncols + column[:, None]) * BR + wanted).astype(jnp.int32)
    blocks = jnp.arange(BR, dtype=jnp.int32)

    def one_hot(o):
        return (slot_row[o][:, None] == blocks[None, :]).astype(jnp.float32)

    def degree(o):
        weights = tiles[source_tile[o]].astype(jnp.float32)
        row_abs = lax.optimization_barrier(jnp.sum(jnp.abs(weights), axis=2))
        return 1.0 + jnp.dot(one_hot(o).T, row_abs, precision=lax.Precision.HIGHEST)
    deg = lax.map(degree, owners).reshape(npts, 1)
    scale = lax.rsqrt(deg)
    current = basis
    for step in range(ITERS):
        scaled = (scale * current.astype(jnp.float32)).astype(jnp.bfloat16).reshape(devs * BR, TILE, WIDTH)

        def apply(o):
            weights = tiles[source_tile[o]].astype(jnp.float32)
            fetched = scaled[col_block[o]].astype(jnp.float32)
            prod = jnp.einsum('sak,skd->sad', weights, fetched, precision=lax.Precision.HIGHEST)
            return jnp.einsum('sj,sad->jad', one_hot(o), prod, precision=lax.Precision.HIGHEST)
        iterate = lax.map(apply, owners).reshape(npts, WIDTH) * scale
        gram = jnp.dot(iterate.T, iterate, precision=lax.Precision.HIGHEST)
        lower = jnp.linalg.cholesky(gram / npts)
        solved = lax.linalg.triangular_solve(lower, iterate, left_side=False, lower=True, transpose_a=True)
        current = solved.astype(jnp.bfloat16)
    return current
```

```python
import functools

import jax
import jax.numpy as jnp
from jax import lax
from jax.experimental import pallas as pl
from jax.experimental.pallas import tpu as pltpu
from jax.sharding import PartitionSpec as P

TILE = 256
WIDTH = 128
ITERS = 6
GROUP = 8
HIGHEST = lax.Precision.HIGHEST
VMEM = pl.BlockSpec(memory_space=pltpu.VMEM)
SMEM = pl.BlockSpec(memory_space=pltpu.SMEM)
ANY = pl.BlockSpec(memory_space=pl.ANY)


def params():
    return pltpu.CompilerParams(vmem_limit_bytes=32 * 1024 * 1024)


def pack_kernel(ncols, per, send_ref, tiles_ref, *refs):
    outs, sums = refs[:ncols], refs[ncols : 2 * ncols]
    buf, inverse, in_sem, out_sem = refs[2 * ncols :]
    me = lax.axis_index("cols")

    def note(i, carry):
        inverse[send_ref[0, i]] = i
        return carry

    lax.fori_loop(0, ncols * per, note, 0)
    order = list(range(1, ncols)) + [0]
    arrive = []
    for d in order:
        dest = lax.rem(me + d, ncols)
        for p in range(per):
            k = d * per + p
            copy = pltpu.make_async_copy(tiles_ref.at[inverse[dest * per + p]], buf.at[k], in_sem.at[k])
            copy.start()
            arrive.append((d, p, k, copy))
    ones = jnp.ones((8, TILE), jnp.bfloat16)
    leave = []
    for d, p, k, copy in arrive:
        copy.wait()
        out = pltpu.make_async_copy(buf.at[k], outs[d].at[p], out_sem.at[k])
        out.start()
        leave.append(out)
        total = lax.dot_general(
            ones, jnp.abs(buf[k]), (((1,), (1,)), ((), ())), preferred_element_type=jnp.float32
        )
        sums[d][p : p + 1, :] = total[0:1, :]
    for out in leave:
        out.wait()


def pack(tiles, send_slot, ncols):
    nslots = tiles.shape[0]
    per = nslots // ncols
    shapes = [jax.ShapeDtypeStruct((per, TILE, TILE), tiles.dtype)] * ncols
    shapes += [jax.ShapeDtypeStruct((per, TILE), jnp.float32)] * ncols
    res = pl.pallas_call(
        functools.partial(pack_kernel, ncols, per),
        out_shape=shapes,
        in_specs=[SMEM, ANY],
        out_specs=[ANY] * ncols + [VMEM] * ncols,
        scratch_shapes=[
            pltpu.VMEM((nslots, TILE, TILE), tiles.dtype),
            pltpu.SMEM((nslots,), jnp.int32),
            pltpu.SemaphoreType.DMA((nslots,)),
            pltpu.SemaphoreType.DMA((nslots,)),
        ],
        compiler_params=params(),
    )(send_slot, tiles)
    return res[:ncols], res[ncols:]


def send_blocks(scaled, wanted, outs):
    for d, out in enumerate(outs):
        out[...] = scaled[pl.ds(pl.multiple_of(wanted[d] * TILE, TILE), TILE), :]


def start_kernel(ncols, groups, blocks, row_ref, *refs):
    lists, refs = refs[:groups], refs[groups:]
    sums, refs = refs[:ncols], refs[ncols:]
    basis_ref, scale_ref, asked_ref, refs = refs[0], refs[1], refs[2], refs[3:]
    outs, (scaled,) = refs[:groups], refs[groups:]
    me, row = lax.axis_index("cols"), lax.axis_index("rows")
    per = sums[0].shape[0]
    degree = [jnp.ones((1, TILE), jnp.float32) for _ in range(blocks)]
    for d in range(ncols):
        source = lax.rem(me + ncols - d, ncols)
        for p in range(per):
            at = row_ref[0, source * per + p]
            line = sums[d][p : p + 1, :]
            for j in range(blocks):
                degree[j] = degree[j] + jnp.where(at == j, line, jnp.zeros_like(line))
    for j in range(blocks):
        line = lax.rsqrt(degree[j])
        here = slice(j * TILE, (j + 1) * TILE)
        scale = jnp.transpose(jnp.broadcast_to(line, (WIDTH, TILE)))
        scale_ref[here, :] = scale
        scaled[here, :] = (scale * basis_ref[here, :].astype(jnp.float32)).astype(jnp.bfloat16)
    wanted = [lists[d][0, row] for d in range(groups)]
    for d in range(groups):
        asked_ref[0, d] = wanted[d]
    send_blocks(scaled, wanted, outs)


def start(slot_row, lists, sums, basis):
    ncols, groups, blocks = len(sums), len(lists), basis.shape[0] // TILE
    shapes = [
        jax.ShapeDtypeStruct((blocks * TILE, WIDTH), jnp.float32),
        jax.ShapeDtypeStruct((1, groups), jnp.int32),
    ] + [jax.ShapeDtypeStruct((TILE, WIDTH), jnp.bfloat16)] * groups
    res = pl.pallas_call(
        functools.partial(start_kernel, ncols, groups, blocks),
        out_shape=shapes,
        in_specs=[SMEM] * (1 + groups) + [VMEM] * (ncols + 1),
        out_specs=[VMEM, SMEM] + [VMEM] * groups,
        scratch_shapes=[pltpu.VMEM((blocks * TILE, WIDTH), jnp.bfloat16)],
        compiler_params=params(),
    )(slot_row, *lists, *sums, basis)
    return res[0], res[1], res[2:]


def step_kernel(ncols, groups, blocks, first, last, row_ref, fetch_ref, asked_ref, scale_ref, *refs):
    if not first:
        inv_ref, refs = refs[0], refs[1:]
    chunks, refs = refs[:ncols], refs[ncols:]
    got, refs = refs[:groups], refs[groups:]
    gram_ref, refs = refs[0], refs[1:]
    if last:
        y_ref, refs = refs[0], refs[1:]
    else:
        outs, refs = refs[:groups], refs[groups:]
    tbuf, ubuf, acc, scaled, t_sem, u_sem = refs
    me, row = lax.axis_index("cols"), lax.axis_index("rows")
    per = chunks[0].shape[0]
    u_copies = [pltpu.make_async_copy(got[d], ubuf.at[d], u_sem.at[d]) for d in range(groups)]
    t_copies = [pltpu.make_async_copy(chunks[d], tbuf.at[d], t_sem.at[d]) for d in range(ncols)]
    for copy in u_copies + t_copies:
        copy.start()
    acc[...] = jnp.zeros_like(acc)
    for copy in u_copies:
        copy.wait()
    for d in range(ncols):
        t_copies[d].wait()
        source = lax.rem(me + ncols - d, ncols)
        for p in range(per):
            slot = source * per + p
            which = jnp.bitwise_xor(fetch_ref[0, slot], row)
            place = pl.ds(pl.multiple_of(row_ref[0, slot] * TILE, TILE), TILE)
            acc[place, :] += jnp.dot(tbuf[d, p], ubuf[which], preferred_element_type=jnp.float32)
    scale = scale_ref[...]
    y = acc[: blocks * TILE, :] * scale
    if not first:
        y = lax.dot_general(
            y, inv_ref[...], (((1,), (1,)), ((), ())), precision=HIGHEST, preferred_element_type=jnp.float32
        )
    if last:
        y_ref[...] = y
    else:
        scaled[...] = (y * scale).astype(jnp.bfloat16)
        send_blocks(scaled, [asked_ref[0, d] for d in range(groups)], outs)
    gram_ref[...] = lax.dot_general(
        y, y, (((0,), (0,)), ((), ())), precision=HIGHEST, preferred_element_type=jnp.float32
    )


def step(slot_row, slot_fetch, asked, scale, inverse, chunks, got, last):
    ncols, groups, rows = len(chunks), len(got), scale.shape[0]
    blocks = rows // TILE
    per = chunks[0].shape[0]
    first = inverse is None
    shapes = [jax.ShapeDtypeStruct((WIDTH, WIDTH), jnp.float32)]
    if last:
        shapes += [jax.ShapeDtypeStruct((rows, WIDTH), jnp.float32)]
    else:
        shapes += [jax.ShapeDtypeStruct((TILE, WIDTH), jnp.bfloat16)] * groups
    res = pl.pallas_call(
        functools.partial(step_kernel, ncols, groups, blocks, first, last),
        out_shape=shapes,
        in_specs=[SMEM] * 3 + [VMEM] * (1 if first else 2) + [ANY] * (ncols + groups),
        out_specs=[VMEM] * len(shapes),
        scratch_shapes=[
            pltpu.VMEM((ncols, per, TILE, TILE), jnp.bfloat16),
            pltpu.VMEM((groups, TILE, WIDTH), jnp.bfloat16),
            pltpu.VMEM((rows + TILE, WIDTH), jnp.float32),
            pltpu.VMEM((rows, WIDTH), jnp.bfloat16),
            pltpu.SemaphoreType.DMA((ncols,)),
            pltpu.SemaphoreType.DMA((groups,)),
        ],
        compiler_params=params(),
    )(slot_row, slot_fetch, asked, scale, *([] if first else [inverse]), *chunks, *got)
    return res[0], (res[1] if last else res[1:])


def factor_rows(matrix, out_ref):
    n = WIDTH
    lane = lax.broadcasted_iota(jnp.int32, (8, n), 1)
    parts = [matrix[8 * i : 8 * i + 8, :] for i in range(n // 8)]
    for j in range(0, n, GROUP):
        here = j // 8
        off = j % 8
        wide = lambda v: jnp.broadcast_to(v, (8, n))
        rows = [wide(parts[here][off + a : off + a + 1, :]) for a in range(GROUP)]
        piv = [[wide(rows[a][:, j + c : j + c + 1]) for c in range(a + 1)] for a in range(GROUP)]
        in_group = (lane >= j) & (lane < j + GROUP)
        rows = [jnp.where(in_group, jnp.where(lane == j + a, 1.0, 0.0), rows[a]) for a in range(GROUP)]
        low = [[None] * GROUP for _ in range(GROUP)]
        inv = []
        for c in range(GROUP):
            inv.append(1.0 / piv[c][c])
            for a in range(c + 1, GROUP):
                low[a][c] = piv[a][c] * inv[c]
            for a in range(c + 1, GROUP):
                for b in range(c + 1, a + 1):
                    piv[a][b] = piv[a][b] - low[a][c] * piv[b][c]
        for a in range(GROUP):
            for c in range(a):
                rows[a] = rows[a] - low[a][c] * rows[c]
        for a in range(GROUP):
            keep = jnp.where(lane <= j + a, rows[a], 0.0) * lax.rsqrt(piv[a][a])
            out_ref[j + a : j + a + 1, :] = keep[0:1, :]
        scaled = [rows[a] * inv[a] for a in range(GROUP)]
        for i in range(here + 1, n // 8):
            cols = [wide(parts[i][:, j + c : j + c + 1]) for c in range(GROUP)]
            new = jnp.where(in_group, 0.0, parts[i])
            for c in range(GROUP):
                for b in range(c):
                    cols[c] = cols[c] - low[c][b] * cols[b]
                new = new - cols[c] * scaled[c]
            parts[i] = new


def factor_kernel(npts, last, a_ref, b_ref, *refs):
    matrix = (a_ref[...] + b_ref[...]) * (1.0 / npts)
    if not last:
        factor_rows(matrix, refs[0])
        return
    y_ref, v_ref, inv = refs
    factor_rows(matrix, inv)
    v_ref[...] = lax.dot_general(
        y_ref[...], inv[...], (((1,), (1,)), ((), ())), precision=HIGHEST, preferred_element_type=jnp.float32
    ).astype(v_ref.dtype)


def factor(pair, npts, y=None):
    square = jax.ShapeDtypeStruct((WIDTH, WIDTH), jnp.float32)
    last = y is not None
    return pl.pallas_call(
        functools.partial(factor_kernel, npts, last),
        out_shape=jax.ShapeDtypeStruct(y.shape, jnp.bfloat16) if last else square,
        in_specs=[VMEM] * (3 if last else 2),
        out_specs=VMEM,
        scratch_shapes=[pltpu.VMEM((WIDTH, WIDTH), jnp.float32)] if last else [],
        compiler_params=params(),
    )(*pair, *([y] if last else []))


def swap(x, axis, n, d):
    return lax.ppermute(x, axis, [(i, i ^ d) for i in range(n)])


def shift(x, axis, n, d):
    return lax.ppermute(x, axis, [(i, (i + d) % n) for i in range(n)])


def on_device(tiles, send_slot, slot_row, slot_fetch, fetch_list, basis):
    groups = lax.axis_size("rows")
    ncols = lax.axis_size("cols")
    npts = basis.shape[0] * groups * ncols
    chunks, sums = pack(tiles, send_slot, ncols)
    sums = [sums[0]] + [shift(sums[d], "cols", ncols, d) for d in range(1, ncols)]
    chunks = [chunks[0]] + [shift(chunks[d], "cols", ncols, d) for d in range(1, ncols)]
    lists = [fetch_list] + [swap(fetch_list, "rows", groups, d) for d in range(1, groups)]
    scale, asked, out = start(slot_row, lists, sums, basis)
    stages = [("rows", groups, 1 << i) for i in range(groups.bit_length() - 1)]
    stages += [("cols", ncols, 1 << i) for i in range(ncols.bit_length() - 1)]
    inverse = None
    for k in range(ITERS):
        got = [out[0]] + [swap(out[d], "rows", groups, d) for d in range(1, groups)]
        gram, out = step(slot_row, slot_fetch, asked, scale, inverse, chunks, got, k == ITERS - 1)
        for i, stage in enumerate(stages):
            other = swap(gram, *stage)
            if i < len(stages) - 1:
                gram = gram + other
        inverse = factor((gram, other), npts, out if k == ITERS - 1 else None)
    return inverse


def solution(mesh):
    in_specs = (
        P(("rows", "cols"), None, None),
        P(("rows", "cols"), None),
        P(("rows", "cols"), None),
        P(("rows", "cols"), None),
        P(("rows", "cols"), None),
        P(("rows", "cols"), None),
    )
    out_specs = P(("rows", "cols"), None)
    return jax.shard_map(
        on_device, mesh=mesh, in_specs=in_specs, out_specs=out_specs, check_vma=False
    )
```

```python
import functools

import jax
import jax.numpy as jnp
from jax import lax
from jax.experimental import pallas as pl
from jax.experimental.pallas import tpu as pltpu
from jax.sharding import PartitionSpec as P

TILE = 256
WIDTH = 128
ITERS = 6
GROUP = 8
HIGHEST = lax.Precision.HIGHEST
VMEM = pl.BlockSpec(memory_space=pltpu.VMEM)
SMEM = pl.BlockSpec(memory_space=pltpu.SMEM)
ANY = pl.BlockSpec(memory_space=pl.ANY)
HBM = pl.BlockSpec(memory_space=pltpu.HBM)


def params():
    return pltpu.CompilerParams(vmem_limit_bytes=32 * 1024 * 1024)


def pack_kernel(ncols, per, shifts, nsums, send_ref, tiles_ref, *refs):
    given, refs = refs[: nsums and ncols - len(shifts)], refs[nsums and ncols - len(shifts) :]
    outs, sums = refs[: len(shifts)], refs[len(shifts) : len(shifts) + nsums]
    inverse, sem = refs[len(shifts) + nsums :]
    me = lax.axis_index("cols")

    def note(i, carry):
        inverse[send_ref[0, i]] = i
        return carry

    lax.fori_loop(0, ncols * per, note, 0)
    copies = {}
    for n, d in enumerate(shifts):
        dest = lax.rem(me + d, ncols)
        for p in range(per):
            copies[d, p] = pltpu.make_async_copy(
                tiles_ref.at[inverse[dest * per + p]], outs[n].at[p], sem.at[n * per + p]
            )
            copies[d, p].start()
    if not nsums:
        for copy in copies.values():
            copy.wait()
        return
    lane = lax.broadcasted_iota(jnp.int32, (TILE, WIDTH), 1)
    total = jnp.zeros((TILE, WIDTH), jnp.float32)
    rest = [d for d in range(ncols) if d not in shifts]
    for d in rest + list(shifts):
        chunk = given[rest.index(d)] if d in rest else outs[shifts.index(d)]
        for p in range(per):
            if d in shifts:
                copies[d, p].wait()
            pick = jnp.where(lane == d * per + p, 1.0, 0.0).astype(jnp.bfloat16)
            total = total + jnp.dot(jnp.abs(chunk[p]), pick, preferred_element_type=jnp.float32)
    flat = jnp.transpose(total)
    for d in range(ncols):
        sums[d][...] = flat[d * per : (d + 1) * per, :]


def pack(tiles, send_slot, ncols, shifts, given=None):
    nslots = tiles.shape[0]
    per = nslots // ncols
    nsums = 0 if given is None else ncols
    given = given or []
    shapes = [jax.ShapeDtypeStruct((per, TILE, TILE), tiles.dtype)] * len(shifts)
    shapes += [jax.ShapeDtypeStruct((per, TILE), jnp.float32)] * nsums
    res = pl.pallas_call(
        functools.partial(pack_kernel, ncols, per, shifts, nsums),
        out_shape=shapes,
        in_specs=[SMEM, HBM] + [VMEM] * len(given),
        out_specs=[VMEM] * len(shapes),
        scratch_shapes=[
            pltpu.SMEM((nslots,), jnp.int32),
            pltpu.SemaphoreType.DMA((len(shifts) * per,)),
        ],
        compiler_params=params(),
    )(send_slot, tiles, *given)
    return res[: len(shifts)], res[len(shifts) :]


def send_blocks(scaled, wanted, outs):
    for d, out in enumerate(outs):
        out[...] = scaled[pl.ds(pl.multiple_of(wanted[d] * TILE, TILE), TILE), :]


def start_kernel(ncols, groups, blocks, held, row_ref, *refs):
    lists, refs = refs[:groups], refs[groups:]
    sums, refs = refs[:ncols], refs[ncols:]
    basis_ref, refs = refs[0], refs[1 + held :]
    scale_ref, asked_ref, refs = refs[0], refs[1], refs[2:]
    outs, scaled = refs[:groups], refs[-1]
    me, row = lax.axis_index("cols"), lax.axis_index("rows")
    per = sums[0].shape[0]
    degree = [jnp.ones((1, TILE), jnp.float32) for _ in range(blocks)]
    for d in range(ncols):
        source = lax.rem(me + ncols - d, ncols)
        for p in range(per):
            at = row_ref[0, source * per + p]
            line = sums[d][p : p + 1, :]
            for j in range(blocks):
                degree[j] = degree[j] + jnp.where(at == j, line, jnp.zeros_like(line))
    for j in range(blocks):
        line = lax.rsqrt(degree[j])
        here = slice(j * TILE, (j + 1) * TILE)
        scale = jnp.transpose(jnp.broadcast_to(line, (WIDTH, TILE)))
        scale_ref[here, :] = scale
        scaled[here, :] = (scale * basis_ref[here, :].astype(jnp.float32)).astype(jnp.bfloat16)
    wanted = [lists[d][0, row] for d in range(groups)]
    for d in range(groups):
        asked_ref[0, d] = wanted[d]
    send_blocks(scaled, wanted, outs)


def start(slot_row, lists, sums, basis, held):
    ncols, groups, blocks = len(sums), len(lists), basis.shape[0] // TILE
    shapes = [
        jax.ShapeDtypeStruct((blocks * TILE, WIDTH), jnp.float32),
        jax.ShapeDtypeStruct((1, groups), jnp.int32),
    ] + [jax.ShapeDtypeStruct((TILE, WIDTH), jnp.bfloat16)] * groups
    shapes += [jax.ShapeDtypeStruct(x.shape, x.dtype) for x in held]
    before = 2 + groups + ncols
    res = pl.pallas_call(
        functools.partial(start_kernel, ncols, groups, blocks, len(held)),
        out_shape=shapes,
        in_specs=[SMEM] * (1 + groups) + [VMEM] * (ncols + 1) + [ANY] * len(held),
        out_specs=[VMEM, SMEM] + [VMEM] * groups + [ANY] * len(held),
        scratch_shapes=[pltpu.VMEM((blocks * TILE, WIDTH), jnp.bfloat16)],
        input_output_aliases={before + i: 2 + groups + i for i in range(len(held))},
        compiler_params=params(),
    )(slot_row, *lists, *sums, basis, *held)
    return res[0], res[1], res[2 : 2 + groups], res[2 + groups :]


def step_kernel(ncols, groups, blocks, first, last, row_ref, fetch_ref, asked_ref, scale_ref, *refs):
    if not first:
        inv_ref, refs = refs[0], refs[1:]
    chunks, refs = refs[:ncols], refs[ncols:]
    got, refs = refs[:groups], refs[groups:]
    gram_ref, refs = refs[0], refs[1:]
    if last:
        y_ref, refs = refs[0], refs[1:]
    else:
        outs, refs = refs[:groups], refs[groups:]
    ubuf, acc, scaled = refs
    me, row = lax.axis_index("cols"), lax.axis_index("rows")
    per = chunks[0].shape[0]
    for d in range(groups):
        ubuf[d] = got[d][...]
    acc[...] = jnp.zeros_like(acc)
    for d in range(ncols):
        source = lax.rem(me + ncols - d, ncols)
        for p in range(per):
            slot = source * per + p
            which = jnp.bitwise_xor(fetch_ref[0, slot], row)
            place = pl.ds(pl.multiple_of(row_ref[0, slot] * TILE, TILE), TILE)
            acc[place, :] += jnp.dot(chunks[d][p], ubuf[which], preferred_element_type=jnp.float32)
    scale = scale_ref[...]
    y = acc[: blocks * TILE, :] * scale
    if not first:
        y = lax.dot_general(
            y, inv_ref[...], (((1,), (1,)), ((), ())), precision=HIGHEST, preferred_element_type=jnp.float32
        )
    if last:
        y_ref[...] = y
    else:
        scaled[...] = (y * scale).astype(jnp.bfloat16)
        send_blocks(scaled, [asked_ref[0, d] for d in range(groups)], outs)
    gram_ref[...] = lax.dot_general(
        y, y, (((0,), (0,)), ((), ())), precision=HIGHEST, preferred_element_type=jnp.float32
    )


def step(slot_row, slot_fetch, asked, scale, inverse, chunks, got, last):
    ncols, groups, rows = len(chunks), len(got), scale.shape[0]
    blocks = rows // TILE
    first = inverse is None
    shapes = [jax.ShapeDtypeStruct((WIDTH, WIDTH), jnp.float32)]
    if last:
        shapes += [jax.ShapeDtypeStruct((rows, WIDTH), jnp.float32)]
    else:
        shapes += [jax.ShapeDtypeStruct((TILE, WIDTH), jnp.bfloat16)] * groups
    res = pl.pallas_call(
        functools.partial(step_kernel, ncols, groups, blocks, first, last),
        out_shape=shapes,
        in_specs=[SMEM] * 3 + [VMEM] * ((1 if first else 2) + ncols + groups),
        out_specs=[VMEM] * len(shapes),
        scratch_shapes=[
            pltpu.VMEM((groups, TILE, WIDTH), jnp.bfloat16),
            pltpu.VMEM((rows + TILE, WIDTH), jnp.float32),
            pltpu.VMEM((rows, WIDTH), jnp.bfloat16),
        ],
        compiler_params=params(),
    )(slot_row, slot_fetch, asked, scale, *([] if first else [inverse]), *chunks, *got)
    return res[0], (res[1] if last else res[1:])


def factor_rows(matrix, out_ref):
    n = WIDTH
    lane = lax.broadcasted_iota(jnp.int32, (8, n), 1)
    parts = [matrix[8 * i : 8 * i + 8, :] for i in range(n // 8)]
    for j in range(0, n, GROUP):
        here = j // 8
        off = j % 8
        wide = lambda v: jnp.broadcast_to(v, (8, n))
        rows = [wide(parts[here][off + a : off + a + 1, :]) for a in range(GROUP)]
        piv = [[wide(rows[a][:, j + c : j + c + 1]) for c in range(a + 1)] for a in range(GROUP)]
        in_group = (lane >= j) & (lane < j + GROUP)
        rows = [jnp.where(in_group, jnp.where(lane == j + a, 1.0, 0.0), rows[a]) for a in range(GROUP)]
        low = [[None] * GROUP for _ in range(GROUP)]
        inv = []
        for c in range(GROUP):
            inv.append(1.0 / piv[c][c])
            for a in range(c + 1, GROUP):
                low[a][c] = piv[a][c] * inv[c]
            for a in range(c + 1, GROUP):
                for b in range(c + 1, a + 1):
                    piv[a][b] = piv[a][b] - low[a][c] * piv[b][c]
        for a in range(GROUP):
            for c in range(a):
                rows[a] = rows[a] - low[a][c] * rows[c]
        for a in range(GROUP):
            keep = jnp.where(lane <= j + a, rows[a], 0.0) * lax.rsqrt(piv[a][a])
            out_ref[j + a : j + a + 1, :] = keep[0:1, :]
        scaled = [rows[a] * inv[a] for a in range(GROUP)]
        for i in range(here + 1, n // 8):
            cols = [wide(parts[i][:, j + c : j + c + 1]) for c in range(GROUP)]
            new = jnp.where(in_group, 0.0, parts[i])
            for c in range(GROUP):
                for b in range(c):
                    cols[c] = cols[c] - low[c][b] * cols[b]
                new = new - cols[c] * scaled[c]
            parts[i] = new


def factor_kernel(npts, last, a_ref, b_ref, *refs):
    matrix = (a_ref[...] + b_ref[...]) * (1.0 / npts)
    if not last:
        factor_rows(matrix, refs[0])
        return
    y_ref, v_ref, inv = refs
    factor_rows(matrix, inv)
    v_ref[...] = lax.dot_general(
        y_ref[...], inv[...], (((1,), (1,)), ((), ())), precision=HIGHEST, preferred_element_type=jnp.float32
    ).astype(v_ref.dtype)


def factor(pair, npts, y=None):
    square = jax.ShapeDtypeStruct((WIDTH, WIDTH), jnp.float32)
    last = y is not None
    return pl.pallas_call(
        functools.partial(factor_kernel, npts, last),
        out_shape=jax.ShapeDtypeStruct(y.shape, jnp.bfloat16) if last else square,
        in_specs=[VMEM] * (3 if last else 2),
        out_specs=VMEM,
        scratch_shapes=[pltpu.VMEM((WIDTH, WIDTH), jnp.float32)] if last else [],
        compiler_params=params(),
    )(*pair, *([y] if last else []))


def swap(x, axis, n, d):
    return lax.ppermute(x, axis, [(i, i ^ d) for i in range(n)])


def shift(x, axis, n, d):
    return lax.ppermute(x, axis, [(i, (i + d) % n) for i in range(n)])


def on_device(tiles, send_slot, slot_row, slot_fetch, fetch_list, basis):
    groups = lax.axis_size("rows")
    ncols = lax.axis_size("cols")
    npts = basis.shape[0] * groups * ncols
    early, _ = pack(tiles, send_slot, ncols, [1])
    chunks = [None, shift(early[0], "cols", ncols, 1)]
    late, sums = pack(tiles, send_slot, ncols, [*range(2, ncols), 0], early)
    sums = [sums[0]] + [shift(sums[d], "cols", ncols, d) for d in range(1, ncols)]
    lists = [fetch_list] + [swap(fetch_list, "rows", groups, d) for d in range(1, groups)]
    scale, asked, out, held = start(slot_row, lists, sums, basis, late[:-1])
    chunks[0] = late[-1]
    chunks += [shift(held[d - 2], "cols", ncols, d) for d in range(2, ncols)]
    stages = [("rows", groups, 1 << i) for i in range(groups.bit_length() - 1)]
    stages += [("cols", ncols, 1 << i) for i in range(ncols.bit_length() - 1)]
    inverse = None
    for k in range(ITERS):
        got = [out[0]] + [swap(out[d], "rows", groups, d) for d in range(1, groups)]
        gram, out = step(slot_row, slot_fetch, asked, scale, inverse, chunks, got, k == ITERS - 1)
        for i, stage in enumerate(stages):
            other = swap(gram, *stage)
            if i < len(stages) - 1:
                gram = gram + other
        inverse = factor((gram, other), npts, out if k == ITERS - 1 else None)
    return inverse


def solution(mesh):
    in_specs = (
        P(("rows", "cols"), None, None),
        P(("rows", "cols"), None),
        P(("rows", "cols"), None),
        P(("rows", "cols"), None),
        P(("rows", "cols"), None),
        P(("rows", "cols"), None),
    )
    out_specs = P(("rows", "cols"), None)
    return jax.shard_map(
        on_device, mesh=mesh, in_specs=in_specs, out_specs=out_specs, check_vma=False
    )
```

```python
import functools

import jax
import jax.numpy as jnp
from jax import lax
from jax.experimental import pallas as pl
from jax.experimental.pallas import tpu as pltpu
from jax.sharding import PartitionSpec as P

TILE = 256
WIDTH = 128
ITERS = 6
GROUP = 8
HIGHEST = lax.Precision.HIGHEST
VMEM = pl.BlockSpec(memory_space=pltpu.VMEM)
SMEM = pl.BlockSpec(memory_space=pltpu.SMEM)
ANY = pl.BlockSpec(memory_space=pl.ANY)


def params():
    return pltpu.CompilerParams(vmem_limit_bytes=32 * 1024 * 1024)


def pack_kernel(ncols, per, send_ref, tiles_ref, *refs):
    outs, sums, inverse = refs[:ncols], refs[ncols : 2 * ncols], refs[2 * ncols]
    me = lax.axis_index("cols")

    def note(i, carry):
        inverse[send_ref[0, i]] = i
        return carry

    lax.fori_loop(0, ncols * per, note, 0)
    lane = lax.broadcasted_iota(jnp.int32, (TILE, WIDTH), 1)
    total = jnp.zeros((TILE, WIDTH), jnp.float32)
    for d in range(ncols):
        dest = lax.rem(me + d, ncols)
        for p in range(per):
            tile = tiles_ref[inverse[dest * per + p]]
            outs[d][p] = tile
            pick = jnp.where(lane == d * per + p, 1.0, 0.0).astype(jnp.bfloat16)
            total = total + jnp.dot(jnp.abs(tile), pick, preferred_element_type=jnp.float32)
    flat = jnp.transpose(total)
    for d in range(ncols):
        sums[d][...] = flat[d * per : (d + 1) * per, :]


def pack(tiles, send_slot, ncols):
    nslots = tiles.shape[0]
    per = nslots // ncols
    shapes = [jax.ShapeDtypeStruct((per, TILE, TILE), tiles.dtype)] * ncols
    shapes += [jax.ShapeDtypeStruct((per, TILE), jnp.float32)] * ncols
    res = pl.pallas_call(
        functools.partial(pack_kernel, ncols, per),
        out_shape=shapes,
        in_specs=[SMEM, VMEM],
        out_specs=[VMEM] * len(shapes),
        scratch_shapes=[pltpu.SMEM((nslots,), jnp.int32)],
        compiler_params=params(),
    )(send_slot, tiles)
    return res[:ncols], res[ncols:]


def start_kernel(ncols, blocks, held, row_ref, *refs):
    sums, basis_ref, refs = refs[:ncols], refs[ncols], refs[ncols + 1 + held :]
    scale_ref, u_ref = refs[0], refs[1]
    me = lax.axis_index("cols")
    per = sums[0].shape[0]
    degree = [jnp.ones((1, TILE), jnp.float32) for _ in range(blocks)]
    for d in range(ncols):
        source = lax.rem(me + ncols - d, ncols)
        for p in range(per):
            at = row_ref[0, source * per + p]
            line = sums[d][p : p + 1, :]
            for j in range(blocks):
                degree[j] = degree[j] + jnp.where(at == j, line, jnp.zeros_like(line))
    for j in range(blocks):
        here = slice(j * TILE, (j + 1) * TILE)
        scale = jnp.transpose(jnp.broadcast_to(lax.rsqrt(degree[j]), (WIDTH, TILE)))
        scale_ref[here, :] = scale
        u_ref[here, :] = (scale * basis_ref[here, :].astype(jnp.float32)).astype(jnp.bfloat16)


def start(slot_row, sums, basis, held):
    ncols, rows = len(sums), basis.shape[0]
    shapes = [
        jax.ShapeDtypeStruct((rows, WIDTH), jnp.float32),
        jax.ShapeDtypeStruct((rows, WIDTH), jnp.bfloat16),
    ] + [jax.ShapeDtypeStruct(x.shape, x.dtype) for x in held]
    res = pl.pallas_call(
        functools.partial(start_kernel, ncols, rows // TILE, len(held)),
        out_shape=shapes,
        in_specs=[SMEM] + [VMEM] * (ncols + 1) + [ANY] * len(held),
        out_specs=[VMEM] * 2 + [ANY] * len(held),
        input_output_aliases={2 + ncols + i: 2 + i for i in range(len(held))},
        compiler_params=params(),
    )(slot_row, *sums, basis, *held)
    return res[0], res[1], res[2:]


def step_kernel(ncols, blocks, first, last, row_ref, fetch_ref, list_ref, scale_ref, *refs):
    if not first:
        inv_ref, refs = refs[0], refs[1:]
    chunks, got, gram_ref, out_ref, acc = refs[:ncols], *refs[ncols:]
    me = lax.axis_index("cols")
    per = chunks[0].shape[0]
    acc[...] = jnp.zeros_like(acc)
    for d in range(ncols):
        source = lax.rem(me + ncols - d, ncols)
        for p in range(per):
            slot = source * per + p
            group = fetch_ref[0, slot]
            block = pl.ds(pl.multiple_of(list_ref[0, group] * TILE, TILE), TILE)
            place = pl.ds(pl.multiple_of(row_ref[0, slot] * TILE, TILE), TILE)
            acc[place, :] += jnp.dot(chunks[d][p], got[group, block, :], preferred_element_type=jnp.float32)
    scale = scale_ref[...]
    y = acc[: blocks * TILE, :] * scale
    if not first:
        y = lax.dot_general(
            y, inv_ref[...], (((1,), (1,)), ((), ())), precision=HIGHEST, preferred_element_type=jnp.float32
        )
    out_ref[...] = y if last else (y * scale).astype(jnp.bfloat16)
    gram_ref[...] = lax.dot_general(
        y, y, (((0,), (0,)), ((), ())), precision=HIGHEST, preferred_element_type=jnp.float32
    )


def step(slot_row, slot_fetch, fetch_list, scale, inverse, chunks, got, last):
    ncols, rows = len(chunks), scale.shape[0]
    first = inverse is None
    return pl.pallas_call(
        functools.partial(step_kernel, ncols, rows // TILE, first, last),
        out_shape=[
            jax.ShapeDtypeStruct((WIDTH, WIDTH), jnp.float32),
            jax.ShapeDtypeStruct((rows, WIDTH), jnp.float32 if last else jnp.bfloat16),
        ],
        in_specs=[SMEM] * 3 + [VMEM] * ((1 if first else 2) + ncols + 1),
        out_specs=[VMEM] * 2,
        scratch_shapes=[pltpu.VMEM((rows + TILE, WIDTH), jnp.float32)],
        compiler_params=params(),
    )(slot_row, slot_fetch, fetch_list, scale, *([] if first else [inverse]), *chunks, got)


def factor_rows(matrix, out_ref):
    n = WIDTH
    lane = lax.broadcasted_iota(jnp.int32, (8, n), 1)
    parts = [matrix[8 * i : 8 * i + 8, :] for i in range(n // 8)]
    for j in range(0, n, GROUP):
        here = j // 8
        off = j % 8
        wide = lambda v: jnp.broadcast_to(v, (8, n))
        rows = [wide(parts[here][off + a : off + a + 1, :]) for a in range(GROUP)]
        piv = [[wide(rows[a][:, j + c : j + c + 1]) for c in range(a + 1)] for a in range(GROUP)]
        in_group = (lane >= j) & (lane < j + GROUP)
        rows = [jnp.where(in_group, jnp.where(lane == j + a, 1.0, 0.0), rows[a]) for a in range(GROUP)]
        low = [[None] * GROUP for _ in range(GROUP)]
        inv = []
        for c in range(GROUP):
            inv.append(1.0 / piv[c][c])
            for a in range(c + 1, GROUP):
                low[a][c] = piv[a][c] * inv[c]
            for a in range(c + 1, GROUP):
                for b in range(c + 1, a + 1):
                    piv[a][b] = piv[a][b] - low[a][c] * piv[b][c]
        for a in range(GROUP):
            for c in range(a):
                rows[a] = rows[a] - low[a][c] * rows[c]
        for a in range(GROUP):
            keep = jnp.where(lane <= j + a, rows[a], 0.0) * lax.rsqrt(piv[a][a])
            out_ref[j + a : j + a + 1, :] = keep[0:1, :]
        scaled = [rows[a] * inv[a] for a in range(GROUP)]
        for i in range(here + 1, n // 8):
            cols = [wide(parts[i][:, j + c : j + c + 1]) for c in range(GROUP)]
            new = jnp.where(in_group, 0.0, parts[i])
            for c in range(GROUP):
                for b in range(c):
                    cols[c] = cols[c] - low[c][b] * cols[b]
                new = new - cols[c] * scaled[c]
            parts[i] = new


def factor_kernel(npts, last, a_ref, b_ref, *refs):
    matrix = (a_ref[...] + b_ref[...]) * (1.0 / npts)
    if not last:
        factor_rows(matrix, refs[0])
        return
    y_ref, v_ref, inv = refs
    factor_rows(matrix, inv)
    v_ref[...] = lax.dot_general(
        y_ref[...], inv[...], (((1,), (1,)), ((), ())), precision=HIGHEST, preferred_element_type=jnp.float32
    ).astype(v_ref.dtype)


def factor(pair, npts, y=None):
    square = jax.ShapeDtypeStruct((WIDTH, WIDTH), jnp.float32)
    last = y is not None
    return pl.pallas_call(
        functools.partial(factor_kernel, npts, last),
        out_shape=jax.ShapeDtypeStruct(y.shape, jnp.bfloat16) if last else square,
        in_specs=[VMEM] * (3 if last else 2),
        out_specs=VMEM,
        scratch_shapes=[pltpu.VMEM((WIDTH, WIDTH), jnp.float32)] if last else [],
        compiler_params=params(),
    )(*pair, *([y] if last else []))


def swap(x, axis, n, d):
    return lax.ppermute(x, axis, [(i, i ^ d) for i in range(n)])


def shift(x, axis, n, d):
    return lax.ppermute(x, axis, [(i, (i + d) % n) for i in range(n)])


def on_device(tiles, send_slot, slot_row, slot_fetch, fetch_list, basis):
    groups = lax.axis_size("rows")
    ncols = lax.axis_size("cols")
    npts = basis.shape[0] * groups * ncols
    chunks, sums = pack(tiles, send_slot, ncols)
    sums = [sums[0]] + [shift(sums[d], "cols", ncols, d) for d in range(1, ncols)]
    scale, out, held = start(slot_row, sums, basis, chunks[2:])
    chunks = [*chunks[:2], *held]
    chunks = [chunks[0]] + [shift(chunks[d], "cols", ncols, d) for d in range(1, ncols)]
    stages = [("rows", groups, 1 << i) for i in range(groups.bit_length() - 1)]
    stages += [("cols", ncols, 1 << i) for i in range(ncols.bit_length() - 1)]
    inverse = None
    for k in range(ITERS):
        got = lax.all_gather(out, "rows")
        last = k == ITERS - 1
        gram, out = step(slot_row, slot_fetch, fetch_list, scale, inverse, chunks, got, last)
        for i, stage in enumerate(stages):
            other = swap(gram, *stage)
            if i < len(stages) - 1:
                gram = gram + other
        inverse = factor((gram, other), npts, out if last else None)
    return inverse


def solution(mesh):
    in_specs = (
        P(("rows", "cols"), None, None),
        P(("rows", "cols"), None),
        P(("rows", "cols"), None),
        P(("rows", "cols"), None),
        P(("rows", "cols"), None),
        P(("rows", "cols"), None),
    )
    out_specs = P(("rows", "cols"), None)
    return jax.shard_map(
        on_device, mesh=mesh, in_specs=in_specs, out_specs=out_specs, check_vma=False
    )
```

```python
import functools

import jax
import jax.numpy as jnp
from jax import lax
from jax.experimental import pallas as pl
from jax.experimental.pallas import tpu as pltpu
from jax.sharding import PartitionSpec as P

TILE = 256
WIDTH = 128
ITERS = 6
GROUP = 8
HALF = WIDTH // 2
HIGHEST = lax.Precision.HIGHEST
VMEM = pl.BlockSpec(memory_space=pltpu.VMEM)
SMEM = pl.BlockSpec(memory_space=pltpu.SMEM)
ANY = pl.BlockSpec(memory_space=pl.ANY)


def params():
    return pltpu.CompilerParams(vmem_limit_bytes=32 * 1024 * 1024)


def pack_kernel(ncols, per, shifts, send_ref, tiles_ref, *refs):
    outs, inverse = refs[-1 - len(shifts) : -1], refs[-1]
    me = lax.axis_index("cols")

    def note(i, carry):
        inverse[send_ref[0, i]] = i
        return carry

    lax.fori_loop(0, ncols * per, note, 0)
    for d, out in zip(shifts, outs):
        dest = lax.rem(me + d, ncols)
        for p in range(per):
            out[p] = tiles_ref[inverse[dest * per + p]]


def pack(tiles, send_slot, ncols, shifts, after=()):
    nslots = tiles.shape[0]
    per = nslots // ncols
    return pl.pallas_call(
        functools.partial(pack_kernel, ncols, per, shifts),
        out_shape=[jax.ShapeDtypeStruct((per, TILE, TILE), tiles.dtype)] * len(shifts),
        in_specs=[SMEM, VMEM] + [ANY] * len(after),
        out_specs=[VMEM] * len(shifts),
        scratch_shapes=[pltpu.SMEM((nslots,), jnp.int32)],
        compiler_params=params(),
    )(send_slot, tiles, *after)


def later_kernel(list_ref, after_ref, out_ref):
    for g in range(out_ref.shape[1]):
        out_ref[0, g] = list_ref[0, g]


def later(fetch_list, after):
    return pl.pallas_call(
        later_kernel,
        out_shape=jax.ShapeDtypeStruct(fetch_list.shape, fetch_list.dtype),
        in_specs=[SMEM, ANY],
        out_specs=SMEM,
        compiler_params=params(),
    )(fetch_list, after)


def sums_kernel(ncols, per, send_ref, tiles_ref, first_ref, *refs):
    stay, sums, inverse = refs[0], refs[1:-1], refs[-1]
    me = lax.axis_index("cols")

    def note(i, carry):
        inverse[send_ref[0, i]] = i
        return carry

    lax.fori_loop(0, ncols * per, note, 0)
    lane = lax.broadcasted_iota(jnp.int32, (TILE, WIDTH), 1)
    total = jnp.zeros((TILE, WIDTH), jnp.float32)
    for d in range(ncols):
        dest = lax.rem(me + d, ncols)
        for p in range(per):
            tile = tiles_ref[inverse[dest * per + p]]
            if d == 0:
                stay[p] = tile
            pick = jnp.where(lane == d * per + p, 1.0, 0.0).astype(jnp.bfloat16)
            total = total + jnp.dot(jnp.abs(tile), pick, preferred_element_type=jnp.float32)
    flat = jnp.transpose(total)
    for d in range(ncols):
        sums[d][...] = flat[d * per : (d + 1) * per, :]


def row_sums(tiles, send_slot, ncols, first):
    nslots = tiles.shape[0]
    per = nslots // ncols
    res = pl.pallas_call(
        functools.partial(sums_kernel, ncols, per),
        out_shape=[jax.ShapeDtypeStruct((per, TILE, TILE), tiles.dtype)]
        + [jax.ShapeDtypeStruct((per, TILE), jnp.float32)] * ncols,
        in_specs=[SMEM, VMEM, ANY],
        out_specs=[VMEM] * (1 + ncols),
        scratch_shapes=[pltpu.SMEM((nslots,), jnp.int32)],
        compiler_params=params(),
    )(send_slot, tiles, first)
    return res[0], res[1:]


def send_blocks(scaled, wanted, outs):
    for d, out in enumerate(outs):
        out[...] = scaled[pl.ds(pl.multiple_of(wanted[d] * TILE, TILE), TILE), :]


def start_kernel(ncols, groups, blocks, row_ref, *refs):
    lists, refs = refs[:groups], refs[groups:]
    sums, (basis_ref, scale_ref, asked_ref, *outs, scaled) = refs[:ncols], refs[ncols:]
    me, row = lax.axis_index("cols"), lax.axis_index("rows")
    per = sums[0].shape[0]
    degree = [jnp.ones((1, TILE), jnp.float32) for _ in range(blocks)]
    for d in range(ncols):
        source = lax.rem(me + ncols - d, ncols)
        for p in range(per):
            at = row_ref[0, source * per + p]
            line = sums[d][p : p + 1, :]
            for j in range(blocks):
                degree[j] = degree[j] + jnp.where(at == j, line, jnp.zeros_like(line))
    for j in range(blocks):
        here = slice(j * TILE, (j + 1) * TILE)
        scale = jnp.transpose(jnp.broadcast_to(lax.rsqrt(degree[j]), (WIDTH, TILE)))
        scale_ref[here, :] = scale
        scaled[here, :] = (scale * basis_ref[here, :].astype(jnp.float32)).astype(jnp.bfloat16)
    wanted = [lists[d][0, row] for d in range(groups)]
    for d in range(groups):
        asked_ref[0, d] = wanted[d]
    send_blocks(scaled, wanted, outs)


def start(slot_row, lists, sums, basis):
    ncols, groups, rows = len(sums), len(lists), basis.shape[0]
    res = pl.pallas_call(
        functools.partial(start_kernel, ncols, groups, rows // TILE),
        out_shape=[
            jax.ShapeDtypeStruct((rows, WIDTH), jnp.float32),
            jax.ShapeDtypeStruct((1, groups), jnp.int32),
        ]
        + [jax.ShapeDtypeStruct((TILE, WIDTH), jnp.bfloat16)] * groups,
        in_specs=[SMEM] * (1 + groups) + [VMEM] * (ncols + 1),
        out_specs=[VMEM, SMEM] + [VMEM] * groups,
        scratch_shapes=[pltpu.VMEM((rows, WIDTH), jnp.bfloat16)],
        compiler_params=params(),
    )(slot_row, *lists, *sums, basis)
    return res[0], res[1], res[2:]


def step_kernel(ncols, groups, first, last, row_ref, fetch_ref, asked_ref, scale_ref, *refs):
    if not first:
        inv_ref, refs = refs[0], refs[1:]
    chunks, got, refs = refs[:ncols], refs[ncols : ncols + groups], refs[ncols + groups :]
    gram_ref, outs, (held, acc, scaled) = refs[0], refs[1:-3], refs[-3:]
    me, row = lax.axis_index("cols"), lax.axis_index("rows")
    per, rows = chunks[0].shape[0], scale_ref.shape[0]
    for d in range(groups):
        held[d] = got[d][...]
    acc[...] = jnp.zeros_like(acc)
    for d in range(ncols):
        source = lax.rem(me + ncols - d, ncols)
        for p in range(per):
            slot = source * per + p
            which = jnp.bitwise_xor(fetch_ref[0, slot], row)
            place = pl.ds(pl.multiple_of(row_ref[0, slot] * TILE, TILE), TILE)
            acc[place, :] += jnp.dot(chunks[d][p], held[which], preferred_element_type=jnp.float32)
    scale = scale_ref[...]
    y = acc[:rows, :] * scale
    if not first:
        y = lax.dot_general(
            y, inv_ref[...], (((1,), (1,)), ((), ())), precision=HIGHEST, preferred_element_type=jnp.float32
        )
    if last:
        outs[0][...] = y
    else:
        scaled[...] = (y * scale).astype(jnp.bfloat16)
        send_blocks(scaled, [asked_ref[0, d] for d in range(groups)], outs)
    gram = lax.dot_general(
        y, y, (((0,), (0,)), ((), ())), precision=HIGHEST, preferred_element_type=jnp.float32
    )
    gram_ref[:HALF, :], gram_ref[HALF:, :] = fold(gram)


def step(slot_row, slot_fetch, asked, scale, inverse, chunks, got, last):
    ncols, groups, rows = len(chunks), len(got), scale.shape[0]
    first = inverse is None
    if last:
        shapes = [jax.ShapeDtypeStruct((rows, WIDTH), jnp.float32)]
    else:
        shapes = [jax.ShapeDtypeStruct((TILE, WIDTH), jnp.bfloat16)] * groups
    res = pl.pallas_call(
        functools.partial(step_kernel, ncols, groups, first, last),
        out_shape=[jax.ShapeDtypeStruct((HALF + 8, WIDTH), jnp.float32)] + shapes,
        in_specs=[SMEM] * 3 + [VMEM] * ((1 if first else 2) + ncols + groups),
        out_specs=[VMEM] * (1 + len(shapes)),
        scratch_shapes=[
            pltpu.VMEM((groups, TILE, WIDTH), jnp.bfloat16),
            pltpu.VMEM((rows + TILE, WIDTH), jnp.float32),
            pltpu.VMEM((rows, WIDTH), jnp.bfloat16),
        ],
        compiler_params=params(),
    )(slot_row, slot_fetch, asked, scale, *([] if first else [inverse]), *chunks, *got)
    return res[0], (res[1] if last else res[1:])


def fold(square):
    row = lax.broadcasted_iota(jnp.int32, (HALF, WIDTH), 0)
    lane = lax.broadcasted_iota(jnp.int32, (HALF, WIDTH), 1)
    low = square[HALF:, :]
    moved = pltpu.roll(low, HALF, 1)
    main = jnp.where((lane < HALF) & (lane > row), moved, square[:HALF, :])
    diagonal = jnp.sum(jnp.where(lane == row + HALF, low, 0.0), axis=0, keepdims=True)
    return main, jnp.broadcast_to(diagonal, (8, WIDTH))


def unfold(folded):
    row = lax.broadcasted_iota(jnp.int32, (HALF, WIDTH), 0)
    lane = lax.broadcasted_iota(jnp.int32, (HALF, WIDTH), 1)
    main = folded[:HALF, :]
    diagonal = jnp.broadcast_to(folded[HALF : HALF + 1, :], (HALF, WIDTH))
    upper = jnp.where((lane >= HALF) | (lane <= row), main, 0.0)
    moved = pltpu.roll(main, HALF, 1)
    lower = jnp.where(lane > row + HALF, moved, jnp.where(lane == row + HALF, diagonal, 0.0))
    whole = jnp.concatenate([upper, lower], axis=0)
    row = lax.broadcasted_iota(jnp.int32, (WIDTH, WIDTH), 0)
    lane = lax.broadcasted_iota(jnp.int32, (WIDTH, WIDTH), 1)
    return jnp.where(row == lane, whole, whole + jnp.transpose(whole))


def factor_rows(matrix, out_ref):
    n = WIDTH
    lane = lax.broadcasted_iota(jnp.int32, (8, n), 1)
    parts = [matrix[8 * i : 8 * i + 8, :] for i in range(n // 8)]
    for j in range(0, n, GROUP):
        here = j // 8
        off = j % 8
        wide = lambda v: jnp.broadcast_to(v, (8, n))
        rows = [wide(parts[here][off + a : off + a + 1, :]) for a in range(GROUP)]
        piv = [[wide(rows[a][:, j + c : j + c + 1]) for c in range(a + 1)] for a in range(GROUP)]
        in_group = (lane >= j) & (lane < j + GROUP)
        rows = [jnp.where(in_group, jnp.where(lane == j + a, 1.0, 0.0), rows[a]) for a in range(GROUP)]
        low = [[None] * GROUP for _ in range(GROUP)]
        inv = []
        for c in range(GROUP):
            inv.append(1.0 / piv[c][c])
            for a in range(c + 1, GROUP):
                low[a][c] = piv[a][c] * inv[c]
            for a in range(c + 1, GROUP):
                for b in range(c + 1, a + 1):
                    piv[a][b] = piv[a][b] - low[a][c] * piv[b][c]
        for a in range(GROUP):
            for c in range(a):
                rows[a] = rows[a] - low[a][c] * rows[c]
        for a in range(GROUP):
            keep = jnp.where(lane <= j + a, rows[a], 0.0) * lax.rsqrt(piv[a][a])
            out_ref[j + a : j + a + 1, :] = keep[0:1, :]
        scaled = [rows[a] * inv[a] for a in range(GROUP)]
        for i in range(here + 1, n // 8):
            cols = [wide(parts[i][:, j + c : j + c + 1]) for c in range(GROUP)]
            new = jnp.where(in_group, 0.0, parts[i])
            for c in range(GROUP):
                for b in range(c):
                    cols[c] = cols[c] - low[c][b] * cols[b]
                new = new - cols[c] * scaled[c]
            parts[i] = new


def factor_kernel(npts, a_ref, b_ref, inv_ref):
    factor_rows(unfold(a_ref[...] + b_ref[...]) * (1.0 / npts), inv_ref)


def factor(pair, npts):
    return pl.pallas_call(
        functools.partial(factor_kernel, npts),
        out_shape=jax.ShapeDtypeStruct((WIDTH, WIDTH), jnp.float32),
        in_specs=[VMEM] * 2,
        out_specs=VMEM,
        compiler_params=params(),
    )(*pair)


def finish_kernel(npts, a_ref, b_ref, y_ref, v_ref, inv):
    factor_rows(unfold(a_ref[...] + b_ref[...]) * (1.0 / npts), inv)
    v_ref[...] = lax.dot_general(
        y_ref[...], inv[...], (((1,), (1,)), ((), ())), precision=HIGHEST, preferred_element_type=jnp.float32
    ).astype(v_ref.dtype)


def finish(pair, y, npts):
    return pl.pallas_call(
        functools.partial(finish_kernel, npts),
        out_shape=jax.ShapeDtypeStruct(y.shape, jnp.bfloat16),
        in_specs=[VMEM] * 3,
        out_specs=VMEM,
        scratch_shapes=[pltpu.VMEM((WIDTH, WIDTH), jnp.float32)],
        compiler_params=params(),
    )(*pair, y)


def swap(x, axis, n, d):
    return lax.ppermute(x, axis, [(i, i ^ d) for i in range(n)])


def shift(x, axis, n, d):
    return lax.ppermute(x, axis, [(i, (i + d) % n) for i in range(n)])


def on_device(tiles, send_slot, slot_row, slot_fetch, fetch_list, basis):
    groups = lax.axis_size("rows")
    ncols = lax.axis_size("cols")
    npts = basis.shape[0] * groups * ncols
    chunks = [None] * ncols
    (early,) = pack(tiles, send_slot, ncols, [1])
    chunks[1] = shift(early, "cols", ncols, 1)
    chunks[0], sums = row_sums(tiles, send_slot, ncols, early)
    sums = [sums[0]] + [shift(sums[d], "cols", ncols, d) for d in range(1, ncols)]
    shifts = list(range(2, ncols))
    late = pack(tiles, send_slot, ncols, shifts, sums[1:])
    for d, chunk in zip(shifts, late):
        chunks[d] = shift(chunk, "cols", ncols, d)
    wish = later(fetch_list, late[0])
    lists = [wish] + [swap(wish, "rows", groups, d) for d in range(1, groups)]
    scale, asked, out = start(slot_row, lists, sums, basis)
    stages = [("rows", groups, 1 << i) for i in range(groups.bit_length() - 1)]
    stages += [("cols", ncols, 1 << i) for i in range(ncols.bit_length() - 1)]
    inverse = None
    for k in range(ITERS):
        got = [out[0]] + [swap(out[d], "rows", groups, d) for d in range(1, groups)]
        last = k == ITERS - 1
        gram, out = step(slot_row, slot_fetch, asked, scale, inverse, chunks, got, last)
        for i, stage in enumerate(stages):
            other = swap(gram, *stage)
            pair = (gram, other)
            gram = gram + other
        if not last:
            inverse = factor(pair, npts)
    return finish(pair, out, npts)


def solution(mesh):
    in_specs = (
        P(("rows", "cols"), None, None),
        P(("rows", "cols"), None),
        P(("rows", "cols"), None),
        P(("rows", "cols"), None),
        P(("rows", "cols"), None),
        P(("rows", "cols"), None),
    )
    out_specs = P(("rows", "cols"), None)
    return jax.shard_map(
        on_device, mesh=mesh, in_specs=in_specs, out_specs=out_specs, check_vma=False
    )
```

```python
import functools

import jax
import jax.numpy as jnp
from jax import lax
from jax.experimental import pallas as pl
from jax.experimental.pallas import tpu as pltpu
from jax.sharding import PartitionSpec as P

TILE = 256
WIDTH = 128
ITERS = 6
GROUP = 8
HALF = WIDTH // 2
HIGHEST = lax.Precision.HIGHEST
VMEM = pl.BlockSpec(memory_space=pltpu.VMEM)
SMEM = pl.BlockSpec(memory_space=pltpu.SMEM)
ANY = pl.BlockSpec(memory_space=pl.ANY)


def params():
    return pltpu.CompilerParams(vmem_limit_bytes=32 * 1024 * 1024)


def pack_kernel(ncols, per, shifts, send_ref, tiles_ref, *refs):
    outs, inverse = refs[-1 - len(shifts) : -1], refs[-1]
    me = lax.axis_index("cols")

    def note(i, carry):
        inverse[send_ref[0, i]] = i
        return carry

    lax.fori_loop(0, ncols * per, note, 0)
    for d, out in zip(shifts, outs):
        dest = lax.rem(me + d, ncols)
        for p in range(per):
            out[p] = tiles_ref[inverse[dest * per + p]]


def pack(tiles, send_slot, ncols, shifts, after=()):
    nslots = tiles.shape[0]
    per = nslots // ncols
    return pl.pallas_call(
        functools.partial(pack_kernel, ncols, per, shifts),
        out_shape=[jax.ShapeDtypeStruct((per, TILE, TILE), tiles.dtype)] * len(shifts),
        in_specs=[SMEM, VMEM] + [ANY] * len(after),
        out_specs=[VMEM] * len(shifts),
        scratch_shapes=[pltpu.SMEM((nslots,), jnp.int32)],
        compiler_params=params(),
    )(send_slot, tiles, *after)


def later_kernel(list_ref, after_ref, out_ref):
    for g in range(out_ref.shape[1]):
        out_ref[0, g] = list_ref[0, g]


def later(fetch_list, after):
    return pl.pallas_call(
        later_kernel,
        out_shape=jax.ShapeDtypeStruct(fetch_list.shape, fetch_list.dtype),
        in_specs=[SMEM, ANY],
        out_specs=SMEM,
        compiler_params=params(),
    )(fetch_list, after)


def sums_kernel(ncols, per, send_ref, tiles_ref, first_ref, *refs):
    stay, sums, inverse = refs[0], refs[1:-1], refs[-1]
    me = lax.axis_index("cols")

    def note(i, carry):
        inverse[send_ref[0, i]] = i
        return carry

    lax.fori_loop(0, ncols * per, note, 0)
    lane = lax.broadcasted_iota(jnp.int32, (TILE, WIDTH), 1)
    total = jnp.zeros((TILE, WIDTH), jnp.float32)
    for d in range(ncols):
        dest = lax.rem(me + d, ncols)
        for p in range(per):
            tile = tiles_ref[inverse[dest * per + p]]
            if d == 0:
                stay[p] = tile
            pick = jnp.where(lane == d * per + p, 1.0, 0.0).astype(jnp.bfloat16)
            total = total + jnp.dot(jnp.abs(tile), pick, preferred_element_type=jnp.float32)
    flat = jnp.transpose(total)
    for d in range(ncols):
        sums[d][...] = flat[d * per : (d + 1) * per, :]


def row_sums(tiles, send_slot, ncols, first):
    nslots = tiles.shape[0]
    per = nslots // ncols
    res = pl.pallas_call(
        functools.partial(sums_kernel, ncols, per),
        out_shape=[jax.ShapeDtypeStruct((per, TILE, TILE), tiles.dtype)]
        + [jax.ShapeDtypeStruct((per, TILE), jnp.float32)] * ncols,
        in_specs=[SMEM, VMEM, ANY],
        out_specs=[VMEM] * (1 + ncols),
        scratch_shapes=[pltpu.SMEM((nslots,), jnp.int32)],
        compiler_params=params(),
    )(send_slot, tiles, first)
    return res[0], res[1:]


def send_blocks(scaled, wanted, outs):
    for d, out in enumerate(outs):
        out[...] = scaled[pl.ds(pl.multiple_of(wanted[d] * TILE, TILE), TILE), :]


def start_kernel(ncols, groups, blocks, row_ref, *refs):
    lists, refs = refs[:groups], refs[groups:]
    sums, (basis_ref, scale_ref, asked_ref, *outs, scaled) = refs[:ncols], refs[ncols:]
    me, row = lax.axis_index("cols"), lax.axis_index("rows")
    per = sums[0].shape[0]
    degree = [jnp.ones((1, TILE), jnp.float32) for _ in range(blocks)]
    for d in range(ncols):
        source = lax.rem(me + ncols - d, ncols)
        for p in range(per):
            at = row_ref[0, source * per + p]
            line = sums[d][p : p + 1, :]
            for j in range(blocks):
                degree[j] = degree[j] + jnp.where(at == j, line, jnp.zeros_like(line))
    for j in range(blocks):
        here = slice(j * TILE, (j + 1) * TILE)
        scale = jnp.transpose(jnp.broadcast_to(lax.rsqrt(degree[j]), (WIDTH, TILE)))
        scale_ref[here, :] = scale
        scaled[here, :] = (scale * basis_ref[here, :].astype(jnp.float32)).astype(jnp.bfloat16)
    wanted = [lists[d][0, row] for d in range(groups)]
    for d in range(groups):
        asked_ref[0, d] = wanted[d]
    send_blocks(scaled, wanted, outs)


def start(slot_row, lists, sums, basis):
    ncols, groups, rows = len(sums), len(lists), basis.shape[0]
    res = pl.pallas_call(
        functools.partial(start_kernel, ncols, groups, rows // TILE),
        out_shape=[
            jax.ShapeDtypeStruct((rows, WIDTH), jnp.float32),
            jax.ShapeDtypeStruct((1, groups), jnp.int32),
        ]
        + [jax.ShapeDtypeStruct((TILE, WIDTH), jnp.bfloat16)] * groups,
        in_specs=[SMEM] * (1 + groups) + [VMEM] * (ncols + 1),
        out_specs=[VMEM, SMEM] + [VMEM] * groups,
        scratch_shapes=[pltpu.VMEM((rows, WIDTH), jnp.bfloat16)],
        compiler_params=params(),
    )(slot_row, *lists, *sums, basis)
    return res[0], res[1], res[2:]


def gram_of(y):
    return lax.dot_general(
        y, y, (((0,), (0,)), ((), ())), precision=HIGHEST, preferred_element_type=jnp.float32
    )


def times(a, b, transposed=False):
    return lax.dot_general(
        a, b, (((1,), (1 if transposed else 0,)), ((), ())), precision=HIGHEST, preferred_element_type=jnp.float32
    )


def step_kernel(ncols, groups, first, last, row_ref, fetch_ref, asked_ref, scale_ref, *refs):
    chunks, got, refs = refs[:ncols], refs[ncols : ncols + groups], refs[ncols + groups :]
    outs, (held, acc, scaled) = refs[:-3], refs[-3:]
    me, row = lax.axis_index("cols"), lax.axis_index("rows")
    per, rows = chunks[0].shape[0], scale_ref.shape[0]
    for d in range(groups):
        held[d] = got[d][...]
    acc[...] = jnp.zeros_like(acc)
    for d in range(ncols):
        source = lax.rem(me + ncols - d, ncols)
        for p in range(per):
            slot = source * per + p
            which = jnp.bitwise_xor(fetch_ref[0, slot], row)
            place = pl.ds(pl.multiple_of(row_ref[0, slot] * TILE, TILE), TILE)
            acc[place, :] += jnp.dot(chunks[d][p], held[which], preferred_element_type=jnp.float32)
    scale = scale_ref[...]
    y = acc[:rows, :] * scale
    if last:
        outs[0][...] = y
        return
    gram_ref, outs = outs[0], outs[1:]
    gram_ref[:HALF, :], gram_ref[HALF:, :] = fold(gram_of(y))
    if first:
        scaled[...] = (y * scale).astype(jnp.bfloat16)
        send_blocks(scaled, [asked_ref[0, d] for d in range(groups)], outs)
    else:
        outs[0][...] = y


def step(slot_row, slot_fetch, asked, scale, chunks, got, first, last):
    ncols, groups, rows = len(chunks), len(got), scale.shape[0]
    shapes = [] if last else [jax.ShapeDtypeStruct((HALF + 8, WIDTH), jnp.float32)]
    if first:
        shapes += [jax.ShapeDtypeStruct((TILE, WIDTH), jnp.bfloat16)] * groups
    else:
        shapes += [jax.ShapeDtypeStruct((rows, WIDTH), jnp.float32)]
    res = pl.pallas_call(
        functools.partial(step_kernel, ncols, groups, first, last),
        out_shape=shapes,
        in_specs=[SMEM] * 3 + [VMEM] * (1 + ncols + groups),
        out_specs=[VMEM] * len(shapes),
        scratch_shapes=[
            pltpu.VMEM((groups, TILE, WIDTH), jnp.bfloat16),
            pltpu.VMEM((rows + TILE, WIDTH), jnp.float32),
            pltpu.VMEM((rows, WIDTH), jnp.bfloat16),
        ],
        compiler_params=params(),
    )(slot_row, slot_fetch, asked, scale, *chunks, *got)
    if last:
        return None, res[0]
    return res[0], (res[1:] if first else res[1])


def turn_kernel(npts, groups, first, last, asked_ref, a_ref, b_ref, scale_ref, p_ref, *refs):
    if not first:
        before_ref, before_inv_ref, refs = refs[0], refs[1], refs[2:]
    outs, (inv, scaled) = refs[:-2], refs[-2:]
    gram = unfold(a_ref[...] + b_ref[...]) * (1.0 / npts)
    factor_rows(gram, inv)
    both = inv[...]
    mine = both if first else times(both, before_ref[...])
    y = times(p_ref[...], mine, True)
    if last:
        gram_ref, y_ref = outs
        y_ref[...] = y
        gram_ref[:HALF, :], gram_ref[HALF:, :] = fold(gram_of(y))
        return
    low_ref, inv_ref, outs = outs[0], outs[1], outs[2:]
    scaled[...] = (y * scale_ref[...]).astype(jnp.bfloat16)
    send_blocks(scaled, [asked_ref[0, d] for d in range(groups)], outs)
    low = times(gram, both, True)
    low_ref[...] = low if first else times(before_inv_ref[...], low)
    inv_ref[...] = mine


def turn(asked, pair, scale, p, before, npts, last):
    rows, groups = p.shape[0], asked.shape[1]
    first = before is None
    square = jax.ShapeDtypeStruct((WIDTH, WIDTH), jnp.float32)
    if last:
        shapes = [jax.ShapeDtypeStruct((HALF + 8, WIDTH), jnp.float32), jax.ShapeDtypeStruct(p.shape, p.dtype)]
    else:
        shapes = [square] * 2 + [jax.ShapeDtypeStruct((TILE, WIDTH), jnp.bfloat16)] * groups
    return pl.pallas_call(
        functools.partial(turn_kernel, npts, groups, first, last),
        out_shape=shapes,
        in_specs=[SMEM] + [VMEM] * (4 if first else 6),
        out_specs=[VMEM] * len(shapes),
        scratch_shapes=[pltpu.VMEM((WIDTH, WIDTH), jnp.float32), pltpu.VMEM((rows, WIDTH), jnp.bfloat16)],
        compiler_params=params(),
    )(asked, *pair, scale, p, *([] if first else before))


def fold(square):
    row = lax.broadcasted_iota(jnp.int32, (HALF, WIDTH), 0)
    lane = lax.broadcasted_iota(jnp.int32, (HALF, WIDTH), 1)
    low = square[HALF:, :]
    moved = pltpu.roll(low, HALF, 1)
    main = jnp.where((lane < HALF) & (lane > row), moved, square[:HALF, :])
    diagonal = jnp.sum(jnp.where(lane == row + HALF, low, 0.0), axis=0, keepdims=True)
    return main, jnp.broadcast_to(diagonal, (8, WIDTH))


def unfold(folded):
    row = lax.broadcasted_iota(jnp.int32, (HALF, WIDTH), 0)
    lane = lax.broadcasted_iota(jnp.int32, (HALF, WIDTH), 1)
    main = folded[:HALF, :]
    diagonal = jnp.broadcast_to(folded[HALF : HALF + 1, :], (HALF, WIDTH))
    upper = jnp.where((lane >= HALF) | (lane <= row), main, 0.0)
    moved = pltpu.roll(main, HALF, 1)
    lower = jnp.where(lane > row + HALF, moved, jnp.where(lane == row + HALF, diagonal, 0.0))
    whole = jnp.concatenate([upper, lower], axis=0)
    row = lax.broadcasted_iota(jnp.int32, (WIDTH, WIDTH), 0)
    lane = lax.broadcasted_iota(jnp.int32, (WIDTH, WIDTH), 1)
    return jnp.where(row == lane, whole, whole + jnp.transpose(whole))


def factor_rows(matrix, out_ref):
    n = WIDTH
    lane = lax.broadcasted_iota(jnp.int32, (8, n), 1)
    parts = [matrix[8 * i : 8 * i + 8, :] for i in range(n // 8)]
    for j in range(0, n, GROUP):
        here = j // 8
        off = j % 8
        wide = lambda v: jnp.broadcast_to(v, (8, n))
        rows = [wide(parts[here][off + a : off + a + 1, :]) for a in range(GROUP)]
        piv = [[wide(rows[a][:, j + c : j + c + 1]) for c in range(a + 1)] for a in range(GROUP)]
        in_group = (lane >= j) & (lane < j + GROUP)
        rows = [jnp.where(in_group, jnp.where(lane == j + a, 1.0, 0.0), rows[a]) for a in range(GROUP)]
        low = [[None] * GROUP for _ in range(GROUP)]
        inv = []
        for c in range(GROUP):
            inv.append(1.0 / piv[c][c])
            for a in range(c + 1, GROUP):
                low[a][c] = piv[a][c] * inv[c]
            for a in range(c + 1, GROUP):
                for b in range(c + 1, a + 1):
                    piv[a][b] = piv[a][b] - low[a][c] * piv[b][c]
        for a in range(GROUP):
            for c in range(a):
                rows[a] = rows[a] - low[a][c] * rows[c]
        for a in range(GROUP):
            keep = jnp.where(lane <= j + a, rows[a], 0.0) * lax.rsqrt(piv[a][a])
            out_ref[j + a : j + a + 1, :] = keep[0:1, :]
        scaled = [rows[a] * inv[a] for a in range(GROUP)]
        for i in range(here + 1, n // 8):
            cols = [wide(parts[i][:, j + c : j + c + 1]) for c in range(GROUP)]
            new = jnp.where(in_group, 0.0, parts[i])
            for c in range(GROUP):
                for b in range(c):
                    cols[c] = cols[c] - low[c][b] * cols[b]
                new = new - cols[c] * scaled[c]
            parts[i] = new


def finish_kernel(npts, a_ref, b_ref, y_ref, v_ref, inv):
    factor_rows(unfold(a_ref[...] + b_ref[...]) * (1.0 / npts), inv)
    v_ref[...] = times(y_ref[...], inv[...], True).astype(v_ref.dtype)


def finish(pair, y, npts):
    return pl.pallas_call(
        functools.partial(finish_kernel, npts),
        out_shape=jax.ShapeDtypeStruct(y.shape, jnp.bfloat16),
        in_specs=[VMEM] * 3,
        out_specs=VMEM,
        scratch_shapes=[pltpu.VMEM((WIDTH, WIDTH), jnp.float32)],
        compiler_params=params(),
    )(*pair, y)


def swap(x, axis, n, d):
    return lax.ppermute(x, axis, [(i, i ^ d) for i in range(n)])


def shift(x, axis, n, d):
    return lax.ppermute(x, axis, [(i, (i + d) % n) for i in range(n)])


def on_device(tiles, send_slot, slot_row, slot_fetch, fetch_list, basis):
    groups = lax.axis_size("rows")
    ncols = lax.axis_size("cols")
    npts = basis.shape[0] * groups * ncols
    chunks = [None] * ncols
    (early,) = pack(tiles, send_slot, ncols, [1])
    chunks[1] = shift(early, "cols", ncols, 1)
    chunks[0], sums = row_sums(tiles, send_slot, ncols, early)
    sums = [sums[0]] + [shift(sums[d], "cols", ncols, d) for d in range(1, ncols)]
    shifts = list(range(2, ncols))
    late = pack(tiles, send_slot, ncols, shifts, sums[1:])
    for d, chunk in zip(shifts, late):
        chunks[d] = shift(chunk, "cols", ncols, d)
    wish = later(fetch_list, late[0])
    lists = [wish] + [swap(wish, "rows", groups, d) for d in range(1, groups)]
    scale, asked, out = start(slot_row, lists, sums, basis)
    stages = [("rows", groups, 1 << i) for i in range(groups.bit_length() - 1)]
    stages += [("cols", ncols, 1 << i) for i in range(ncols.bit_length() - 1)]

    def total(gram):
        for stage in stages:
            pair = gram, swap(gram, *stage)
            gram = pair[0] + pair[1]
        return pair

    pair = before = None
    for k in range(ITERS):
        last = k == ITERS - 1
        got = [out[0]] + [swap(out[d], "rows", groups, d) for d in range(1, groups)]
        gram, out = step(slot_row, slot_fetch, asked, scale, chunks, got, k == 0, last)
        if k:
            res = turn(asked, pair, scale, out, before, npts, last)
            before, out = res[:2], res[2:]
        if not last:
            pair = total(gram)
    gram, y = res
    return finish(total(gram), y, npts)


def solution(mesh):
    in_specs = (
        P(("rows", "cols"), None, None),
        P(("rows", "cols"), None),
        P(("rows", "cols"), None),
        P(("rows", "cols"), None),
        P(("rows", "cols"), None),
        P(("rows", "cols"), None),
    )
    out_specs = P(("rows", "cols"), None)
    return jax.shard_map(
        on_device, mesh=mesh, in_specs=in_specs, out_specs=out_specs, check_vma=False
    )
```

```python
import functools

import jax
import jax.numpy as jnp
from jax import lax
from jax.experimental import pallas as pl
from jax.experimental.pallas import tpu as pltpu
from jax.sharding import PartitionSpec as P

TILE = 256
WIDTH = 128
ITERS = 6
GROUP = 8
HALF = WIDTH // 2
HIGHEST = lax.Precision.HIGHEST
VMEM = pl.BlockSpec(memory_space=pltpu.VMEM)
SMEM = pl.BlockSpec(memory_space=pltpu.SMEM)
ANY = pl.BlockSpec(memory_space=pl.ANY)


def params():
    return pltpu.CompilerParams(vmem_limit_bytes=32 * 1024 * 1024)


def pack_kernel(ncols, per, shifts, send_ref, tiles_ref, *refs):
    outs, inverse = refs[-1 - len(shifts) : -1], refs[-1]
    me = lax.axis_index("cols")

    def note(i, carry):
        inverse[send_ref[0, i]] = i
        return carry

    lax.fori_loop(0, ncols * per, note, 0)
    for d, out in zip(shifts, outs):
        dest = lax.rem(me + d, ncols)
        for p in range(per):
            out[p] = tiles_ref[inverse[dest * per + p]]


def pack(tiles, send_slot, ncols, shifts, after=()):
    nslots = tiles.shape[0]
    per = nslots // ncols
    shapes = [jax.ShapeDtypeStruct((per, TILE, TILE), tiles.dtype)] * len(shifts)
    return pl.pallas_call(
        functools.partial(pack_kernel, ncols, per, shifts),
        out_shape=shapes,
        in_specs=[SMEM, VMEM] + [ANY] * len(after),
        out_specs=[VMEM] * len(shapes),
        scratch_shapes=[pltpu.SMEM((nslots,), jnp.int32)],
        compiler_params=params(),
    )(send_slot, tiles, *after)


def later_kernel(list_ref, after_ref, out_ref):
    for g in range(out_ref.shape[1]):
        out_ref[0, g] = list_ref[0, g]


def later(fetch_list, after):
    return pl.pallas_call(
        later_kernel,
        out_shape=jax.ShapeDtypeStruct(fetch_list.shape, fetch_list.dtype),
        in_specs=[SMEM, ANY],
        out_specs=SMEM,
        compiler_params=params(),
    )(fetch_list, after)


def sums_kernel(ncols, per, send_ref, tiles_ref, first_ref, *refs):
    stay, sums, inverse = refs[0], refs[1:-1], refs[-1]
    me = lax.axis_index("cols")

    def note(i, carry):
        inverse[send_ref[0, i]] = i
        return carry

    lax.fori_loop(0, ncols * per, note, 0)
    lane = lax.broadcasted_iota(jnp.int32, (TILE, WIDTH), 1)
    total = jnp.zeros((TILE, WIDTH), jnp.float32)
    for d in range(ncols):
        dest = lax.rem(me + d, ncols)
        for p in range(per):
            tile = tiles_ref[inverse[dest * per + p]]
            if d == 0:
                stay[p] = tile
            pick = jnp.where(lane == d * per + p, 1.0, 0.0).astype(jnp.bfloat16)
            total = total + jnp.dot(jnp.abs(tile), pick, preferred_element_type=jnp.float32)
    flat = jnp.transpose(total)
    for d in range(ncols):
        sums[d][...] = flat[d * per : (d + 1) * per, :]


def row_sums(tiles, send_slot, ncols, first):
    nslots = tiles.shape[0]
    per = nslots // ncols
    res = pl.pallas_call(
        functools.partial(sums_kernel, ncols, per),
        out_shape=[jax.ShapeDtypeStruct((per, TILE, TILE), tiles.dtype)]
        + [jax.ShapeDtypeStruct((per, TILE), jnp.float32)] * ncols,
        in_specs=[SMEM, VMEM, ANY],
        out_specs=[VMEM] * (1 + ncols),
        scratch_shapes=[pltpu.SMEM((nslots,), jnp.int32)],
        compiler_params=params(),
    )(send_slot, tiles, first)
    return res[0], res[1:]


def send_blocks(scaled, wanted, outs):
    for d, out in enumerate(outs):
        out[...] = scaled[pl.ds(pl.multiple_of(wanted[d] * TILE, TILE), TILE), :]


def start_kernel(ncols, groups, blocks, row_ref, *refs):
    lists, refs = refs[:groups], refs[groups:]
    sums, (basis_ref, scale_ref, asked_ref, *outs, scaled) = refs[:ncols], refs[ncols:]
    me, row = lax.axis_index("cols"), lax.axis_index("rows")
    per = sums[0].shape[0]
    degree = [jnp.ones((1, TILE), jnp.float32) for _ in range(blocks)]
    for d in range(ncols):
        source = lax.rem(me + ncols - d, ncols)
        for p in range(per):
            at = row_ref[0, source * per + p]
            line = sums[d][p : p + 1, :]
            for j in range(blocks):
                degree[j] = degree[j] + jnp.where(at == j, line, jnp.zeros_like(line))
    for j in range(blocks):
        here = slice(j * TILE, (j + 1) * TILE)
        scale = jnp.transpose(jnp.broadcast_to(lax.rsqrt(degree[j]), (WIDTH, TILE)))
        scale_ref[here, :] = scale
        scaled[here, :] = (scale * basis_ref[here, :].astype(jnp.float32)).astype(jnp.bfloat16)
    wanted = [lists[d][0, row] for d in range(groups)]
    for d in range(groups):
        asked_ref[0, d] = wanted[d]
    send_blocks(scaled, wanted, outs)


def start(slot_row, lists, sums, basis):
    ncols, groups, rows = len(sums), len(lists), basis.shape[0]
    res = pl.pallas_call(
        functools.partial(start_kernel, ncols, groups, rows // TILE),
        out_shape=[
            jax.ShapeDtypeStruct((rows, WIDTH), jnp.float32),
            jax.ShapeDtypeStruct((1, groups), jnp.int32),
        ]
        + [jax.ShapeDtypeStruct((TILE, WIDTH), jnp.bfloat16)] * groups,
        in_specs=[SMEM] * (1 + groups) + [VMEM] * (ncols + 1),
        out_specs=[VMEM, SMEM] + [VMEM] * groups,
        scratch_shapes=[pltpu.VMEM((rows, WIDTH), jnp.bfloat16)],
        compiler_params=params(),
    )(slot_row, *lists, *sums, basis)
    return res[0], res[1], res[2:]


def gram_of(y):
    return lax.dot_general(
        y, y, (((0,), (0,)), ((), ())), precision=HIGHEST, preferred_element_type=jnp.float32
    )


def times(a, b, transposed=False):
    return lax.dot_general(
        a, b, (((1,), (1 if transposed else 0,)), ((), ())), precision=HIGHEST, preferred_element_type=jnp.float32
    )


def step_kernel(ncols, groups, first, row_ref, fetch_ref, asked_ref, scale_ref, *refs):
    chunks, got, refs = refs[:ncols], refs[ncols : ncols + groups], refs[ncols + groups :]
    outs, (held, acc, scaled) = refs[:-3], refs[-3:]
    me, row = lax.axis_index("cols"), lax.axis_index("rows")
    per, rows = chunks[0].shape[0], scale_ref.shape[0]
    for d in range(groups):
        held[d] = got[d][...]
    acc[...] = jnp.zeros_like(acc)
    for d in range(ncols):
        source = lax.rem(me + ncols - d, ncols)
        for p in range(per):
            slot = source * per + p
            which = jnp.bitwise_xor(fetch_ref[0, slot], row)
            place = pl.ds(pl.multiple_of(row_ref[0, slot] * TILE, TILE), TILE)
            acc[place, :] += jnp.dot(chunks[d][p], held[which], preferred_element_type=jnp.float32)
    scale = scale_ref[...]
    y = acc[:rows, :] * scale
    gram_ref, outs = outs[0], outs[1:]
    gram_ref[:HALF, :], gram_ref[HALF:, :] = fold(gram_of(y))
    if first:
        scaled[...] = (y * scale).astype(jnp.bfloat16)
        send_blocks(scaled, [asked_ref[0, d] for d in range(groups)], outs)
    else:
        outs[0][...] = y


def step(slot_row, slot_fetch, asked, scale, chunks, got, first):
    ncols, groups, rows = len(chunks), len(got), scale.shape[0]
    shapes = [jax.ShapeDtypeStruct((HALF + 8, WIDTH), jnp.float32)]
    if first:
        shapes += [jax.ShapeDtypeStruct((TILE, WIDTH), jnp.bfloat16)] * groups
    else:
        shapes += [jax.ShapeDtypeStruct((rows, WIDTH), jnp.float32)]
    res = pl.pallas_call(
        functools.partial(step_kernel, ncols, groups, first),
        out_shape=shapes,
        in_specs=[SMEM] * 3 + [VMEM] * (1 + ncols + groups),
        out_specs=[VMEM] * len(shapes),
        scratch_shapes=[
            pltpu.VMEM((groups, TILE, WIDTH), jnp.bfloat16),
            pltpu.VMEM((rows + TILE, WIDTH), jnp.float32),
            pltpu.VMEM((rows, WIDTH), jnp.bfloat16),
        ],
        compiler_params=params(),
    )(slot_row, slot_fetch, asked, scale, *chunks, *got)
    return res[0], (res[1:] if first else res[1])


def summed(refs):
    total = refs[0][...]
    for ref in refs[1:]:
        total = total + ref[...]
    return total


def turn_kernel(npts, groups, nparts, first, last, asked_ref, scale_ref, p_ref, *refs):
    parts, refs = refs[:nparts], refs[nparts:]
    if not first:
        before_ref, before_inv_ref, refs = refs[0], refs[1], refs[2:]
    outs, (inv, scaled) = refs[:-2], refs[-2:]
    gram = unfold(summed(parts)) * (1.0 / npts)
    factor_rows(gram, inv)
    both = inv[...]
    mine = both if first else times(both, before_ref[...])
    y = times(p_ref[...], mine, True)
    low_ref, inv_ref, outs = outs[0], outs[1], outs[2:]
    if last:
        outs[0][...] = y
    else:
        scaled[...] = (y * scale_ref[...]).astype(jnp.bfloat16)
        send_blocks(scaled, [asked_ref[0, d] for d in range(groups)], outs)
    low = times(gram, both, True)
    low_ref[...] = low if first else times(before_inv_ref[...], low)
    inv_ref[...] = mine


def turn(asked, parts, scale, p, before, npts, last):
    rows, groups = p.shape[0], asked.shape[1]
    first = before is None
    square = jax.ShapeDtypeStruct((WIDTH, WIDTH), jnp.float32)
    if last:
        shapes = [square] * 2 + [jax.ShapeDtypeStruct(p.shape, p.dtype)]
    else:
        shapes = [square] * 2 + [jax.ShapeDtypeStruct((TILE, WIDTH), jnp.bfloat16)] * groups
    return pl.pallas_call(
        functools.partial(turn_kernel, npts, groups, len(parts), first, last),
        out_shape=shapes,
        in_specs=[SMEM] + [VMEM] * (2 + len(parts) + (0 if first else 2)),
        out_specs=[VMEM] * len(shapes),
        scratch_shapes=[pltpu.VMEM((WIDTH, WIDTH), jnp.float32), pltpu.VMEM((rows, WIDTH), jnp.bfloat16)],
        compiler_params=params(),
    )(asked, scale, p, *parts, *([] if first else before))


def fold(square):
    row = lax.broadcasted_iota(jnp.int32, (HALF, WIDTH), 0)
    lane = lax.broadcasted_iota(jnp.int32, (HALF, WIDTH), 1)
    low = square[HALF:, :]
    moved = pltpu.roll(low, HALF, 1)
    main = jnp.where((lane < HALF) & (lane > row), moved, square[:HALF, :])
    diagonal = jnp.sum(jnp.where(lane == row + HALF, low, 0.0), axis=0, keepdims=True)
    return main, jnp.broadcast_to(diagonal, (8, WIDTH))


def unfold(folded):
    row = lax.broadcasted_iota(jnp.int32, (HALF, WIDTH), 0)
    lane = lax.broadcasted_iota(jnp.int32, (HALF, WIDTH), 1)
    main = folded[:HALF, :]
    diagonal = jnp.broadcast_to(folded[HALF : HALF + 1, :], (HALF, WIDTH))
    upper = jnp.where((lane >= HALF) | (lane <= row), main, 0.0)
    moved = pltpu.roll(main, HALF, 1)
    lower = jnp.where(lane > row + HALF, moved, jnp.where(lane == row + HALF, diagonal, 0.0))
    whole = jnp.concatenate([upper, lower], axis=0)
    row = lax.broadcasted_iota(jnp.int32, (WIDTH, WIDTH), 0)
    lane = lax.broadcasted_iota(jnp.int32, (WIDTH, WIDTH), 1)
    return jnp.where(row == lane, whole, whole + jnp.transpose(whole))


def factor_rows(matrix, out_ref):
    n = WIDTH
    lane = lax.broadcasted_iota(jnp.int32, (8, n), 1)
    parts = [matrix[8 * i : 8 * i + 8, :] for i in range(n // 8)]
    for j in range(0, n, GROUP):
        here = j // 8
        off = j % 8
        wide = lambda v: jnp.broadcast_to(v, (8, n))
        rows = [wide(parts[here][off + a : off + a + 1, :]) for a in range(GROUP)]
        piv = [[wide(rows[a][:, j + c : j + c + 1]) for c in range(a + 1)] for a in range(GROUP)]
        in_group = (lane >= j) & (lane < j + GROUP)
        rows = [jnp.where(in_group, jnp.where(lane == j + a, 1.0, 0.0), rows[a]) for a in range(GROUP)]
        low = [[None] * GROUP for _ in range(GROUP)]
        inv = []
        for c in range(GROUP):
            inv.append(1.0 / piv[c][c])
            for a in range(c + 1, GROUP):
                low[a][c] = piv[a][c] * inv[c]
            for a in range(c + 1, GROUP):
                for b in range(c + 1, a + 1):
                    piv[a][b] = piv[a][b] - low[a][c] * piv[b][c]
        for a in range(GROUP):
            for c in range(a):
                rows[a] = rows[a] - low[a][c] * rows[c]
        for a in range(GROUP):
            keep = jnp.where(lane <= j + a, rows[a], 0.0) * lax.rsqrt(piv[a][a])
            out_ref[j + a : j + a + 1, :] = keep[0:1, :]
        scaled = [rows[a] * inv[a] for a in range(GROUP)]
        for i in range(here + 1, n // 8):
            cols = [wide(parts[i][:, j + c : j + c + 1]) for c in range(GROUP)]
            new = jnp.where(in_group, 0.0, parts[i])
            for c in range(GROUP):
                for b in range(c):
                    cols[c] = cols[c] - low[c][b] * cols[b]
                new = new - cols[c] * scaled[c]
            parts[i] = new


def finish_kernel(npts, nparts, low_ref, y_ref, *refs):
    v_ref, inv = refs[nparts:]
    factor_rows(unfold(summed(refs[:nparts])) * (1.0 / npts), inv)
    v_ref[...] = times(y_ref[...], times(inv[...], low_ref[...]), True).astype(v_ref.dtype)


def finish(parts, low, y, npts):
    return pl.pallas_call(
        functools.partial(finish_kernel, npts, len(parts)),
        out_shape=jax.ShapeDtypeStruct(y.shape, jnp.bfloat16),
        in_specs=[VMEM] * (2 + len(parts)),
        out_specs=VMEM,
        scratch_shapes=[pltpu.VMEM((WIDTH, WIDTH), jnp.float32)],
        compiler_params=params(),
    )(low, y, *parts)


def swap(x, axis, n, d):
    return lax.ppermute(x, axis, [(i, i ^ d) for i in range(n)])


def shift(x, axis, n, d):
    return lax.ppermute(x, axis, [(i, (i + d) % n) for i in range(n)])


def on_device(tiles, send_slot, slot_row, slot_fetch, fetch_list, basis):
    groups = lax.axis_size("rows")
    ncols = lax.axis_size("cols")
    npts = basis.shape[0] * groups * ncols
    chunks = [None] * ncols
    (early,) = pack(tiles, send_slot, ncols, [1])
    chunks[1] = shift(early, "cols", ncols, 1)
    chunks[0], sums = row_sums(tiles, send_slot, ncols, early)
    sums = [sums[0]] + [shift(sums[d], "cols", ncols, d) for d in range(1, ncols)]
    shifts = list(range(2, ncols))
    late = pack(tiles, send_slot, ncols, shifts, sums[1:])
    for d, chunk in zip(shifts, late):
        chunks[d] = shift(chunk, "cols", ncols, d)
    wish = later(fetch_list, late[0])
    lists = [wish] + [swap(wish, "rows", groups, d) for d in range(1, groups)]
    scale, asked, out = start(slot_row, lists, sums, basis)
    stages = [("rows", groups, [1])]
    bit = 2
    while bit < groups:
        wide = bit * 2 < groups
        stages.append(("rows", groups, [bit, 2 * bit, 3 * bit] if wide else [bit]))
        bit *= 4 if wide else 2
    stages += [("cols", ncols, [1 << i]) for i in range(ncols.bit_length() - 1)]

    def total(gram):
        for axis, size, partners in stages:
            parts = [gram] + [swap(gram, axis, size, d) for d in partners]
            gram = sum(parts[1:], parts[0])
        return parts

    parts = before = None
    for k in range(ITERS):
        last = k == ITERS - 1
        got = [out[0]] + [swap(out[d], "rows", groups, d) for d in range(1, groups)]
        gram, out = step(slot_row, slot_fetch, asked, scale, chunks, got, k == 0)
        if k:
            res = turn(asked, parts, scale, out, before, npts, last)
            before, out = res[:2], res[2:]
        parts = total(gram)
    return finish(parts, before[0], out[0], npts)


def solution(mesh):
    in_specs = (
        P(("rows", "cols"), None, None),
        P(("rows", "cols"), None),
        P(("rows", "cols"), None),
        P(("rows", "cols"), None),
        P(("rows", "cols"), None),
        P(("rows", "cols"), None),
    )
    out_specs = P(("rows", "cols"), None)
    return jax.shard_map(
        on_device, mesh=mesh, in_specs=in_specs, out_specs=out_specs, check_vma=False
    )
```

```python
import functools

import jax
import jax.numpy as jnp
from jax import lax
from jax.experimental import pallas as pl
from jax.experimental.pallas import tpu as pltpu
from jax.sharding import PartitionSpec as P

TILE = 256
WIDTH = 128
ITERS = 6
GROUP = 8
HALF = WIDTH // 2
HIGHEST = lax.Precision.HIGHEST
VMEM = pl.BlockSpec(memory_space=pltpu.VMEM)
SMEM = pl.BlockSpec(memory_space=pltpu.SMEM)
ANY = pl.BlockSpec(memory_space=pl.ANY)


def params():
    return pltpu.CompilerParams(vmem_limit_bytes=32 * 1024 * 1024)


def pack_kernel(ncols, per, shifts, send_ref, tiles_ref, *refs):
    outs, inverse = refs[-1 - len(shifts) : -1], refs[-1]
    me = lax.axis_index("cols")

    def note(i, carry):
        inverse[send_ref[0, i]] = i
        return carry

    lax.fori_loop(0, ncols * per, note, 0)
    for d, out in zip(shifts, outs):
        dest = lax.rem(me + d, ncols)
        for p in range(per):
            out[p] = tiles_ref[inverse[dest * per + p]]


def pack(tiles, send_slot, ncols, shifts, after=()):
    nslots = tiles.shape[0]
    per = nslots // ncols
    shapes = [jax.ShapeDtypeStruct((per, TILE, TILE), tiles.dtype)] * len(shifts)
    return pl.pallas_call(
        functools.partial(pack_kernel, ncols, per, shifts),
        out_shape=shapes,
        in_specs=[SMEM, VMEM] + [ANY] * len(after),
        out_specs=[VMEM] * len(shapes),
        scratch_shapes=[pltpu.SMEM((nslots,), jnp.int32)],
        compiler_params=params(),
    )(send_slot, tiles, *after)


def later_kernel(list_ref, after_ref, out_ref):
    for g in range(out_ref.shape[1]):
        out_ref[0, g] = list_ref[0, g]


def later(fetch_list, after):
    return pl.pallas_call(
        later_kernel,
        out_shape=jax.ShapeDtypeStruct(fetch_list.shape, fetch_list.dtype),
        in_specs=[SMEM, ANY],
        out_specs=SMEM,
        compiler_params=params(),
    )(fetch_list, after)


def sums_kernel(ncols, per, send_ref, tiles_ref, first_ref, *refs):
    stay, sums, inverse = refs[0], refs[1:-1], refs[-1]
    me = lax.axis_index("cols")

    def note(i, carry):
        inverse[send_ref[0, i]] = i
        return carry

    lax.fori_loop(0, ncols * per, note, 0)
    lane = lax.broadcasted_iota(jnp.int32, (TILE, WIDTH), 1)
    total = jnp.zeros((TILE, WIDTH), jnp.float32)
    for d in range(ncols):
        dest = lax.rem(me + d, ncols)
        for p in range(per):
            tile = tiles_ref[inverse[dest * per + p]]
            if d == 0:
                stay[p] = tile
            pick = jnp.where(lane == d * per + p, 1.0, 0.0).astype(jnp.bfloat16)
            total = total + jnp.dot(jnp.abs(tile), pick, preferred_element_type=jnp.float32)
    flat = jnp.transpose(total)
    for d in range(ncols):
        sums[d][...] = flat[d * per : (d + 1) * per, :]


def row_sums(tiles, send_slot, ncols, first):
    nslots = tiles.shape[0]
    per = nslots // ncols
    res = pl.pallas_call(
        functools.partial(sums_kernel, ncols, per),
        out_shape=[jax.ShapeDtypeStruct((per, TILE, TILE), tiles.dtype)]
        + [jax.ShapeDtypeStruct((per, TILE), jnp.float32)] * ncols,
        in_specs=[SMEM, VMEM, ANY],
        out_specs=[VMEM] * (1 + ncols),
        scratch_shapes=[pltpu.SMEM((nslots,), jnp.int32)],
        compiler_params=params(),
    )(send_slot, tiles, first)
    return res[0], res[1:]


def send_blocks(scaled, wanted, outs):
    for d, out in enumerate(outs):
        out[...] = scaled[pl.ds(pl.multiple_of(wanted[d] * TILE, TILE), TILE), :]


def start_kernel(ncols, groups, blocks, row_ref, *refs):
    lists, refs = refs[:groups], refs[groups:]
    sums, (basis_ref, scale_ref, asked_ref, *outs, scaled) = refs[:ncols], refs[ncols:]
    me, row = lax.axis_index("cols"), lax.axis_index("rows")
    per = sums[0].shape[0]
    degree = [jnp.ones((1, TILE), jnp.float32) for _ in range(blocks)]
    for d in range(ncols):
        source = lax.rem(me + ncols - d, ncols)
        for p in range(per):
            at = row_ref[0, source * per + p]
            line = sums[d][p : p + 1, :]
            for j in range(blocks):
                degree[j] = degree[j] + jnp.where(at == j, line, jnp.zeros_like(line))
    for j in range(blocks):
        here = slice(j * TILE, (j + 1) * TILE)
        scale = jnp.transpose(jnp.broadcast_to(lax.rsqrt(degree[j]), (WIDTH, TILE)))
        scale_ref[here, :] = scale
        scaled[here, :] = (scale * basis_ref[here, :].astype(jnp.float32)).astype(jnp.bfloat16)
    wanted = [lists[d][0, row] for d in range(groups)]
    for d in range(groups):
        asked_ref[0, d] = wanted[d]
    send_blocks(scaled, wanted, outs)


def start(slot_row, lists, sums, basis):
    ncols, groups, rows = len(sums), len(lists), basis.shape[0]
    res = pl.pallas_call(
        functools.partial(start_kernel, ncols, groups, rows // TILE),
        out_shape=[
            jax.ShapeDtypeStruct((rows, WIDTH), jnp.float32),
            jax.ShapeDtypeStruct((1, groups), jnp.int32),
        ]
        + [jax.ShapeDtypeStruct((TILE, WIDTH), jnp.bfloat16)] * groups,
        in_specs=[SMEM] * (1 + groups) + [VMEM] * (ncols + 1),
        out_specs=[VMEM, SMEM] + [VMEM] * groups,
        scratch_shapes=[pltpu.VMEM((rows, WIDTH), jnp.bfloat16)],
        compiler_params=params(),
    )(slot_row, *lists, *sums, basis)
    return res[0], res[1], res[2:]


def gram_of(y):
    return lax.dot_general(
        y, y, (((0,), (0,)), ((), ())), precision=HIGHEST, preferred_element_type=jnp.float32
    )


def times(a, b, transposed=False):
    return lax.dot_general(
        a, b, (((1,), (1 if transposed else 0,)), ((), ())), precision=HIGHEST, preferred_element_type=jnp.float32
    )


def step_kernel(ncols, groups, first, last, row_ref, fetch_ref, asked_ref, scale_ref, *refs):
    chunks, got, refs = refs[:ncols], refs[ncols : ncols + groups], refs[ncols + groups :]
    outs, (held, acc, scaled) = refs[:-3], refs[-3:]
    me, row = lax.axis_index("cols"), lax.axis_index("rows")
    per, rows = chunks[0].shape[0], scale_ref.shape[0]
    for d in range(groups):
        held[d] = got[d][...]
    acc[...] = jnp.zeros_like(acc)
    for d in range(ncols):
        source = lax.rem(me + ncols - d, ncols)
        for p in range(per):
            slot = source * per + p
            which = jnp.bitwise_xor(fetch_ref[0, slot], row)
            place = pl.ds(pl.multiple_of(row_ref[0, slot] * TILE, TILE), TILE)
            acc[place, :] += jnp.dot(chunks[d][p], held[which], preferred_element_type=jnp.float32)
    scale = scale_ref[...]
    y = acc[:rows, :] * scale
    if last:
        outs[0][...] = y
        return
    gram_ref, outs = outs[0], outs[1:]
    gram_ref[:HALF, :], gram_ref[HALF:, :] = fold(gram_of(y))
    if first:
        scaled[...] = (y * scale).astype(jnp.bfloat16)
        send_blocks(scaled, [asked_ref[0, d] for d in range(groups)], outs)
    else:
        outs[0][...] = y


def step(slot_row, slot_fetch, asked, scale, chunks, got, first, last):
    ncols, groups, rows = len(chunks), len(got), scale.shape[0]
    shapes = [] if last else [jax.ShapeDtypeStruct((HALF + 8, WIDTH), jnp.float32)]
    if first:
        shapes += [jax.ShapeDtypeStruct((TILE, WIDTH), jnp.bfloat16)] * groups
    else:
        shapes += [jax.ShapeDtypeStruct((rows, WIDTH), jnp.float32)]
    res = pl.pallas_call(
        functools.partial(step_kernel, ncols, groups, first, last),
        out_shape=shapes,
        in_specs=[SMEM] * 3 + [VMEM] * (1 + ncols + groups),
        out_specs=[VMEM] * len(shapes),
        scratch_shapes=[
            pltpu.VMEM((groups, TILE, WIDTH), jnp.bfloat16),
            pltpu.VMEM((rows + TILE, WIDTH), jnp.float32),
            pltpu.VMEM((rows, WIDTH), jnp.bfloat16),
        ],
        compiler_params=params(),
    )(slot_row, slot_fetch, asked, scale, *chunks, *got)
    if last:
        return None, res[0]
    return res[0], (res[1:] if first else res[1])


def added(parts):
    while len(parts) > 1:
        parts = [parts[i] + parts[i + 1] for i in range(0, len(parts), 2)]
    return parts[0]


def summed(refs):
    return added([ref[...] for ref in refs])


def turn_kernel(npts, groups, nparts, first, last, asked_ref, scale_ref, p_ref, *refs):
    parts, refs = refs[:nparts], refs[nparts:]
    if not first:
        before_ref, before_inv_ref, refs = refs[0], refs[1], refs[2:]
    outs, (inv, scaled) = refs[:-2], refs[-2:]
    gram = unfold(summed(parts)) * (1.0 / npts)
    factor_rows(gram, inv)
    both = inv[...]
    mine = both if first else times(both, before_ref[...])
    y = times(p_ref[...], mine, True)
    if last:
        gram_ref, y_ref = outs
        y_ref[...] = y
        gram_ref[:HALF, :], gram_ref[HALF:, :] = fold(gram_of(y))
        return
    low_ref, inv_ref, outs = outs[0], outs[1], outs[2:]
    scaled[...] = (y * scale_ref[...]).astype(jnp.bfloat16)
    send_blocks(scaled, [asked_ref[0, d] for d in range(groups)], outs)
    low = times(gram, both, True)
    low_ref[...] = low if first else times(before_inv_ref[...], low)
    inv_ref[...] = mine


def turn(asked, parts, scale, p, before, npts, last):
    rows, groups = p.shape[0], asked.shape[1]
    first = before is None
    square = jax.ShapeDtypeStruct((WIDTH, WIDTH), jnp.float32)
    if last:
        shapes = [jax.ShapeDtypeStruct((HALF + 8, WIDTH), jnp.float32), jax.ShapeDtypeStruct(p.shape, p.dtype)]
    else:
        shapes = [square] * 2 + [jax.ShapeDtypeStruct((TILE, WIDTH), jnp.bfloat16)] * groups
    return pl.pallas_call(
        functools.partial(turn_kernel, npts, groups, len(parts), first, last),
        out_shape=shapes,
        in_specs=[SMEM] + [VMEM] * (2 + len(parts) + (0 if first else 2)),
        out_specs=[VMEM] * len(shapes),
        scratch_shapes=[pltpu.VMEM((WIDTH, WIDTH), jnp.float32), pltpu.VMEM((rows, WIDTH), jnp.bfloat16)],
        compiler_params=params(),
    )(asked, scale, p, *parts, *([] if first else before))


def fold(square):
    row = lax.broadcasted_iota(jnp.int32, (HALF, WIDTH), 0)
    lane = lax.broadcasted_iota(jnp.int32, (HALF, WIDTH), 1)
    low = square[HALF:, :]
    moved = pltpu.roll(low, HALF, 1)
    main = jnp.where((lane < HALF) & (lane > row), moved, square[:HALF, :])
    diagonal = jnp.sum(jnp.where(lane == row + HALF, low, 0.0), axis=0, keepdims=True)
    return main, jnp.broadcast_to(diagonal, (8, WIDTH))


def unfold(folded):
    row = lax.broadcasted_iota(jnp.int32, (HALF, WIDTH), 0)
    lane = lax.broadcasted_iota(jnp.int32, (HALF, WIDTH), 1)
    main = folded[:HALF, :]
    diagonal = jnp.broadcast_to(folded[HALF : HALF + 1, :], (HALF, WIDTH))
    upper = jnp.where((lane >= HALF) | (lane <= row), main, 0.0)
    moved = pltpu.roll(main, HALF, 1)
    lower = jnp.where(lane > row + HALF, moved, jnp.where(lane == row + HALF, diagonal, 0.0))
    whole = jnp.concatenate([upper, lower], axis=0)
    row = lax.broadcasted_iota(jnp.int32, (WIDTH, WIDTH), 0)
    lane = lax.broadcasted_iota(jnp.int32, (WIDTH, WIDTH), 1)
    return jnp.where(row == lane, whole, whole + jnp.transpose(whole))


def factor_rows(matrix, out_ref):
    n = WIDTH
    lane = lax.broadcasted_iota(jnp.int32, (8, n), 1)
    parts = [matrix[8 * i : 8 * i + 8, :] for i in range(n // 8)]
    for j in range(0, n, GROUP):
        here = j // 8
        off = j % 8
        wide = lambda v: jnp.broadcast_to(v, (8, n))
        rows = [wide(parts[here][off + a : off + a + 1, :]) for a in range(GROUP)]
        piv = [[wide(rows[a][:, j + c : j + c + 1]) for c in range(a + 1)] for a in range(GROUP)]
        in_group = (lane >= j) & (lane < j + GROUP)
        rows = [jnp.where(in_group, jnp.where(lane == j + a, 1.0, 0.0), rows[a]) for a in range(GROUP)]
        low = [[None] * GROUP for _ in range(GROUP)]
        inv = []
        for c in range(GROUP):
            inv.append(1.0 / piv[c][c])
            for a in range(c + 1, GROUP):
                low[a][c] = piv[a][c] * inv[c]
            for a in range(c + 1, GROUP):
                for b in range(c + 1, a + 1):
                    piv[a][b] = piv[a][b] - low[a][c] * piv[b][c]
        for a in range(GROUP):
            for c in range(a):
                rows[a] = rows[a] - low[a][c] * rows[c]
        for a in range(GROUP):
            keep = jnp.where(lane <= j + a, rows[a], 0.0) * lax.rsqrt(piv[a][a])
            out_ref[j + a : j + a + 1, :] = keep[0:1, :]
        scaled = [rows[a] * inv[a] for a in range(GROUP)]
        for c in reversed(range(GROUP)):
            for a in range(c):
                scaled[a] = scaled[a] - low[c][a] * scaled[c]
        for i in range(here + 1, n // 8):
            new = jnp.where(in_group, 0.0, parts[i])
            for c in range(GROUP):
                new = new - wide(parts[i][:, j + c : j + c + 1]) * scaled[c]
            parts[i] = new


def finish_kernel(npts, nparts, y_ref, *refs):
    v_ref, inv = refs[nparts:]
    factor_rows(unfold(summed(refs[:nparts])) * (1.0 / npts), inv)
    v_ref[...] = times(y_ref[...], inv[...], True).astype(v_ref.dtype)


def finish(parts, y, npts):
    return pl.pallas_call(
        functools.partial(finish_kernel, npts, len(parts)),
        out_shape=jax.ShapeDtypeStruct(y.shape, jnp.bfloat16),
        in_specs=[VMEM] * (1 + len(parts)),
        out_specs=VMEM,
        scratch_shapes=[pltpu.VMEM((WIDTH, WIDTH), jnp.float32)],
        compiler_params=params(),
    )(y, *parts)


def swap(x, axis, n, d):
    return lax.ppermute(x, axis, [(i, i ^ d) for i in range(n)])


def shift(x, axis, n, d):
    return lax.ppermute(x, axis, [(i, (i + d) % n) for i in range(n)])


def on_device(tiles, send_slot, slot_row, slot_fetch, fetch_list, basis):
    groups = lax.axis_size("rows")
    ncols = lax.axis_size("cols")
    npts = basis.shape[0] * groups * ncols
    chunks = [None] * ncols
    (early,) = pack(tiles, send_slot, ncols, [1])
    chunks[1] = shift(early, "cols", ncols, 1)
    chunks[0], sums = row_sums(tiles, send_slot, ncols, early)
    sums = [sums[0]] + [shift(sums[d], "cols", ncols, d) for d in range(1, ncols)]
    shifts = list(range(2, ncols))
    late = pack(tiles, send_slot, ncols, shifts, sums[1:])
    for d, chunk in zip(shifts, late):
        chunks[d] = shift(chunk, "cols", ncols, d)
    wish = later(fetch_list, late[0])
    lists = [wish] + [swap(wish, "rows", groups, d) for d in range(1, groups)]
    scale, asked, out = start(slot_row, lists, sums, basis)
    stages = [("rows", groups, [1])]
    bit = 2
    while bit < groups:
        wide = bit * 2 < groups
        stages.append(("rows", groups, [bit, 2 * bit, 3 * bit] if wide else [bit]))
        bit *= 4 if wide else 2
    apart = [("cols", ncols, [1 << i]) for i in range(ncols.bit_length() - 1)]
    at_once = [("cols", ncols, list(range(1, ncols)))]

    def total(gram, more):
        for axis, size, partners in stages + more:
            parts = [gram] + [swap(gram, axis, size, d) for d in partners]
            gram = added(parts)
        return parts

    parts = before = None
    for k in range(ITERS):
        last = k == ITERS - 1
        got = [out[0]] + [swap(out[d], "rows", groups, d) for d in range(1, groups)]
        gram, out = step(slot_row, slot_fetch, asked, scale, chunks, got, k == 0, last)
        if k:
            res = turn(asked, parts, scale, out, before, npts, last)
            before, out = res[:2], res[2:]
        if not last:
            parts = total(gram, apart)
    gram, y = res
    return finish(total(gram, at_once), y, npts)


def solution(mesh):
    in_specs = (
        P(("rows", "cols"), None, None),
        P(("rows", "cols"), None),
        P(("rows", "cols"), None),
        P(("rows", "cols"), None),
        P(("rows", "cols"), None),
        P(("rows", "cols"), None),
    )
    out_specs = P(("rows", "cols"), None)
    return jax.shard_map(
        on_device, mesh=mesh, in_specs=in_specs, out_specs=out_specs, check_vma=False
    )
```

```python
import functools

import jax
import jax.numpy as jnp
from jax import lax
from jax.experimental import pallas as pl
from jax.experimental.pallas import tpu as pltpu
from jax.sharding import PartitionSpec as P

TILE = 256
WIDTH = 128
ITERS = 6
GROUP = 8
HALF = WIDTH // 2
GROWTH = 60.0
HIGHEST = lax.Precision.HIGHEST
VMEM = pl.BlockSpec(memory_space=pltpu.VMEM)
SMEM = pl.BlockSpec(memory_space=pltpu.SMEM)
ANY = pl.BlockSpec(memory_space=pl.ANY)


def params():
    return pltpu.CompilerParams(vmem_limit_bytes=32 * 1024 * 1024)


def pack_kernel(ncols, per, shifts, send_ref, tiles_ref, *refs):
    outs, inverse = refs[-1 - len(shifts) : -1], refs[-1]
    me = lax.axis_index("cols")

    def note(i, carry):
        inverse[send_ref[0, i]] = i
        return carry

    lax.fori_loop(0, ncols * per, note, 0)
    for d, out in zip(shifts, outs):
        dest = lax.rem(me + d, ncols)
        for p in range(per):
            out[p] = tiles_ref[inverse[dest * per + p]]


def pack(tiles, send_slot, ncols, shifts, after=()):
    nslots = tiles.shape[0]
    per = nslots // ncols
    shapes = [jax.ShapeDtypeStruct((per, TILE, TILE), tiles.dtype)] * len(shifts)
    return pl.pallas_call(
        functools.partial(pack_kernel, ncols, per, shifts),
        out_shape=shapes,
        in_specs=[SMEM, VMEM] + [ANY] * len(after),
        out_specs=[VMEM] * len(shapes),
        scratch_shapes=[pltpu.SMEM((nslots,), jnp.int32)],
        compiler_params=params(),
    )(send_slot, tiles, *after)


def later_kernel(list_ref, after_ref, out_ref):
    for g in range(out_ref.shape[1]):
        out_ref[0, g] = list_ref[0, g]


def later(fetch_list, after):
    return pl.pallas_call(
        later_kernel,
        out_shape=jax.ShapeDtypeStruct(fetch_list.shape, fetch_list.dtype),
        in_specs=[SMEM, ANY],
        out_specs=SMEM,
        compiler_params=params(),
    )(fetch_list, after)


def sums_kernel(ncols, per, send_ref, tiles_ref, first_ref, *refs):
    stay, sums, inverse = refs[0], refs[1:-1], refs[-1]
    me = lax.axis_index("cols")

    def note(i, carry):
        inverse[send_ref[0, i]] = i
        return carry

    lax.fori_loop(0, ncols * per, note, 0)
    lane = lax.broadcasted_iota(jnp.int32, (TILE, WIDTH), 1)
    total = jnp.zeros((TILE, WIDTH), jnp.float32)
    for d in range(ncols):
        dest = lax.rem(me + d, ncols)
        for p in range(per):
            tile = tiles_ref[inverse[dest * per + p]]
            if d == 0:
                stay[p] = tile
            pick = jnp.where(lane == d * per + p, 1.0, 0.0).astype(jnp.bfloat16)
            total = total + jnp.dot(jnp.abs(tile), pick, preferred_element_type=jnp.float32)
    flat = jnp.transpose(total)
    for d in range(ncols):
        sums[d][...] = flat[d * per : (d + 1) * per, :]


def row_sums(tiles, send_slot, ncols, first):
    nslots = tiles.shape[0]
    per = nslots // ncols
    res = pl.pallas_call(
        functools.partial(sums_kernel, ncols, per),
        out_shape=[jax.ShapeDtypeStruct((per, TILE, TILE), tiles.dtype)]
        + [jax.ShapeDtypeStruct((per, TILE), jnp.float32)] * ncols,
        in_specs=[SMEM, VMEM, ANY],
        out_specs=[VMEM] * (1 + ncols),
        scratch_shapes=[pltpu.SMEM((nslots,), jnp.int32)],
        compiler_params=params(),
    )(send_slot, tiles, first)
    return res[0], res[1:]


def send_blocks(scaled, wanted, outs):
    for d, out in enumerate(outs):
        out[...] = scaled[pl.ds(pl.multiple_of(wanted[d] * TILE, TILE), TILE), :]


def start_kernel(ncols, groups, blocks, row_ref, *refs):
    lists, refs = refs[:groups], refs[groups:]
    sums, (basis_ref, scale_ref, asked_ref, *outs, scaled) = refs[:ncols], refs[ncols:]
    me, row = lax.axis_index("cols"), lax.axis_index("rows")
    per = sums[0].shape[0]
    degree = [jnp.ones((1, TILE), jnp.float32) for _ in range(blocks)]
    for d in range(ncols):
        source = lax.rem(me + ncols - d, ncols)
        for p in range(per):
            at = row_ref[0, source * per + p]
            line = sums[d][p : p + 1, :]
            for j in range(blocks):
                degree[j] = degree[j] + jnp.where(at == j, line, jnp.zeros_like(line))
    for j in range(blocks):
        here = slice(j * TILE, (j + 1) * TILE)
        scale = jnp.transpose(jnp.broadcast_to(lax.rsqrt(degree[j]), (WIDTH, TILE)))
        scale_ref[here, :] = scale
        scaled[here, :] = (scale * basis_ref[here, :].astype(jnp.float32)).astype(jnp.bfloat16)
    wanted = [lists[d][0, row] for d in range(groups)]
    for d in range(groups):
        asked_ref[0, d] = wanted[d]
    send_blocks(scaled, wanted, outs)


def start(slot_row, lists, sums, basis):
    ncols, groups, rows = len(sums), len(lists), basis.shape[0]
    res = pl.pallas_call(
        functools.partial(start_kernel, ncols, groups, rows // TILE),
        out_shape=[
            jax.ShapeDtypeStruct((rows, WIDTH), jnp.float32),
            jax.ShapeDtypeStruct((1, groups), jnp.int32),
        ]
        + [jax.ShapeDtypeStruct((TILE, WIDTH), jnp.bfloat16)] * groups,
        in_specs=[SMEM] * (1 + groups) + [VMEM] * (ncols + 1),
        out_specs=[VMEM, SMEM] + [VMEM] * groups,
        scratch_shapes=[pltpu.VMEM((rows, WIDTH), jnp.bfloat16)],
        compiler_params=params(),
    )(slot_row, *lists, *sums, basis)
    return res[0], res[1], res[2:]


def gram_of(y):
    return lax.dot_general(
        y, y, (((0,), (0,)), ((), ())), precision=HIGHEST, preferred_element_type=jnp.float32
    )


def times(a, b, transposed=False):
    return lax.dot_general(
        a, b, (((1,), (1 if transposed else 0,)), ((), ())), precision=HIGHEST, preferred_element_type=jnp.float32
    )


def step_kernel(ncols, groups, first, last, row_ref, fetch_ref, asked_ref, scale_ref, *refs):
    chunks, got, refs = refs[:ncols], refs[ncols : ncols + groups], refs[ncols + groups :]
    outs, (held, acc, scaled) = refs[:-3], refs[-3:]
    me, row = lax.axis_index("cols"), lax.axis_index("rows")
    per, rows = chunks[0].shape[0], scale_ref.shape[0]
    for d in range(groups):
        held[d] = got[d][...]
    acc[...] = jnp.zeros_like(acc)
    for d in range(ncols):
        source = lax.rem(me + ncols - d, ncols)
        for p in range(per):
            slot = source * per + p
            which = jnp.bitwise_xor(fetch_ref[0, slot], row)
            place = pl.ds(pl.multiple_of(row_ref[0, slot] * TILE, TILE), TILE)
            acc[place, :] += jnp.dot(chunks[d][p], held[which], preferred_element_type=jnp.float32)
    scale = scale_ref[...]
    y = acc[:rows, :] * scale
    if last:
        outs[0][...] = y
        return
    gram_ref, outs = outs[0], outs[1:]
    gram_ref[:HALF, :], gram_ref[HALF:, :] = fold(gram_of(y))
    if first:
        scaled[...] = (y * scale).astype(jnp.bfloat16)
        send_blocks(scaled, [asked_ref[0, d] for d in range(groups)], outs)
    else:
        outs[0][...] = y


def step(slot_row, slot_fetch, asked, scale, chunks, got, first, last):
    ncols, groups, rows = len(chunks), len(got), scale.shape[0]
    shapes = [] if last else [jax.ShapeDtypeStruct((HALF + 8, WIDTH), jnp.float32)]
    if first:
        shapes += [jax.ShapeDtypeStruct((TILE, WIDTH), jnp.bfloat16)] * groups
    else:
        shapes += [jax.ShapeDtypeStruct((rows, WIDTH), jnp.float32)]
    res = pl.pallas_call(
        functools.partial(step_kernel, ncols, groups, first, last),
        out_shape=shapes,
        in_specs=[SMEM] * 3 + [VMEM] * (1 + ncols + groups),
        out_specs=[VMEM] * len(shapes),
        scratch_shapes=[
            pltpu.VMEM((groups, TILE, WIDTH), jnp.bfloat16),
            pltpu.VMEM((rows + TILE, WIDTH), jnp.float32),
            pltpu.VMEM((rows, WIDTH), jnp.bfloat16),
        ],
        compiler_params=params(),
    )(slot_row, slot_fetch, asked, scale, *chunks, *got)
    if last:
        return None, res[0]
    return res[0], (res[1:] if first else res[1])


def added(parts):
    while len(parts) > 1:
        parts = [parts[i] + parts[i + 1] for i in range(0, len(parts), 2)]
    return parts[0]


def summed(refs):
    return added([ref[...] for ref in refs])


def turn_kernel(npts, groups, nparts, first, last, asked_ref, scale_ref, p_ref, *refs):
    parts, refs = refs[:nparts], refs[nparts:]
    if not first:
        before_ref, before_inv_ref, growth_ref, refs = refs[0], refs[1], refs[2], refs[3:]
    outs, (inv, scaled) = refs[:-2], refs[-2:]
    gram = unfold(summed(parts)) * (1.0 / npts)
    factor_rows(gram, inv)
    both = inv[...]
    mine = both if first else times(both, before_ref[...])
    y = times(p_ref[...], mine, True)
    if last:
        gram_ref, y_ref = outs[0], outs[1]
        y_ref[...] = y
        gram_ref[:HALF, :], gram_ref[HALF:, :] = fold(gram_of(y))
    else:
        scaled[...] = (y * scale_ref[...]).astype(jnp.bfloat16)
        send_blocks(scaled, [asked_ref[0, d] for d in range(groups)], outs[3:])
    low = times(gram, both, True)
    low = low if first else times(before_inv_ref[...], low)
    if not last:
        outs[0][...] = low
        outs[1][...] = mine
    weights = lax.dot_general(
        jnp.ones((8, WIDTH), jnp.float32), low * low, (((1,), (1,)), ((), ())), preferred_element_type=jnp.float32
    )
    growth = jnp.sum(mine * mine * weights[0:1, :]) * (1.0 / WIDTH)
    outs[2][...] = jnp.full((8, WIDTH), growth) + (0.0 if first else growth_ref[...])


def turn(asked, parts, scale, p, before, npts, last):
    rows, groups = p.shape[0], asked.shape[1]
    first = before is None
    square = jax.ShapeDtypeStruct((WIDTH, WIDTH), jnp.float32)
    growth = jax.ShapeDtypeStruct((8, WIDTH), jnp.float32)
    if last:
        shapes = [jax.ShapeDtypeStruct((HALF + 8, WIDTH), jnp.float32), jax.ShapeDtypeStruct(p.shape, p.dtype), growth]
    else:
        shapes = [square, square, growth] + [jax.ShapeDtypeStruct((TILE, WIDTH), jnp.bfloat16)] * groups
    return pl.pallas_call(
        functools.partial(turn_kernel, npts, groups, len(parts), first, last),
        out_shape=shapes,
        in_specs=[SMEM] + [VMEM] * (2 + len(parts) + (0 if first else 3)),
        out_specs=[VMEM] * len(shapes),
        scratch_shapes=[pltpu.VMEM((WIDTH, WIDTH), jnp.float32), pltpu.VMEM((rows, WIDTH), jnp.bfloat16)],
        compiler_params=params(),
    )(asked, scale, p, *parts, *([] if first else before))


def careful_kernel(npts, groups, nparts, asked_ref, scale_ref, y_ref, *refs):
    parts, (v_ref, *outs), (inv, scaled) = refs[:nparts], refs[nparts:-2], refs[-2:]
    factor_rows(unfold(summed(parts)) * (1.0 / npts), inv)
    v = times(y_ref[...], inv[...], True).astype(jnp.bfloat16)
    v_ref[...] = v
    scaled[...] = (v.astype(jnp.float32) * scale_ref[...]).astype(jnp.bfloat16)
    send_blocks(scaled, [asked_ref[0, d] for d in range(groups)], outs)


def careful(asked, parts, scale, y, npts):
    rows, groups = y.shape[0], asked.shape[1]
    res = pl.pallas_call(
        functools.partial(careful_kernel, npts, groups, len(parts)),
        out_shape=[jax.ShapeDtypeStruct(y.shape, jnp.bfloat16)]
        + [jax.ShapeDtypeStruct((TILE, WIDTH), jnp.bfloat16)] * groups,
        in_specs=[SMEM] + [VMEM] * (2 + len(parts)),
        out_specs=[VMEM] * (1 + groups),
        scratch_shapes=[pltpu.VMEM((WIDTH, WIDTH), jnp.float32), pltpu.VMEM((rows, WIDTH), jnp.bfloat16)],
        compiler_params=params(),
    )(asked, scale, y, *parts)
    return res[0], res[1:]


def fold(square):
    row = lax.broadcasted_iota(jnp.int32, (HALF, WIDTH), 0)
    lane = lax.broadcasted_iota(jnp.int32, (HALF, WIDTH), 1)
    low = square[HALF:, :]
    moved = pltpu.roll(low, HALF, 1)
    main = jnp.where((lane < HALF) & (lane > row), moved, square[:HALF, :])
    diagonal = jnp.sum(jnp.where(lane == row + HALF, low, 0.0), axis=0, keepdims=True)
    return main, jnp.broadcast_to(diagonal, (8, WIDTH))


def unfold(folded):
    row = lax.broadcasted_iota(jnp.int32, (HALF, WIDTH), 0)
    lane = lax.broadcasted_iota(jnp.int32, (HALF, WIDTH), 1)
    main = folded[:HALF, :]
    diagonal = jnp.broadcast_to(folded[HALF : HALF + 1, :], (HALF, WIDTH))
    upper = jnp.where((lane >= HALF) | (lane <= row), main, 0.0)
    moved = pltpu.roll(main, HALF, 1)
    lower = jnp.where(lane > row + HALF, moved, jnp.where(lane == row + HALF, diagonal, 0.0))
    whole = jnp.concatenate([upper, lower], axis=0)
    row = lax.broadcasted_iota(jnp.int32, (WIDTH, WIDTH), 0)
    lane = lax.broadcasted_iota(jnp.int32, (WIDTH, WIDTH), 1)
    return jnp.where(row == lane, whole, whole + jnp.transpose(whole))


def factor_rows(matrix, out_ref):
    n = WIDTH
    lane = lax.broadcasted_iota(jnp.int32, (8, n), 1)
    parts = [matrix[8 * i : 8 * i + 8, :] for i in range(n // 8)]
    for j in range(0, n, GROUP):
        here = j // 8
        off = j % 8
        wide = lambda v: jnp.broadcast_to(v, (8, n))
        rows = [wide(parts[here][off + a : off + a + 1, :]) for a in range(GROUP)]
        piv = [[wide(rows[a][:, j + c : j + c + 1]) for c in range(a + 1)] for a in range(GROUP)]
        in_group = (lane >= j) & (lane < j + GROUP)
        rows = [jnp.where(in_group, jnp.where(lane == j + a, 1.0, 0.0), rows[a]) for a in range(GROUP)]
        low = [[None] * GROUP for _ in range(GROUP)]
        inv = []
        for c in range(GROUP):
            inv.append(1.0 / piv[c][c])
            for a in range(c + 1, GROUP):
                low[a][c] = piv[a][c] * inv[c]
            for a in range(c + 1, GROUP):
                for b in range(c + 1, a + 1):
                    piv[a][b] = piv[a][b] - low[a][c] * piv[b][c]
        for a in range(GROUP):
            for c in range(a):
                rows[a] = rows[a] - low[a][c] * rows[c]
        for a in range(GROUP):
            keep = jnp.where(lane <= j + a, rows[a], 0.0) * lax.rsqrt(piv[a][a])
            out_ref[j + a : j + a + 1, :] = keep[0:1, :]
        scaled = [rows[a] * inv[a] for a in range(GROUP)]
        for i in range(here + 1, n // 8):
            cols = [wide(parts[i][:, j + c : j + c + 1]) for c in range(GROUP)]
            new = jnp.where(in_group, 0.0, parts[i])
            for c in range(GROUP):
                for b in range(c):
                    cols[c] = cols[c] - low[c][b] * cols[b]
                new = new - cols[c] * scaled[c]
            parts[i] = new


def finish_kernel(npts, nparts, y_ref, *refs):
    v_ref, inv = refs[nparts:]
    factor_rows(unfold(summed(refs[:nparts])) * (1.0 / npts), inv)
    v_ref[...] = times(y_ref[...], inv[...], True).astype(v_ref.dtype)


def finish(parts, y, npts):
    return pl.pallas_call(
        functools.partial(finish_kernel, npts, len(parts)),
        out_shape=jax.ShapeDtypeStruct(y.shape, jnp.bfloat16),
        in_specs=[VMEM] * (1 + len(parts)),
        out_specs=VMEM,
        scratch_shapes=[pltpu.VMEM((WIDTH, WIDTH), jnp.float32)],
        compiler_params=params(),
    )(y, *parts)


def swap(x, axis, n, d):
    return lax.ppermute(x, axis, [(i, i ^ d) for i in range(n)])


def shift(x, axis, n, d):
    return lax.ppermute(x, axis, [(i, (i + d) % n) for i in range(n)])


def on_device(tiles, send_slot, slot_row, slot_fetch, fetch_list, basis):
    groups = lax.axis_size("rows")
    ncols = lax.axis_size("cols")
    npts = basis.shape[0] * groups * ncols
    chunks = [None] * ncols
    (early,) = pack(tiles, send_slot, ncols, [1])
    chunks[1] = shift(early, "cols", ncols, 1)
    chunks[0], sums = row_sums(tiles, send_slot, ncols, early)
    sums = [sums[0]] + [shift(sums[d], "cols", ncols, d) for d in range(1, ncols)]
    shifts = list(range(2, ncols))
    late = pack(tiles, send_slot, ncols, shifts, sums[1:])
    for d, chunk in zip(shifts, late):
        chunks[d] = shift(chunk, "cols", ncols, d)
    wish = later(fetch_list, late[0])
    lists = [wish] + [swap(wish, "rows", groups, d) for d in range(1, groups)]
    scale, asked, out = start(slot_row, lists, sums, basis)
    stages = [("rows", groups, [1])]
    bit = 2
    while bit < groups:
        wide = bit * 2 < groups
        stages.append(("rows", groups, [bit, 2 * bit, 3 * bit] if wide else [bit]))
        bit *= 4 if wide else 2
    apart = [("cols", ncols, [1 << i]) for i in range(ncols.bit_length() - 1)]
    at_once = [("cols", ncols, list(range(1, ncols)))]

    def total(gram, more):
        for axis, size, partners in stages + more:
            parts = [gram] + [swap(gram, axis, size, d) for d in partners]
            gram = added(parts)
        return parts

    def fetched(out):
        return [out[0]] + [swap(out[d], "rows", groups, d) for d in range(1, groups)]

    first_out = out
    parts = before = None
    for k in range(ITERS):
        last = k == ITERS - 1
        gram, out = step(slot_row, slot_fetch, asked, scale, chunks, fetched(out), k == 0, last)
        if k:
            res = turn(asked, parts, scale, out, before, npts, last)
            before, out = res[:3], res[3:]
        if not last:
            parts = total(gram, apart)
    gram, y, growth = res
    fast = finish(total(gram, at_once), y, npts)

    def repeat(k, state):
        gram, y = step(slot_row, slot_fetch, asked, scale, chunks, fetched(state[1]), False, False)
        v, out = careful(asked, total(gram, apart), scale, y, npts)
        return v, tuple(out)

    return lax.cond(
        growth[0, 0] < GROWTH,
        lambda: fast,
        lambda: lax.fori_loop(0, ITERS, repeat, (fast, tuple(first_out)))[0],
    )


def solution(mesh):
    in_specs = (
        P(("rows", "cols"), None, None),
        P(("rows", "cols"), None),
        P(("rows", "cols"), None),
        P(("rows", "cols"), None),
        P(("rows", "cols"), None),
        P(("rows", "cols"), None),
    )
    out_specs = P(("rows", "cols"), None)
    return jax.shard_map(
        on_device, mesh=mesh, in_specs=in_specs, out_specs=out_specs, check_vma=False
    )
```

```python
import functools

import jax
import jax.numpy as jnp
from jax import lax
from jax.experimental import pallas as pl
from jax.experimental.pallas import tpu as pltpu
from jax.sharding import PartitionSpec as P

TILE = 256
WIDTH = 128
ITERS = 6
GROUP = 8
HALF = WIDTH // 2
GROWTH = 35.0
LEAD = 3
HIGHEST = lax.Precision.HIGHEST
VMEM = pl.BlockSpec(memory_space=pltpu.VMEM)
SMEM = pl.BlockSpec(memory_space=pltpu.SMEM)
ANY = pl.BlockSpec(memory_space=pl.ANY)


def params():
    return pltpu.CompilerParams(vmem_limit_bytes=32 * 1024 * 1024)


def find_inverse(send_ref, inverse):
    def note(i, carry):
        inverse[send_ref[0, i]] = i
        return carry

    lax.fori_loop(0, inverse.shape[0], note, 0)


def lead_kernel(ncols, per, send_ref, tiles_ref, sums_ref, *refs):
    stay, leads, inverse = refs[0], refs[1:-1], refs[-1]
    me = lax.axis_index("cols")
    find_inverse(send_ref, inverse)
    lane = lax.broadcasted_iota(jnp.int32, (TILE, WIDTH), 1)
    total = jnp.zeros((TILE, WIDTH), jnp.float32)
    half = per * LEAD // 8
    for d in range(ncols):
        dest = lax.rem(me + d, ncols)
        for p in range(per):
            tile = tiles_ref[inverse[dest * per + p]]
            if d == 0:
                stay[p] = tile
            elif p < half:
                leads[d - 1][p * TILE : (p + 1) * TILE, :] = tile
            pick = jnp.where(lane == d * per + p, 1.0, 0.0).astype(jnp.bfloat16)
            total = total + jnp.dot(jnp.abs(tile), pick, preferred_element_type=jnp.float32)
    flat = jnp.transpose(total)
    sums_ref[...] = flat[:per, :]
    for d in range(1, ncols):
        rest = flat[d * per : (d + 1) * per, :]
        pieces = []
        for _ in range(3):
            pieces.append(rest.astype(jnp.bfloat16).astype(jnp.float32))
            rest = rest - pieces[-1]
        pieces.append(jnp.zeros_like(rest))
        leads[d - 1][half * TILE :, :] = jnp.concatenate(pieces, axis=0).astype(jnp.bfloat16)


def lead(tiles, send_slot, ncols):
    nslots = tiles.shape[0]
    per = nslots // ncols
    res = pl.pallas_call(
        functools.partial(lead_kernel, ncols, per),
        out_shape=[
            jax.ShapeDtypeStruct((per, TILE), jnp.float32),
            jax.ShapeDtypeStruct((per, TILE, TILE), tiles.dtype),
        ]
        + [jax.ShapeDtypeStruct((per * LEAD // 8 * TILE + 4 * per, TILE), tiles.dtype)] * (ncols - 1),
        in_specs=[SMEM, VMEM],
        out_specs=[VMEM] * (1 + ncols),
        scratch_shapes=[pltpu.SMEM((nslots,), jnp.int32)],
        compiler_params=params(),
    )(send_slot, tiles)
    return res[0], res[1], res[2:]


def rest_kernel(ncols, per, send_ref, tiles_ref, after_ref, *refs):
    outs, inverse = refs[:-1], refs[-1]
    me = lax.axis_index("cols")
    find_inverse(send_ref, inverse)
    half = per * LEAD // 8
    for d in range(1, ncols):
        dest = lax.rem(me + d, ncols)
        for p in range(half, per):
            outs[d - 1][p - half] = tiles_ref[inverse[dest * per + p]]


def rest(tiles, send_slot, ncols, after):
    nslots = tiles.shape[0]
    per = nslots // ncols
    return pl.pallas_call(
        functools.partial(rest_kernel, ncols, per),
        out_shape=[jax.ShapeDtypeStruct((per - per * LEAD // 8, TILE, TILE), tiles.dtype)] * (ncols - 1),
        in_specs=[SMEM, VMEM, ANY],
        out_specs=[VMEM] * (ncols - 1),
        scratch_shapes=[pltpu.SMEM((nslots,), jnp.int32)],
        compiler_params=params(),
    )(send_slot, tiles, after)


def later_kernel(list_ref, after_ref, out_ref):
    for g in range(out_ref.shape[1]):
        out_ref[0, g] = list_ref[0, g]


def later(fetch_list, after):
    return pl.pallas_call(
        later_kernel,
        out_shape=jax.ShapeDtypeStruct(fetch_list.shape, fetch_list.dtype),
        in_specs=[SMEM, ANY],
        out_specs=SMEM,
        compiler_params=params(),
    )(fetch_list, after)


def send_blocks(scaled, wanted, outs):
    for d, out in enumerate(outs):
        out[...] = scaled[pl.ds(pl.multiple_of(wanted[d] * TILE, TILE), TILE), :]


def start_kernel(ncols, groups, blocks, row_ref, *refs):
    lists, refs = refs[:groups], refs[groups:]
    (sums_ref, *leads), (basis_ref, scale_ref, asked_ref, *outs, scaled) = refs[:ncols], refs[ncols:]
    me, row = lax.axis_index("cols"), lax.axis_index("rows")
    per = sums_ref.shape[0]
    sums = [sums_ref[...]]
    for ref in leads:
        tail = ref[per * LEAD // 8 * TILE :, :].astype(jnp.float32)
        sums.append(tail[:per, :] + tail[per : 2 * per, :] + tail[2 * per : 3 * per, :])
    degree = [jnp.ones((1, TILE), jnp.float32) for _ in range(blocks)]
    for d in range(ncols):
        source = lax.rem(me + ncols - d, ncols)
        for p in range(per):
            at = row_ref[0, source * per + p]
            line = sums[d][p : p + 1, :]
            for j in range(blocks):
                degree[j] = degree[j] + jnp.where(at == j, line, jnp.zeros_like(line))
    for j in range(blocks):
        here = slice(j * TILE, (j + 1) * TILE)
        scale = jnp.transpose(jnp.broadcast_to(lax.rsqrt(degree[j]), (WIDTH, TILE)))
        scale_ref[here, :] = scale
        scaled[here, :] = (scale * basis_ref[here, :].astype(jnp.float32)).astype(jnp.bfloat16)
    wanted = [lists[d][0, row] for d in range(groups)]
    for d in range(groups):
        asked_ref[0, d] = wanted[d]
    send_blocks(scaled, wanted, outs)


def start(slot_row, lists, sums, basis):
    ncols, groups, rows = len(sums), len(lists), basis.shape[0]
    res = pl.pallas_call(
        functools.partial(start_kernel, ncols, groups, rows // TILE),
        out_shape=[
            jax.ShapeDtypeStruct((rows, WIDTH), jnp.float32),
            jax.ShapeDtypeStruct((1, groups), jnp.int32),
        ]
        + [jax.ShapeDtypeStruct((TILE, WIDTH), jnp.bfloat16)] * groups,
        in_specs=[SMEM] * (1 + groups) + [VMEM] * (ncols + 1),
        out_specs=[VMEM, SMEM] + [VMEM] * groups,
        scratch_shapes=[pltpu.VMEM((rows, WIDTH), jnp.bfloat16)],
        compiler_params=params(),
    )(slot_row, *lists, *sums, basis)
    return res[0], res[1], res[2:]


def gram_of(y):
    return lax.dot_general(
        y, y, (((0,), (0,)), ((), ())), precision=HIGHEST, preferred_element_type=jnp.float32
    )


def times(a, b, transposed=False):
    return lax.dot_general(
        a, b, (((1,), (1 if transposed else 0,)), ((), ())), precision=HIGHEST, preferred_element_type=jnp.float32
    )


def step_kernel(ncols, groups, first, last, row_ref, fetch_ref, asked_ref, scale_ref, *refs):
    stay, leads, rests, refs = refs[0], refs[1:ncols], refs[ncols : 2 * ncols - 1], refs[2 * ncols - 1 :]
    got, refs = refs[:groups], refs[groups:]
    outs, (held, acc, scaled) = refs[:-3], refs[-3:]
    me, row = lax.axis_index("cols"), lax.axis_index("rows")
    per, rows = stay.shape[0], scale_ref.shape[0]
    half = per * LEAD // 8
    for d in range(groups):
        held[d] = got[d][...]
    acc[...] = jnp.zeros_like(acc)
    for d in range(ncols):
        source = lax.rem(me + ncols - d, ncols)
        for p in range(per):
            slot = source * per + p
            which = jnp.bitwise_xor(fetch_ref[0, slot], row)
            place = pl.ds(pl.multiple_of(row_ref[0, slot] * TILE, TILE), TILE)
            if d == 0:
                tile = stay[p]
            elif p < half:
                tile = leads[d - 1][p * TILE : (p + 1) * TILE, :]
            else:
                tile = rests[d - 1][p - half]
            acc[place, :] += jnp.dot(tile, held[which], preferred_element_type=jnp.float32)
    scale = scale_ref[...]
    y = acc[:rows, :] * scale
    if last:
        outs[0][...] = y
        return
    gram_ref, outs = outs[0], outs[1:]
    gram_ref[:HALF, :], gram_ref[HALF:, :] = fold(gram_of(y))
    if first:
        scaled[...] = (y * scale).astype(jnp.bfloat16)
        send_blocks(scaled, [asked_ref[0, d] for d in range(groups)], outs)
    else:
        outs[0][...] = y


def step(slot_row, slot_fetch, asked, scale, chunks, got, first, last):
    ncols, groups, rows = (len(chunks) + 1) // 2, len(got), scale.shape[0]
    shapes = [] if last else [jax.ShapeDtypeStruct((HALF + 8, WIDTH), jnp.float32)]
    if first:
        shapes += [jax.ShapeDtypeStruct((TILE, WIDTH), jnp.bfloat16)] * groups
    else:
        shapes += [jax.ShapeDtypeStruct((rows, WIDTH), jnp.float32)]
    res = pl.pallas_call(
        functools.partial(step_kernel, ncols, groups, first, last),
        out_shape=shapes,
        in_specs=[SMEM] * 3 + [VMEM] * (1 + len(chunks) + groups),
        out_specs=[VMEM] * len(shapes),
        scratch_shapes=[
            pltpu.VMEM((groups, TILE, WIDTH), jnp.bfloat16),
            pltpu.VMEM((rows + TILE, WIDTH), jnp.float32),
            pltpu.VMEM((rows, WIDTH), jnp.bfloat16),
        ],
        compiler_params=params(),
    )(slot_row, slot_fetch, asked, scale, *chunks, *got)
    if last:
        return None, res[0]
    return res[0], (res[1:] if first else res[1])


def added(parts):
    while len(parts) > 1:
        parts = [parts[i] + parts[i + 1] for i in range(0, len(parts), 2)]
    return parts[0]


def summed(refs):
    return added([ref[...] for ref in refs])


def turn_kernel(npts, groups, nparts, first, last, gauge, asked_ref, scale_ref, p_ref, *refs):
    parts, refs = refs[:nparts], refs[nparts:]
    if not first:
        before_ref, before_inv_ref, refs = refs[0], refs[1], refs[2:]
    outs, (inv, scaled) = refs[:-2], refs[-2:]
    gram = unfold(summed(parts)) * (1.0 / npts)
    factor_rows(gram, inv)
    both = inv[...]
    mine = both if first else times(both, before_ref[...])
    y = times(p_ref[...], mine, True)
    if last:
        gram_ref, y_ref = outs
        y_ref[...] = y
        gram_ref[:HALF, :], gram_ref[HALF:, :] = fold(gram_of(y))
        return
    low_ref, inv_ref, growth_ref, outs = outs[0], outs[1], outs[2], outs[3:]
    scaled[...] = (y * scale_ref[...]).astype(jnp.bfloat16)
    send_blocks(scaled, [asked_ref[0, d] for d in range(groups)], outs)
    low = times(gram, both, True)
    low = low if first else times(before_inv_ref[...], low)
    low_ref[...] = low
    inv_ref[...] = mine
    if not gauge:
        return
    weights = lax.dot_general(
        jnp.ones((8, WIDTH), jnp.float32), low * low, (((1,), (1,)), ((), ())), preferred_element_type=jnp.float32
    )
    growth = jnp.sum(mine * mine * weights[0:1, :]) * (1.0 / WIDTH)
    growth_ref[...] = jnp.full((8, WIDTH), growth)


def turn(asked, parts, scale, p, before, npts, last, gauge):
    rows, groups = p.shape[0], asked.shape[1]
    first = before is None
    square = jax.ShapeDtypeStruct((WIDTH, WIDTH), jnp.float32)
    growth = jax.ShapeDtypeStruct((8, WIDTH), jnp.float32)
    if last:
        shapes = [jax.ShapeDtypeStruct((HALF + 8, WIDTH), jnp.float32), jax.ShapeDtypeStruct(p.shape, p.dtype)]
    else:
        shapes = [square, square, growth] + [jax.ShapeDtypeStruct((TILE, WIDTH), jnp.bfloat16)] * groups
    return pl.pallas_call(
        functools.partial(turn_kernel, npts, groups, len(parts), first, last, gauge),
        out_shape=shapes,
        in_specs=[SMEM] + [VMEM] * (2 + len(parts) + (0 if first else 2)),
        out_specs=[VMEM] * len(shapes),
        scratch_shapes=[pltpu.VMEM((WIDTH, WIDTH), jnp.float32), pltpu.VMEM((rows, WIDTH), jnp.bfloat16)],
        compiler_params=params(),
    )(asked, scale, p, *parts, *([] if first else before))


def careful_kernel(npts, groups, nparts, asked_ref, scale_ref, y_ref, *refs):
    parts, (v_ref, *outs), (inv, scaled) = refs[:nparts], refs[nparts:-2], refs[-2:]
    factor_rows(unfold(summed(parts)) * (1.0 / npts), inv)
    v = times(y_ref[...], inv[...], True).astype(jnp.bfloat16)
    v_ref[...] = v
    scaled[...] = (v.astype(jnp.float32) * scale_ref[...]).astype(jnp.bfloat16)
    send_blocks(scaled, [asked_ref[0, d] for d in range(groups)], outs)


def careful(asked, parts, scale, y, npts):
    rows, groups = y.shape[0], asked.shape[1]
    res = pl.pallas_call(
        functools.partial(careful_kernel, npts, groups, len(parts)),
        out_shape=[jax.ShapeDtypeStruct(y.shape, jnp.bfloat16)]
        + [jax.ShapeDtypeStruct((TILE, WIDTH), jnp.bfloat16)] * groups,
        in_specs=[SMEM] + [VMEM] * (2 + len(parts)),
        out_specs=[VMEM] * (1 + groups),
        scratch_shapes=[pltpu.VMEM((WIDTH, WIDTH), jnp.float32), pltpu.VMEM((rows, WIDTH), jnp.bfloat16)],
        compiler_params=params(),
    )(asked, scale, y, *parts)
    return res[0], res[1:]


def fold(square):
    row = lax.broadcasted_iota(jnp.int32, (HALF, WIDTH), 0)
    lane = lax.broadcasted_iota(jnp.int32, (HALF, WIDTH), 1)
    low = square[HALF:, :]
    moved = pltpu.roll(low, HALF, 1)
    main = jnp.where((lane < HALF) & (lane > row), moved, square[:HALF, :])
    diagonal = jnp.sum(jnp.where(lane == row + HALF, low, 0.0), axis=0, keepdims=True)
    return main, jnp.broadcast_to(diagonal, (8, WIDTH))


def unfold(folded):
    row = lax.broadcasted_iota(jnp.int32, (HALF, WIDTH), 0)
    lane = lax.broadcasted_iota(jnp.int32, (HALF, WIDTH), 1)
    main = folded[:HALF, :]
    diagonal = jnp.broadcast_to(folded[HALF : HALF + 1, :], (HALF, WIDTH))
    upper = jnp.where((lane >= HALF) | (lane <= row), main, 0.0)
    moved = pltpu.roll(main, HALF, 1)
    lower = jnp.where(lane > row + HALF, moved, jnp.where(lane == row + HALF, diagonal, 0.0))
    whole = jnp.concatenate([upper, lower], axis=0)
    row = lax.broadcasted_iota(jnp.int32, (WIDTH, WIDTH), 0)
    lane = lax.broadcasted_iota(jnp.int32, (WIDTH, WIDTH), 1)
    return jnp.where(row == lane, whole, whole + jnp.transpose(whole))


def factor_rows(matrix, out_ref):
    n = WIDTH
    lane = lax.broadcasted_iota(jnp.int32, (8, n), 1)
    parts = [matrix[8 * i : 8 * i + 8, :] for i in range(n // 8)]
    for j in range(0, n, GROUP):
        here = j // 8
        off = j % 8
        wide = lambda v: jnp.broadcast_to(v, (8, n))
        rows = [wide(parts[here][off + a : off + a + 1, :]) for a in range(GROUP)]
        piv = [[wide(rows[a][:, j + c : j + c + 1]) for c in range(a + 1)] for a in range(GROUP)]
        in_group = (lane >= j) & (lane < j + GROUP)
        rows = [jnp.where(in_group, jnp.where(lane == j + a, 1.0, 0.0), rows[a]) for a in range(GROUP)]
        low = [[None] * GROUP for _ in range(GROUP)]
        inv = []
        for c in range(GROUP):
            inv.append(1.0 / piv[c][c])
            for a in range(c + 1, GROUP):
                low[a][c] = piv[a][c] * inv[c]
            for a in range(c + 1, GROUP):
                for b in range(c + 1, a + 1):
                    piv[a][b] = piv[a][b] - low[a][c] * piv[b][c]
        for a in range(GROUP):
            for c in range(a):
                rows[a] = rows[a] - low[a][c] * rows[c]
        for a in range(GROUP):
            keep = jnp.where(lane <= j + a, rows[a], 0.0) * lax.rsqrt(piv[a][a])
            out_ref[j + a : j + a + 1, :] = keep[0:1, :]
        scaled = [rows[a] * inv[a] for a in range(GROUP)]
        for i in range(here + 1, n // 8):
            cols = [wide(parts[i][:, j + c : j + c + 1]) for c in range(GROUP)]
            new = jnp.where(in_group, 0.0, parts[i])
            for c in range(GROUP):
                for b in range(c):
                    cols[c] = cols[c] - low[c][b] * cols[b]
                new = new - cols[c] * scaled[c]
            parts[i] = new


def finish_kernel(npts, nparts, y_ref, *refs):
    v_ref, inv = refs[nparts:]
    factor_rows(unfold(summed(refs[:nparts])) * (1.0 / npts), inv)
    v_ref[...] = times(y_ref[...], inv[...], True).astype(v_ref.dtype)


def finish(parts, y, npts):
    return pl.pallas_call(
        functools.partial(finish_kernel, npts, len(parts)),
        out_shape=jax.ShapeDtypeStruct(y.shape, jnp.bfloat16),
        in_specs=[VMEM] * (1 + len(parts)),
        out_specs=VMEM,
        scratch_shapes=[pltpu.VMEM((WIDTH, WIDTH), jnp.float32)],
        compiler_params=params(),
    )(y, *parts)


def swap(x, axis, n, d):
    return lax.ppermute(x, axis, [(i, i ^ d) for i in range(n)])


def shift(x, axis, n, d):
    return lax.ppermute(x, axis, [(i, (i + d) % n) for i in range(n)])


def on_device(tiles, send_slot, slot_row, slot_fetch, fetch_list, basis):
    groups = lax.axis_size("rows")
    ncols = lax.axis_size("cols")
    npts = basis.shape[0] * groups * ncols
    sums, stay, leads = lead(tiles, send_slot, ncols)
    rests = rest(tiles, send_slot, ncols, leads[0])
    wish = later(fetch_list, rests[0])
    leads = [shift(leads[d - 1], "cols", ncols, d) for d in range(1, ncols)]
    rests = [shift(rests[d - 1], "cols", ncols, d) for d in range(1, ncols)]
    chunks = [stay, *leads, *rests]
    lists = [wish] + [swap(wish, "rows", groups, d) for d in range(1, groups)]
    scale, asked, out = start(slot_row, lists, [sums, *leads], basis)
    stages = [("rows", groups, [1])]
    bit = 2
    while bit < groups:
        wide = bit * 2 < groups
        stages.append(("rows", groups, [bit, 2 * bit, 3 * bit] if wide else [bit]))
        bit *= 4 if wide else 2
    apart = [("cols", ncols, [1 << i]) for i in range(ncols.bit_length() - 1)]
    at_once = [("cols", ncols, list(range(1, ncols)))]

    def total(gram, more):
        for axis, size, partners in stages + more:
            parts = [gram] + [swap(gram, axis, size, d) for d in partners]
            gram = added(parts)
        return parts

    def fetched(out):
        return [out[0]] + [swap(out[d], "rows", groups, d) for d in range(1, groups)]

    first_out, growth = out, []
    parts = before = None
    for k in range(ITERS):
        last = k == ITERS - 1
        gram, out = step(slot_row, slot_fetch, asked, scale, chunks, fetched(out), k == 0, last)
        if k:
            gauge = k in (2, ITERS - 2)
            res = turn(asked, parts, scale, out, before, npts, last, gauge)
            before, out = res[:2], res[3:]
            if gauge:
                growth.append(res[2][0, 0])
        if not last:
            parts = total(gram, apart)
    gram, y = res
    fast = finish(total(gram, at_once), y, npts)

    def repeat(k, state):
        gram, y = step(slot_row, slot_fetch, asked, scale, chunks, fetched(state[1]), False, False)
        v, out = careful(asked, total(gram, apart), scale, y, npts)
        return v, tuple(out)

    return lax.cond(
        sum(growth) < GROWTH,
        lambda: fast,
        lambda: lax.fori_loop(0, ITERS, repeat, (fast, tuple(first_out)))[0],
    )


def solution(mesh):
    in_specs = (
        P(("rows", "cols"), None, None),
        P(("rows", "cols"), None),
        P(("rows", "cols"), None),
        P(("rows", "cols"), None),
        P(("rows", "cols"), None),
        P(("rows", "cols"), None),
    )
    out_specs = P(("rows", "cols"), None)
    return jax.shard_map(
        on_device, mesh=mesh, in_specs=in_specs, out_specs=out_specs, check_vma=False
    )
```

```python
import functools

import jax
import jax.numpy as jnp
from jax import lax
from jax.experimental import pallas as pl
from jax.experimental.pallas import tpu as pltpu
from jax.sharding import PartitionSpec as P

TILE = 256
WIDTH = 128
ITERS = 6
GROUP = 8
HALF = WIDTH // 2
GROWTH = 35.0
LEAD = 3
HIGHEST = lax.Precision.HIGHEST
VMEM = pl.BlockSpec(memory_space=pltpu.VMEM)
SMEM = pl.BlockSpec(memory_space=pltpu.SMEM)
ANY = pl.BlockSpec(memory_space=pl.ANY)


def params():
    return pltpu.CompilerParams(vmem_limit_bytes=16 * 1024 * 1024)


def find_inverse(send_ref, inverse):
    def note(i, carry):
        inverse[send_ref[0, i]] = i
        return carry

    lax.fori_loop(0, inverse.shape[0], note, 0)


def lead_kernel(ncols, per, send_ref, tiles_ref, sums_ref, *refs):
    stay, leads, inverse = refs[0], refs[1:-1], refs[-1]
    me = lax.axis_index("cols")
    find_inverse(send_ref, inverse)
    lane = lax.broadcasted_iota(jnp.int32, (TILE, WIDTH), 1)
    total = jnp.zeros((TILE, WIDTH), jnp.float32)
    half = per * LEAD // 8
    for d in range(ncols):
        dest = lax.rem(me + d, ncols)
        for p in range(per):
            tile = tiles_ref[inverse[dest * per + p]]
            if d == 0:
                stay[p] = tile
            elif p < half:
                leads[d - 1][p * TILE : (p + 1) * TILE, :] = tile
            pick = jnp.where(lane == d * per + p, 1.0, 0.0).astype(jnp.bfloat16)
            total = total + jnp.dot(jnp.abs(tile), pick, preferred_element_type=jnp.float32)
    flat = jnp.transpose(total)
    sums_ref[...] = flat[:per, :]
    for d in range(1, ncols):
        rest = flat[d * per : (d + 1) * per, :]
        pieces = []
        for _ in range(3):
            pieces.append(rest.astype(jnp.bfloat16).astype(jnp.float32))
            rest = rest - pieces[-1]
        pieces.append(jnp.zeros_like(rest))
        leads[d - 1][half * TILE :, :] = jnp.concatenate(pieces, axis=0).astype(jnp.bfloat16)


def lead(tiles, send_slot, ncols):
    nslots = tiles.shape[0]
    per = nslots // ncols
    res = pl.pallas_call(
        functools.partial(lead_kernel, ncols, per),
        out_shape=[
            jax.ShapeDtypeStruct((per, TILE), jnp.float32),
            jax.ShapeDtypeStruct((per, TILE, TILE), tiles.dtype),
        ]
        + [jax.ShapeDtypeStruct((per * LEAD // 8 * TILE + 4 * per, TILE), tiles.dtype)] * (ncols - 1),
        in_specs=[SMEM, VMEM],
        out_specs=[VMEM] * (1 + ncols),
        scratch_shapes=[pltpu.SMEM((nslots,), jnp.int32)],
        compiler_params=params(),
    )(send_slot, tiles)
    return res[0], res[1], res[2:]


def rest_kernel(ncols, per, send_ref, tiles_ref, after_ref, *refs):
    outs, inverse = refs[:-1], refs[-1]
    me = lax.axis_index("cols")
    find_inverse(send_ref, inverse)
    half = per * LEAD // 8
    for d in range(1, ncols):
        dest = lax.rem(me + d, ncols)
        for p in range(half, per):
            outs[d - 1][p - half] = tiles_ref[inverse[dest * per + p]]


def rest(tiles, send_slot, ncols, after):
    nslots = tiles.shape[0]
    per = nslots // ncols
    return pl.pallas_call(
        functools.partial(rest_kernel, ncols, per),
        out_shape=[jax.ShapeDtypeStruct((per - per * LEAD // 8, TILE, TILE), tiles.dtype)] * (ncols - 1),
        in_specs=[SMEM, VMEM, ANY],
        out_specs=[VMEM] * (ncols - 1),
        scratch_shapes=[pltpu.SMEM((nslots,), jnp.int32)],
        compiler_params=params(),
    )(send_slot, tiles, after)


def later_kernel(list_ref, after_ref, out_ref):
    for g in range(out_ref.shape[1]):
        out_ref[0, g] = list_ref[0, g]


def later(fetch_list, after):
    return pl.pallas_call(
        later_kernel,
        out_shape=jax.ShapeDtypeStruct(fetch_list.shape, fetch_list.dtype),
        in_specs=[SMEM, ANY],
        out_specs=SMEM,
        compiler_params=params(),
    )(fetch_list, after)


def send_blocks(scaled, wanted, outs):
    for d, out in enumerate(outs):
        out[...] = scaled[pl.ds(pl.multiple_of(wanted[d] * TILE, TILE), TILE), :]


def start_kernel(ncols, groups, blocks, row_ref, *refs):
    lists, refs = refs[:groups], refs[groups:]
    (sums_ref, *leads), (basis_ref, scale_ref, asked_ref, *outs, scaled) = refs[:ncols], refs[ncols:]
    me, row = lax.axis_index("cols"), lax.axis_index("rows")
    per = sums_ref.shape[0]
    sums = [sums_ref[...]]
    for ref in leads:
        tail = ref[per * LEAD // 8 * TILE :, :].astype(jnp.float32)
        sums.append(tail[:per, :] + tail[per : 2 * per, :] + tail[2 * per : 3 * per, :])
    degree = [jnp.ones((1, TILE), jnp.float32) for _ in range(blocks)]
    for d in range(ncols):
        source = lax.rem(me + ncols - d, ncols)
        for p in range(per):
            at = row_ref[0, source * per + p]
            line = sums[d][p : p + 1, :]
            for j in range(blocks):
                degree[j] = degree[j] + jnp.where(at == j, line, jnp.zeros_like(line))
    for j in range(blocks):
        here = slice(j * TILE, (j + 1) * TILE)
        scale = jnp.transpose(jnp.broadcast_to(lax.rsqrt(degree[j]), (WIDTH, TILE)))
        scale_ref[here, :] = scale
        scaled[here, :] = (scale * basis_ref[here, :].astype(jnp.float32)).astype(jnp.bfloat16)
    wanted = [lists[d][0, row] for d in range(groups)]
    for d in range(groups):
        asked_ref[0, d] = wanted[d]
    send_blocks(scaled, wanted, outs)


def start(slot_row, lists, sums, basis):
    ncols, groups, rows = len(sums), len(lists), basis.shape[0]
    res = pl.pallas_call(
        functools.partial(start_kernel, ncols, groups, rows // TILE),
        out_shape=[
            jax.ShapeDtypeStruct((rows, WIDTH), jnp.float32),
            jax.ShapeDtypeStruct((1, groups), jnp.int32),
        ]
        + [jax.ShapeDtypeStruct((TILE, WIDTH), jnp.bfloat16)] * groups,
        in_specs=[SMEM] * (1 + groups) + [VMEM] * (ncols + 1),
        out_specs=[VMEM, SMEM] + [VMEM] * groups,
        scratch_shapes=[pltpu.VMEM((rows, WIDTH), jnp.bfloat16)],
        compiler_params=params(),
    )(slot_row, *lists, *sums, basis)
    return res[0], res[1], res[2:]


def gram_of(y):
    return lax.dot_general(
        y, y, (((0,), (0,)), ((), ())), precision=HIGHEST, preferred_element_type=jnp.float32
    )


def times(a, b, transposed=False):
    return lax.dot_general(
        a, b, (((1,), (1 if transposed else 0,)), ((), ())), precision=HIGHEST, preferred_element_type=jnp.float32
    )


def step_kernel(ncols, groups, first, last, row_ref, fetch_ref, asked_ref, scale_ref, *refs):
    stay, leads, rests, refs = refs[0], refs[1:ncols], refs[ncols : 2 * ncols - 1], refs[2 * ncols - 1 :]
    got, refs = refs[:groups], refs[groups:]
    outs, (held, acc, scaled) = refs[:-3], refs[-3:]
    me, row = lax.axis_index("cols"), lax.axis_index("rows")
    per, rows = stay.shape[0], scale_ref.shape[0]
    half = per * LEAD // 8
    for d in range(groups):
        held[d] = got[d][...]
    acc[...] = jnp.zeros_like(acc)
    for d in range(ncols):
        source = lax.rem(me + ncols - d, ncols)
        for p in range(per):
            slot = source * per + p
            which = jnp.bitwise_xor(fetch_ref[0, slot], row)
            place = pl.ds(pl.multiple_of(row_ref[0, slot] * TILE, TILE), TILE)
            if d == 0:
                tile = stay[p]
            elif p < half:
                tile = leads[d - 1][p * TILE : (p + 1) * TILE, :]
            else:
                tile = rests[d - 1][p - half]
            acc[place, :] += jnp.dot(tile, held[which], preferred_element_type=jnp.float32)
    scale = scale_ref[...]
    y = acc[:rows, :] * scale
    if last:
        outs[0][...] = y
        return
    gram_ref, outs = outs[0], outs[1:]
    gram_ref[:HALF, :], gram_ref[HALF:, :] = fold(gram_of(y))
    if first:
        scaled[...] = (y * scale).astype(jnp.bfloat16)
        send_blocks(scaled, [asked_ref[0, d] for d in range(groups)], outs)
    else:
        outs[0][...] = y


def step(slot_row, slot_fetch, asked, scale, chunks, got, first, last):
    ncols, groups, rows = (len(chunks) + 1) // 2, len(got), scale.shape[0]
    shapes = [] if last else [jax.ShapeDtypeStruct((HALF + 8, WIDTH), jnp.float32)]
    if first:
        shapes += [jax.ShapeDtypeStruct((TILE, WIDTH), jnp.bfloat16)] * groups
    else:
        shapes += [jax.ShapeDtypeStruct((rows, WIDTH), jnp.float32)]
    res = pl.pallas_call(
        functools.partial(step_kernel, ncols, groups, first, last),
        out_shape=shapes,
        in_specs=[SMEM] * 3 + [VMEM] * (1 + len(chunks) + groups),
        out_specs=[VMEM] * len(shapes),
        scratch_shapes=[
            pltpu.VMEM((groups, TILE, WIDTH), jnp.bfloat16),
            pltpu.VMEM((rows + TILE, WIDTH), jnp.float32),
            pltpu.VMEM((rows, WIDTH), jnp.bfloat16),
        ],
        compiler_params=params(),
    )(slot_row, slot_fetch, asked, scale, *chunks, *got)
    if last:
        return None, res[0]
    return res[0], (res[1:] if first else res[1])


def added(parts):
    while len(parts) > 1:
        parts = [parts[i] + parts[i + 1] for i in range(0, len(parts), 2)]
    return parts[0]


def summed(refs):
    return added([ref[...] for ref in refs])


def turn_kernel(npts, groups, nparts, first, last, gauge, asked_ref, scale_ref, p_ref, *refs):
    parts, refs = refs[:nparts], refs[nparts:]
    if not first:
        before_ref, before_inv_ref, refs = refs[0], refs[1], refs[2:]
    outs, (inv, scaled) = refs[:-2], refs[-2:]
    gram = unfold(summed(parts)) * (1.0 / npts)
    factor_rows(gram, inv)
    both = inv[...]
    mine = both if first else times(both, before_ref[...])
    y = times(p_ref[...], mine, True)
    if last:
        gram_ref, y_ref = outs
        y_ref[...] = y
        gram_ref[:HALF, :], gram_ref[HALF:, :] = fold(gram_of(y))
        return
    low_ref, inv_ref, growth_ref, outs = outs[0], outs[1], outs[2], outs[3:]
    scaled[...] = (y * scale_ref[...]).astype(jnp.bfloat16)
    send_blocks(scaled, [asked_ref[0, d] for d in range(groups)], outs)
    low = times(gram, both, True)
    low = low if first else times(before_inv_ref[...], low)
    low_ref[...] = low
    inv_ref[...] = mine
    if not gauge:
        return
    weights = lax.dot_general(
        jnp.ones((8, WIDTH), jnp.float32), low * low, (((1,), (1,)), ((), ())), preferred_element_type=jnp.float32
    )
    growth = jnp.sum(mine * mine * weights[0:1, :]) * (1.0 / WIDTH)
    growth_ref[...] = jnp.full((8, WIDTH), growth)


def turn(asked, parts, scale, p, before, npts, last, gauge):
    rows, groups = p.shape[0], asked.shape[1]
    first = before is None
    square = jax.ShapeDtypeStruct((WIDTH, WIDTH), jnp.float32)
    growth = jax.ShapeDtypeStruct((8, WIDTH), jnp.float32)
    if last:
        shapes = [jax.ShapeDtypeStruct((HALF + 8, WIDTH), jnp.float32), jax.ShapeDtypeStruct(p.shape, p.dtype)]
    else:
        shapes = [square, square, growth] + [jax.ShapeDtypeStruct((TILE, WIDTH), jnp.bfloat16)] * groups
    return pl.pallas_call(
        functools.partial(turn_kernel, npts, groups, len(parts), first, last, gauge),
        out_shape=shapes,
        in_specs=[SMEM] + [VMEM] * (2 + len(parts) + (0 if first else 2)),
        out_specs=[VMEM] * len(shapes),
        scratch_shapes=[pltpu.VMEM((WIDTH, WIDTH), jnp.float32), pltpu.VMEM((rows, WIDTH), jnp.bfloat16)],
        compiler_params=params(),
    )(asked, scale, p, *parts, *([] if first else before))


def careful_kernel(npts, groups, nparts, asked_ref, scale_ref, y_ref, *refs):
    parts, (v_ref, *outs), (inv, scaled) = refs[:nparts], refs[nparts:-2], refs[-2:]
    factor_rows(unfold(summed(parts)) * (1.0 / npts), inv)
    v = times(y_ref[...], inv[...], True).astype(jnp.bfloat16)
    v_ref[...] = v
    scaled[...] = (v.astype(jnp.float32) * scale_ref[...]).astype(jnp.bfloat16)
    send_blocks(scaled, [asked_ref[0, d] for d in range(groups)], outs)


def careful(asked, parts, scale, y, npts):
    rows, groups = y.shape[0], asked.shape[1]
    res = pl.pallas_call(
        functools.partial(careful_kernel, npts, groups, len(parts)),
        out_shape=[jax.ShapeDtypeStruct(y.shape, jnp.bfloat16)]
        + [jax.ShapeDtypeStruct((TILE, WIDTH), jnp.bfloat16)] * groups,
        in_specs=[SMEM] + [VMEM] * (2 + len(parts)),
        out_specs=[VMEM] * (1 + groups),
        scratch_shapes=[pltpu.VMEM((WIDTH, WIDTH), jnp.float32), pltpu.VMEM((rows, WIDTH), jnp.bfloat16)],
        compiler_params=params(),
    )(asked, scale, y, *parts)
    return res[0], res[1:]


def fold(square):
    row = lax.broadcasted_iota(jnp.int32, (HALF, WIDTH), 0)
    lane = lax.broadcasted_iota(jnp.int32, (HALF, WIDTH), 1)
    low = square[HALF:, :]
    moved = pltpu.roll(low, HALF, 1)
    main = jnp.where((lane < HALF) & (lane > row), moved, square[:HALF, :])
    diagonal = jnp.sum(jnp.where(lane == row + HALF, low, 0.0), axis=0, keepdims=True)
    return main, jnp.broadcast_to(diagonal, (8, WIDTH))


def unfold(folded):
    row = lax.broadcasted_iota(jnp.int32, (HALF, WIDTH), 0)
    lane = lax.broadcasted_iota(jnp.int32, (HALF, WIDTH), 1)
    main = folded[:HALF, :]
    diagonal = jnp.broadcast_to(folded[HALF : HALF + 1, :], (HALF, WIDTH))
    upper = jnp.where((lane >= HALF) | (lane <= row), main, 0.0)
    moved = pltpu.roll(main, HALF, 1)
    lower = jnp.where(lane > row + HALF, moved, jnp.where(lane == row + HALF, diagonal, 0.0))
    whole = jnp.concatenate([upper, lower], axis=0)
    row = lax.broadcasted_iota(jnp.int32, (WIDTH, WIDTH), 0)
    lane = lax.broadcasted_iota(jnp.int32, (WIDTH, WIDTH), 1)
    return jnp.where(row == lane, whole, whole + jnp.transpose(whole))


def factor_rows(matrix, out_ref):
    n = WIDTH
    lane = lax.broadcasted_iota(jnp.int32, (8, n), 1)
    parts = [matrix[8 * i : 8 * i + 8, :] for i in range(n // 8)]
    for j in range(0, n, GROUP):
        here = j // 8
        off = j % 8
        wide = lambda v: jnp.broadcast_to(v, (8, n))
        rows = [wide(parts[here][off + a : off + a + 1, :]) for a in range(GROUP)]
        piv = [[wide(rows[a][:, j + c : j + c + 1]) for c in range(a + 1)] for a in range(GROUP)]
        in_group = (lane >= j) & (lane < j + GROUP)
        rows = [jnp.where(in_group, jnp.where(lane == j + a, 1.0, 0.0), rows[a]) for a in range(GROUP)]
        low = [[None] * GROUP for _ in range(GROUP)]
        inv = []
        for c in range(GROUP):
            inv.append(1.0 / piv[c][c])
            for a in range(c + 1, GROUP):
                low[a][c] = piv[a][c] * inv[c]
            for a in range(c + 1, GROUP):
                for b in range(c + 1, a + 1):
                    piv[a][b] = piv[a][b] - low[a][c] * piv[b][c]
        for a in range(GROUP):
            for c in range(a):
                rows[a] = rows[a] - low[a][c] * rows[c]
        for a in range(GROUP):
            keep = jnp.where(lane <= j + a, rows[a], 0.0) * lax.rsqrt(piv[a][a])
            out_ref[j + a : j + a + 1, :] = keep[0:1, :]
        scaled = [rows[a] * inv[a] for a in range(GROUP)]
        for i in range(here + 1, n // 8):
            cols = [wide(parts[i][:, j + c : j + c + 1]) for c in range(GROUP)]
            new = jnp.where(in_group, 0.0, parts[i])
            for c in range(GROUP):
                for b in range(c):
                    cols[c] = cols[c] - low[c][b] * cols[b]
                new = new - cols[c] * scaled[c]
            parts[i] = new


def finish_kernel(npts, nparts, y_ref, *refs):
    v_ref, inv = refs[nparts:]
    factor_rows(unfold(summed(refs[:nparts])) * (1.0 / npts), inv)
    v_ref[...] = times(y_ref[...], inv[...], True).astype(v_ref.dtype)


def finish(parts, y, npts):
    return pl.pallas_call(
        functools.partial(finish_kernel, npts, len(parts)),
        out_shape=jax.ShapeDtypeStruct(y.shape, jnp.bfloat16),
        in_specs=[VMEM] * (1 + len(parts)),
        out_specs=VMEM,
        scratch_shapes=[pltpu.VMEM((WIDTH, WIDTH), jnp.float32)],
        compiler_params=params(),
    )(y, *parts)


def swap(x, axis, n, d):
    return lax.ppermute(x, axis, [(i, i ^ d) for i in range(n)])


def shift(x, axis, n, d):
    return lax.ppermute(x, axis, [(i, (i + d) % n) for i in range(n)])


def on_device(tiles, send_slot, slot_row, slot_fetch, fetch_list, basis):
    groups = lax.axis_size("rows")
    ncols = lax.axis_size("cols")
    npts = basis.shape[0] * groups * ncols
    sums, stay, leads = lead(tiles, send_slot, ncols)
    rests = rest(tiles, send_slot, ncols, leads[0])
    wish = later(fetch_list, rests[0])
    leads = [shift(leads[d - 1], "cols", ncols, d) for d in range(1, ncols)]
    rests = [shift(rests[d - 1], "cols", ncols, d) for d in range(1, ncols)]
    chunks = [stay, *leads, *rests]
    lists = [wish] + [swap(wish, "rows", groups, d) for d in range(1, groups)]
    scale, asked, out = start(slot_row, lists, [sums, *leads], basis)
    stages = [("rows", groups, [1])]
    bit = 2
    while bit < groups:
        wide = bit * 2 < groups
        stages.append(("rows", groups, [bit, 2 * bit, 3 * bit] if wide else [bit]))
        bit *= 4 if wide else 2
    apart = [("cols", ncols, [1 << i]) for i in range(ncols.bit_length() - 1)]
    at_once = [("cols", ncols, list(range(1, ncols)))]

    def total(gram, more):
        for axis, size, partners in stages + more:
            parts = [gram] + [swap(gram, axis, size, d) for d in partners]
            gram = added(parts)
        return parts

    def fetched(out):
        return [out[0]] + [swap(out[d], "rows", groups, d) for d in range(1, groups)]

    first_out, growth = out, []
    parts = before = None
    for k in range(ITERS):
        last = k == ITERS - 1
        gram, out = step(slot_row, slot_fetch, asked, scale, chunks, fetched(out), k == 0, last)
        if k:
            gauge = k in (2, ITERS - 2)
            res = turn(asked, parts, scale, out, before, npts, last, gauge)
            before, out = res[:2], res[3:]
            if gauge:
                growth.append(res[2][0, 0])
        if not last:
            parts = total(gram, apart)
    gram, y = res
    fast = finish(total(gram, at_once), y, npts)

    def repeat(k, state):
        gram, y = step(slot_row, slot_fetch, asked, scale, chunks, fetched(state[1]), False, False)
        v, out = careful(asked, total(gram, apart), scale, y, npts)
        return v, tuple(out)

    return lax.cond(
        sum(growth) < GROWTH,
        lambda: fast,
        lambda: lax.fori_loop(0, ITERS, repeat, (fast, tuple(first_out)))[0],
    )


def solution(mesh):
    in_specs = (
        P(("rows", "cols"), None, None),
        P(("rows", "cols"), None),
        P(("rows", "cols"), None),
        P(("rows", "cols"), None),
        P(("rows", "cols"), None),
        P(("rows", "cols"), None),
    )
    out_specs = P(("rows", "cols"), None)
    return jax.shard_map(
        on_device, mesh=mesh, in_specs=in_specs, out_specs=out_specs, check_vma=False
    )
```

```python
import functools

import jax
import jax.numpy as jnp
from jax import lax
from jax.experimental import pallas as pl
from jax.experimental.pallas import tpu as pltpu
from jax.sharding import PartitionSpec as P

TILE = 256
WIDTH = 128
ITERS = 6
GROUP = 8
HALF = WIDTH // 2
GROWTH = 35.0
LEAD = 3
HIGHEST = lax.Precision.HIGHEST
VMEM = pl.BlockSpec(memory_space=pltpu.VMEM)
SMEM = pl.BlockSpec(memory_space=pltpu.SMEM)
ANY = pl.BlockSpec(memory_space=pl.ANY)


def params():
    return pltpu.CompilerParams(vmem_limit_bytes=16 * 1024 * 1024)


def find_inverse(send_ref, inverse):
    def note(i, carry):
        inverse[send_ref[0, i]] = i
        return carry

    lax.fori_loop(0, inverse.shape[0], note, 0)


def lead_kernel(ncols, per, send_ref, tiles_ref, sums_ref, *refs):
    stay, leads, inverse = refs[0], refs[1:-1], refs[-1]
    me = lax.axis_index("cols")
    find_inverse(send_ref, inverse)
    lane = lax.broadcasted_iota(jnp.int32, (TILE, WIDTH), 1)
    total = jnp.zeros((TILE, WIDTH), jnp.float32)
    half = per * LEAD // 8
    for d in range(ncols):
        dest = lax.rem(me + d, ncols)
        for p in range(per):
            tile = tiles_ref[inverse[dest * per + p]]
            if d == 0:
                stay[p] = tile
            elif p < half:
                leads[d - 1][p * TILE : (p + 1) * TILE, :] = tile
            pick = jnp.where(lane == d * per + p, 1.0, 0.0).astype(jnp.bfloat16)
            total = total + jnp.dot(jnp.abs(tile), pick, preferred_element_type=jnp.float32)
    flat = jnp.transpose(total)
    sums_ref[...] = flat[:per, :]
    for d in range(1, ncols):
        rest = flat[d * per : (d + 1) * per, :]
        pieces = []
        for _ in range(3):
            pieces.append(rest.astype(jnp.bfloat16).astype(jnp.float32))
            rest = rest - pieces[-1]
        pieces.append(jnp.zeros_like(rest))
        leads[d - 1][half * TILE :, :] = jnp.concatenate(pieces, axis=0).astype(jnp.bfloat16)


def lead(tiles, send_slot, ncols):
    nslots = tiles.shape[0]
    per = nslots // ncols
    res = pl.pallas_call(
        functools.partial(lead_kernel, ncols, per),
        out_shape=[
            jax.ShapeDtypeStruct((per, TILE), jnp.float32),
            jax.ShapeDtypeStruct((per, TILE, TILE), tiles.dtype),
        ]
        + [jax.ShapeDtypeStruct((per * LEAD // 8 * TILE + 4 * per, TILE), tiles.dtype)] * (ncols - 1),
        in_specs=[SMEM, VMEM],
        out_specs=[VMEM] * (1 + ncols),
        scratch_shapes=[pltpu.SMEM((nslots,), jnp.int32)],
        compiler_params=params(),
    )(send_slot, tiles)
    return res[0], res[1], res[2:]


def rest_kernel(ncols, per, send_ref, tiles_ref, after_ref, *refs):
    outs, inverse = refs[:-1], refs[-1]
    me = lax.axis_index("cols")
    find_inverse(send_ref, inverse)
    half = per * LEAD // 8
    for d in range(1, ncols):
        dest = lax.rem(me + d, ncols)
        for p in range(half, per):
            outs[d - 1][p - half] = tiles_ref[inverse[dest * per + p]]


def rest(tiles, send_slot, ncols, after):
    nslots = tiles.shape[0]
    per = nslots // ncols
    return pl.pallas_call(
        functools.partial(rest_kernel, ncols, per),
        out_shape=[jax.ShapeDtypeStruct((per - per * LEAD // 8, TILE, TILE), tiles.dtype)] * (ncols - 1),
        in_specs=[SMEM, VMEM, ANY],
        out_specs=[VMEM] * (ncols - 1),
        scratch_shapes=[pltpu.SMEM((nslots,), jnp.int32)],
        compiler_params=params(),
    )(send_slot, tiles, after)


def later_kernel(list_ref, after_ref, out_ref):
    for g in range(out_ref.shape[1]):
        out_ref[0, g] = list_ref[0, g]


def later(fetch_list, after):
    return pl.pallas_call(
        later_kernel,
        out_shape=jax.ShapeDtypeStruct(fetch_list.shape, fetch_list.dtype),
        in_specs=[SMEM, ANY],
        out_specs=SMEM,
        compiler_params=params(),
    )(fetch_list, after)


def send_blocks(scaled, wanted, outs):
    for d, out in enumerate(outs):
        out[...] = scaled[pl.ds(pl.multiple_of(wanted[d] * TILE, TILE), TILE), :]


def start_kernel(ncols, groups, blocks, row_ref, *refs):
    lists, refs = refs[:groups], refs[groups:]
    (sums_ref, *leads), (basis_ref, scale_ref, asked_ref, *outs, scaled) = refs[:ncols], refs[ncols:]
    me, row = lax.axis_index("cols"), lax.axis_index("rows")
    per = sums_ref.shape[0]
    sums = [sums_ref[...]]
    for ref in leads:
        tail = ref[per * LEAD // 8 * TILE :, :].astype(jnp.float32)
        sums.append(tail[:per, :] + tail[per : 2 * per, :] + tail[2 * per : 3 * per, :])
    degree = [jnp.ones((1, TILE), jnp.float32) for _ in range(blocks)]
    for d in range(ncols):
        source = lax.rem(me + ncols - d, ncols)
        for p in range(per):
            at = row_ref[0, source * per + p]
            line = sums[d][p : p + 1, :]
            for j in range(blocks):
                degree[j] = degree[j] + jnp.where(at == j, line, jnp.zeros_like(line))
    for j in range(blocks):
        here = slice(j * TILE, (j + 1) * TILE)
        scale = jnp.transpose(jnp.broadcast_to(lax.rsqrt(degree[j]), (WIDTH, TILE)))
        scale_ref[here, :] = scale
        scaled[here, :] = (scale * basis_ref[here, :].astype(jnp.float32)).astype(jnp.bfloat16)
    wanted = [lists[d][0, row] for d in range(groups)]
    for d in range(groups):
        asked_ref[0, d] = wanted[d]
    send_blocks(scaled, wanted, outs)


def start(slot_row, lists, sums, basis):
    ncols, groups, rows = len(sums), len(lists), basis.shape[0]
    res = pl.pallas_call(
        functools.partial(start_kernel, ncols, groups, rows // TILE),
        out_shape=[
            jax.ShapeDtypeStruct((rows, WIDTH), jnp.float32),
            jax.ShapeDtypeStruct((1, groups), jnp.int32),
        ]
        + [jax.ShapeDtypeStruct((TILE, WIDTH), jnp.bfloat16)] * groups,
        in_specs=[SMEM] * (1 + groups) + [VMEM] * (ncols + 1),
        out_specs=[VMEM, SMEM] + [VMEM] * groups,
        scratch_shapes=[pltpu.VMEM((rows, WIDTH), jnp.bfloat16)],
        compiler_params=params(),
    )(slot_row, *lists, *sums, basis)
    return res[0], res[1], res[2:]


def gram_of(y):
    return lax.dot_general(
        y, y, (((0,), (0,)), ((), ())), precision=HIGHEST, preferred_element_type=jnp.float32
    )


def times(a, b, transposed=False):
    return lax.dot_general(
        a, b, (((1,), (1 if transposed else 0,)), ((), ())), precision=HIGHEST, preferred_element_type=jnp.float32
    )


def step_kernel(ncols, groups, first, last, row_ref, fetch_ref, asked_ref, scale_ref, *refs):
    stay, leads, rests, refs = refs[0], refs[1:ncols], refs[ncols : 2 * ncols - 1], refs[2 * ncols - 1 :]
    got, refs = refs[:groups], refs[groups:]
    outs, (held, acc, scaled) = refs[:-3], refs[-3:]
    me, row = lax.axis_index("cols"), lax.axis_index("rows")
    per, rows = stay.shape[0], scale_ref.shape[0]
    half = per * LEAD // 8
    for d in range(groups):
        held[d] = got[d][...]
    acc[...] = jnp.zeros_like(acc)
    for d in range(ncols):
        source = lax.rem(me + ncols - d, ncols)
        for p in range(per):
            slot = source * per + p
            which = jnp.bitwise_xor(fetch_ref[0, slot], row)
            place = pl.ds(pl.multiple_of(row_ref[0, slot] * TILE, TILE), TILE)
            if d == 0:
                tile = stay[p]
            elif p < half:
                tile = leads[d - 1][p * TILE : (p + 1) * TILE, :]
            else:
                tile = rests[d - 1][p - half]
            acc[place, :] += jnp.dot(tile, held[which], preferred_element_type=jnp.float32)
    scale = scale_ref[...]
    y = acc[:rows, :] * scale
    if last:
        outs[0][...] = y
        return
    gram_ref, outs = outs[0], outs[1:]
    gram_ref[:HALF, :], gram_ref[HALF:, :] = fold(gram_of(y))
    if first:
        scaled[...] = (y * scale).astype(jnp.bfloat16)
        send_blocks(scaled, [asked_ref[0, d] for d in range(groups)], outs)
    else:
        outs[0][...] = y


def step(slot_row, slot_fetch, asked, scale, chunks, got, first, last):
    ncols, groups, rows = (len(chunks) + 1) // 2, len(got), scale.shape[0]
    shapes = [] if last else [jax.ShapeDtypeStruct((HALF + 8, WIDTH), jnp.float32)]
    if first:
        shapes += [jax.ShapeDtypeStruct((TILE, WIDTH), jnp.bfloat16)] * groups
    else:
        shapes += [jax.ShapeDtypeStruct((rows, WIDTH), jnp.float32)]
    res = pl.pallas_call(
        functools.partial(step_kernel, ncols, groups, first, last),
        out_shape=shapes,
        in_specs=[SMEM] * 3 + [VMEM] * (1 + len(chunks) + groups),
        out_specs=[VMEM] * len(shapes),
        scratch_shapes=[
            pltpu.VMEM((groups, TILE, WIDTH), jnp.bfloat16),
            pltpu.VMEM((rows + TILE, WIDTH), jnp.float32),
            pltpu.VMEM((rows, WIDTH), jnp.bfloat16),
        ],
        compiler_params=params(),
    )(slot_row, slot_fetch, asked, scale, *chunks, *got)
    if last:
        return None, res[0]
    return res[0], (res[1:] if first else res[1])


def added(parts):
    while len(parts) > 1:
        parts = [parts[i] + parts[i + 1] for i in range(0, len(parts), 2)]
    return parts[0]


def summed(refs):
    return added([ref[...] for ref in refs])


def turn_kernel(npts, groups, nparts, first, last, gauge, asked_ref, scale_ref, p_ref, *refs):
    parts, refs = refs[:nparts], refs[nparts:]
    if not first:
        before_ref, before_inv_ref, refs = refs[0], refs[1], refs[2:]
    outs, (inv, scaled) = refs[:-2], refs[-2:]
    gram = unfold(summed(parts)) * (1.0 / npts)
    factor_rows(gram, inv)
    both = inv[...]
    mine = both if first else times(both, before_ref[...])
    y = times(p_ref[...], mine, True)
    if last:
        gram_ref, y_ref = outs
        y_ref[...] = y
        gram_ref[:HALF, :], gram_ref[HALF:, :] = fold(gram_of(y))
        return
    low_ref, inv_ref, growth_ref, outs = outs[0], outs[1], outs[2], outs[3:]
    scaled[...] = (y * scale_ref[...]).astype(jnp.bfloat16)
    send_blocks(scaled, [asked_ref[0, d] for d in range(groups)], outs)
    low = times(gram, both, True)
    low = low if first else times(before_inv_ref[...], low)
    low_ref[...] = low
    inv_ref[...] = mine
    if not gauge:
        return
    weights = lax.dot_general(
        jnp.ones((8, WIDTH), jnp.float32), low * low, (((1,), (1,)), ((), ())), preferred_element_type=jnp.float32
    )
    growth = jnp.sum(mine * mine * weights[0:1, :]) * (1.0 / WIDTH)
    growth_ref[...] = jnp.full((8, WIDTH), growth)


def turn(asked, parts, scale, p, before, npts, last, gauge):
    rows, groups = p.shape[0], asked.shape[1]
    first = before is None
    square = jax.ShapeDtypeStruct((WIDTH, WIDTH), jnp.float32)
    growth = jax.ShapeDtypeStruct((8, WIDTH), jnp.float32)
    if last:
        shapes = [jax.ShapeDtypeStruct((HALF + 8, WIDTH), jnp.float32), jax.ShapeDtypeStruct(p.shape, p.dtype)]
    else:
        shapes = [square, square, growth] + [jax.ShapeDtypeStruct((TILE, WIDTH), jnp.bfloat16)] * groups
    return pl.pallas_call(
        functools.partial(turn_kernel, npts, groups, len(parts), first, last, gauge),
        out_shape=shapes,
        in_specs=[SMEM] + [VMEM] * (2 + len(parts) + (0 if first else 2)),
        out_specs=[VMEM] * len(shapes),
        scratch_shapes=[pltpu.VMEM((WIDTH, WIDTH), jnp.float32), pltpu.VMEM((rows, WIDTH), jnp.bfloat16)],
        compiler_params=params(),
    )(asked, scale, p, *parts, *([] if first else before))


def careful_kernel(npts, groups, nparts, asked_ref, scale_ref, y_ref, *refs):
    parts, (v_ref, *outs), (inv, scaled) = refs[:nparts], refs[nparts:-2], refs[-2:]
    factor_rows(unfold(summed(parts)) * (1.0 / npts), inv)
    v = times(y_ref[...], inv[...], True).astype(jnp.bfloat16)
    v_ref[...] = v
    scaled[...] = (v.astype(jnp.float32) * scale_ref[...]).astype(jnp.bfloat16)
    send_blocks(scaled, [asked_ref[0, d] for d in range(groups)], outs)


def careful(asked, parts, scale, y, npts):
    rows, groups = y.shape[0], asked.shape[1]
    res = pl.pallas_call(
        functools.partial(careful_kernel, npts, groups, len(parts)),
        out_shape=[jax.ShapeDtypeStruct(y.shape, jnp.bfloat16)]
        + [jax.ShapeDtypeStruct((TILE, WIDTH), jnp.bfloat16)] * groups,
        in_specs=[SMEM] + [VMEM] * (2 + len(parts)),
        out_specs=[VMEM] * (1 + groups),
        scratch_shapes=[pltpu.VMEM((WIDTH, WIDTH), jnp.float32), pltpu.VMEM((rows, WIDTH), jnp.bfloat16)],
        compiler_params=params(),
    )(asked, scale, y, *parts)
    return res[0], res[1:]


def fold(square):
    row = lax.broadcasted_iota(jnp.int32, (HALF, WIDTH), 0)
    lane = lax.broadcasted_iota(jnp.int32, (HALF, WIDTH), 1)
    low = square[HALF:, :]
    moved = pltpu.roll(low, HALF, 1)
    main = jnp.where((lane < HALF) & (lane > row), moved, square[:HALF, :])
    diagonal = jnp.sum(jnp.where(lane == row + HALF, low, 0.0), axis=0, keepdims=True)
    return main, jnp.broadcast_to(diagonal, (8, WIDTH))


def unfold(folded):
    row = lax.broadcasted_iota(jnp.int32, (HALF, WIDTH), 0)
    lane = lax.broadcasted_iota(jnp.int32, (HALF, WIDTH), 1)
    main = folded[:HALF, :]
    diagonal = jnp.broadcast_to(folded[HALF : HALF + 1, :], (HALF, WIDTH))
    upper = jnp.where((lane >= HALF) | (lane <= row), main, 0.0)
    moved = pltpu.roll(main, HALF, 1)
    lower = jnp.where(lane > row + HALF, moved, jnp.where(lane == row + HALF, diagonal, 0.0))
    whole = jnp.concatenate([upper, lower], axis=0)
    row = lax.broadcasted_iota(jnp.int32, (WIDTH, WIDTH), 0)
    lane = lax.broadcasted_iota(jnp.int32, (WIDTH, WIDTH), 1)
    return jnp.where(row == lane, whole, whole + jnp.transpose(whole))


def factor_rows(matrix, out_ref):
    n = WIDTH
    lane = lax.broadcasted_iota(jnp.int32, (8, n), 1)
    parts = [matrix[8 * i : 8 * i + 8, :] for i in range(n // 8)]
    for j in range(0, n, GROUP):
        here = j // 8
        off = j % 8
        wide = lambda v: jnp.broadcast_to(v, (8, n))
        rows = [wide(parts[here][off + a : off + a + 1, :]) for a in range(GROUP)]
        piv = [[wide(rows[a][:, j + c : j + c + 1]) for c in range(a + 1)] for a in range(GROUP)]
        in_group = (lane >= j) & (lane < j + GROUP)
        rows = [jnp.where(in_group, jnp.where(lane == j + a, 1.0, 0.0), rows[a]) for a in range(GROUP)]
        low = [[None] * GROUP for _ in range(GROUP)]
        inv = []
        for c in range(GROUP):
            inv.append(1.0 / piv[c][c])
            for a in range(c + 1, GROUP):
                low[a][c] = piv[a][c] * inv[c]
            for a in range(c + 1, GROUP):
                for b in range(c + 1, a + 1):
                    piv[a][b] = piv[a][b] - low[a][c] * piv[b][c]
        for a in range(GROUP):
            for c in range(a):
                rows[a] = rows[a] - low[a][c] * rows[c]
        for a in range(GROUP):
            keep = jnp.where(lane <= j + a, rows[a], 0.0) * lax.rsqrt(piv[a][a])
            out_ref[j + a : j + a + 1, :] = keep[0:1, :]
        scaled = [rows[a] * inv[a] for a in range(GROUP)]
        for i in range(here + 1, n // 8):
            cols = [wide(parts[i][:, j + c : j + c + 1]) for c in range(GROUP)]
            new = jnp.where(in_group, 0.0, parts[i])
            for c in range(GROUP):
                for b in range(c):
                    cols[c] = cols[c] - low[c][b] * cols[b]
                new = new - cols[c] * scaled[c]
            parts[i] = new


def finish_kernel(npts, nparts, y_ref, *refs):
    v_ref, inv = refs[nparts:]
    factor_rows(unfold(summed(refs[:nparts])) * (1.0 / npts), inv)
    v_ref[...] = times(y_ref[...], inv[...], True).astype(v_ref.dtype)


def finish(parts, y, npts):
    return pl.pallas_call(
        functools.partial(finish_kernel, npts, len(parts)),
        out_shape=jax.ShapeDtypeStruct(y.shape, jnp.bfloat16),
        in_specs=[VMEM] * (1 + len(parts)),
        out_specs=VMEM,
        scratch_shapes=[pltpu.VMEM((WIDTH, WIDTH), jnp.float32)],
        compiler_params=params(),
    )(y, *parts)


def swap(x, axis, n, d):
    return lax.ppermute(x, axis, [(i, i ^ d) for i in range(n)])


def shift(x, axis, n, d):
    return lax.ppermute(x, axis, [(i, (i + d) % n) for i in range(n)])


def prepare(tiles, send_slot, slot_row, fetch_list, basis):
    groups = lax.axis_size("rows")
    ncols = lax.axis_size("cols")
    sums, stay, leads = lead(tiles, send_slot, ncols)
    rests = rest(tiles, send_slot, ncols, leads[0])
    wish = later(fetch_list, rests[0])
    leads = [shift(leads[d - 1], "cols", ncols, d) for d in range(1, ncols)]
    rests = [shift(rests[d - 1], "cols", ncols, d) for d in range(1, ncols)]
    chunks = [stay, *leads, *rests]
    lists = [wish] + [swap(wish, "rows", groups, d) for d in range(1, groups)]
    scale, asked, out = start(slot_row, lists, [sums, *leads], basis)
    return chunks, scale, asked, out


def on_device(tiles, send_slot, slot_row, slot_fetch, fetch_list, basis):
    groups = lax.axis_size("rows")
    ncols = lax.axis_size("cols")
    npts = basis.shape[0] * groups * ncols
    chunks, scale, asked, out = prepare(tiles, send_slot, slot_row, fetch_list, basis)
    stages = [("rows", groups, [1])]
    bit = 2
    while bit < groups:
        wide = bit * 2 < groups
        stages.append(("rows", groups, [bit, 2 * bit, 3 * bit] if wide else [bit]))
        bit *= 4 if wide else 2
    apart = [("cols", ncols, [1 << i]) for i in range(ncols.bit_length() - 1)]
    at_once = [("cols", ncols, list(range(1, ncols)))]

    def total(gram, more):
        for axis, size, partners in stages + more:
            parts = [gram] + [swap(gram, axis, size, d) for d in partners]
            gram = added(parts)
        return parts

    def fetched(out):
        return [out[0]] + [swap(out[d], "rows", groups, d) for d in range(1, groups)]

    growth = []
    parts = before = None
    for k in range(ITERS):
        last = k == ITERS - 1
        gram, out = step(slot_row, slot_fetch, asked, scale, chunks, fetched(out), k == 0, last)
        if k:
            gauge = k in (2, ITERS - 2)
            res = turn(asked, parts, scale, out, before, npts, last, gauge)
            before, out = res[:2], res[3:]
            if gauge:
                growth.append(res[2][0, 0])
        if not last:
            parts = total(gram, apart)
    gram, y = res
    fast = finish(total(gram, at_once), y, npts)

    def again():
        chunks, scale, asked, out = prepare(tiles, send_slot, slot_row, fetch_list, basis)

        def repeat(k, state):
            gram, y = step(slot_row, slot_fetch, asked, scale, chunks, fetched(state[1]), False, False)
            v, out = careful(asked, total(gram, apart), scale, y, npts)
            return v, tuple(out)

        return lax.fori_loop(0, ITERS, repeat, (basis, tuple(out)))[0]

    return lax.cond(sum(growth) < GROWTH, lambda: fast, again)


def solution(mesh):
    in_specs = (
        P(("rows", "cols"), None, None),
        P(("rows", "cols"), None),
        P(("rows", "cols"), None),
        P(("rows", "cols"), None),
        P(("rows", "cols"), None),
        P(("rows", "cols"), None),
    )
    out_specs = P(("rows", "cols"), None)
    return jax.shard_map(
        on_device, mesh=mesh, in_specs=in_specs, out_specs=out_specs, check_vma=False
    )
```
